32 devices in a mesh: section: 2 (over core), dp: 4 (over z), tensor: 4 (over y, x).
Axes of the slice: x: 2, y: 2, z: 4, core: 2. Of those that a mesh axis runs over, the one named last changes fastest.
Arguments:
- boundary: bfloat16 [2, 8, 256, 1792], P('section', 'dp', 'tensor'), may hold values from -6 to 6
- lengths: int32 [8], P('dp'), may hold values from 32 to 256, as said below
- norm_gains: float32 [2, 2, 1792], P('section'), may hold values from 0.5 to 1.5
- conv_taps: float32 [2, 3, 1792], P('section'), may hold values from -3 to 3
- lin_qk: bfloat16 [1792, 2, 256], P('dp', None, 'tensor'), may hold values from -0.125 to 0.125
- win_qk: bfloat16 [1792, 2, 1792], P('dp', None, 'tensor'), may hold values from -0.125 to 0.125
- value_gate: bfloat16 [2, 1792, 2, 1792], P('section', 'dp', None, 'tensor'), may hold values from -0.125 to 0.125
- out_weight: bfloat16 [2, 1792, 1792], P('section', 'tensor', 'dp'), may hold values from -1 to 1
- gate_up: bfloat16 [2, 1792, 2, 4864], P('section', 'dp', None, 'tensor'), may hold values from -0.125 to 0.125
- down_weight: bfloat16 [2, 4864, 1792], P('section', 'tensor', 'dp'), may hold values from -0.078125 to 0.078125
Outputs:
- ends: float32 [2, 8, 256, 1792], P('section', 'dp', 'tensor')
- grad_gains: float32 [2, 2, 1792], P('section')
- grad_taps: float32 [2, 3, 1792], P('section')
- grad_lin_qk: float32 [1792, 2, 256], P('dp', None, 'tensor')
- grad_win_qk: float32 [1792, 2, 1792], P('dp', None, 'tensor')
- grad_value_gate: float32 [2, 1792, 2, 1792], P('section', 'dp', None, 'tensor')
- grad_out_weight: float32 [2, 1792, 1792], P('section', 'tensor', 'dp')
- grad_gate_up: float32 [2, 1792, 2, 4864], P('section', 'dp', None, 'tensor')
- grad_down_weight: float32 [2, 4864, 1792], P('section', 'tensor', 'dp')
The draws below stay inside these ranges and needn't reach their ends.
Inputs may be any that keep to these rules, and one draw needn't show every extreme that they name: `lengths`: in each aligned block of 2 sequences (those of one dp index) one sequence, drawn from the seed, has length 256.
All inputs are finite; a program needn't handle non-finite values.
Results may differ from the reference program's by a relative error of at most 0.04.
Values may be sent and summed in bfloat16 or wider, within the bound.
No kernel may reach another device: no remote copies, remote signals or barrier semaphores. Data moves between devices by JAX's collectives and lax.ppermute only.
A program may use at most 320 MiB of HBM per device.

```python
import math
from functools import partial
import jax
import jax.numpy as jnp
from jax import lax

D = 1792
H = 16
FEAT = 16
FF = 4864
WIN = 64
CONV = 3
MB = 2
LEN = 256
SEQS = 8


def draw_lengths(key, part):
    key = jax.random.fold_in(key, 11)
    spread_key, pick_key = jax.random.split(key)
    groups = SEQS // MB
    drawn = jax.random.randint(spread_key, (groups, MB), LEN // 8, LEN + 1)
    chosen = jax.random.randint(pick_key, (groups, 1), 0, MB)
    slots = jnp.arange(MB)[None, :]
    return jnp.where(slots == chosen, LEN, drawn).reshape(SEQS).astype(jnp.int32)


def block_levels(rng, dims, cuts, low, largest):
    factor_of, own = 1.0, jax.random.fold_in(rng, 6)
    for axis_at, shards_of in cuts:
        draws = jnp.exp(jax.random.uniform(jax.random.fold_in(own, axis_at), (shards_of,), jnp.float32, low / len(cuts), largest / len(cuts)))
        factor_of = factor_of * jnp.repeat(draws, dims[axis_at] // shards_of).reshape([-1 if axis == axis_at else 1 for axis in range(len(dims))])
    return factor_of


def normal_values(stream_key, shape, spread, reach, cuts=(), dtype=jnp.bfloat16):
    loudness = block_levels(stream_key, shape, cuts, -0.22, 0.18) if cuts else 1.0
    entries = jax.random.normal(stream_key, shape, jnp.float32) * spread * loudness
    return jnp.minimum(jnp.maximum(entries, -reach), reach).astype(dtype)


def setup_inputs(seed: int = 0) -> dict:
    keys = jax.random.split(jax.random.key(seed), 11)
    return {
        "boundary": normal_values(keys[0], (2, SEQS, LEN, D), 1.0, 6.0, ((0, 2), (1, 4), (2, 4))),
        "lengths": draw_lengths(jax.random.fold_in(keys[10], 71), 0),
        "norm_gains": jnp.clip(1.0 + 0.1 * jax.random.normal(keys[2], (2, 2, D), jnp.float32), 0.5, 1.5),
        "conv_taps": normal_values(keys[3], (2, CONV, D), 0.6, 3.0, ((0, 2),), jnp.float32),
        "lin_qk": normal_values(keys[4], (D, 2, H * FEAT), D ** -0.5, 0.125, ((0, 4), (2, 4))),
        "win_qk": normal_values(keys[5], (D, 2, D), D ** -0.5, 0.125, ((0, 4), (2, 4))),
        "value_gate": normal_values(keys[6], (2, D, 2, D), D ** -0.5, 0.125, ((0, 2), (1, 4), (3, 4))),
        "out_weight": normal_values(keys[7], (2, D, D), (D // 64) ** -0.5, 1.0, ((0, 2), (1, 4), (2, 4))),
        "gate_up": normal_values(keys[8], (2, D, 2, FF), D ** -0.5, 0.125, ((0, 2), (1, 4), (3, 4))),
        "down_weight": normal_values(keys[9], (2, FF, D), FF ** -0.5, 0.078125, ((0, 2), (1, 4), (2, 4))),
    }


EPS = 1e-06
MAXIMUM_ACCURACY = lax.Precision.HIGHEST

@jax.custom_vjp
def low(v):
    return lax.optimization_barrier(v.astype(jnp.bfloat16)).astype(jnp.float32)

@jax.custom_vjp
def low_back(v):
    return v

def low_keep(v):
    return (low(v), None)

def low_pass(kept, grad):
    return (grad,)

def back_keep(v):
    return (v, None)

def back_low(kept, grad):
    return (low(grad),)
low.defvjp(low_keep, low_pass)
low_back.defvjp(back_keep, back_low)

def causal_conv(values, taps):
    total = values * taps[0]
    for offset in range(1, taps.shape[0]):
        moved = jnp.pad(values[:-offset], ((offset, 0), (0, 0)))
        total = total + moved * taps[offset]
    return total

def rms_scale(rows, gain):
    return rows * lax.rsqrt(lax.optimization_barrier(jnp.mean(rows * rows, axis=-1, keepdims=True)) + EPS) * gain

def mixer(full, values, weight, taylor):
    length = full.shape[0]
    window_width = weight.shape[-1] // H
    query_key_pair = low_back(low(jnp.dot(full, weight.reshape(weight.shape[0], -1), precision=MAXIMUM_ACCURACY)))
    query_key_pair = query_key_pair.reshape(length, 2, H, window_width)
    logit_scores = jnp.einsum('loc,moc->olm', query_key_pair[:, 0], query_key_pair[:, 1], precision=MAXIMUM_ACCURACY) / math.sqrt(window_width)
    logit_scores = low_back(logit_scores)
    place = jnp.arange(length)
    causal = place[None, :] <= place[:, None]
    if taylor:
        kernel = jnp.where(causal[None], 1.0 + logit_scores + 0.5 * logit_scores * logit_scores, 0.0)
        probs = kernel / lax.optimization_barrier(jnp.sum(kernel, axis=-1, keepdims=True))
    else:
        allowed = causal & (place[:, None] - place[None, :] < WIN)
        probs = jax.nn.softmax(jnp.where(allowed[None], logit_scores, -1e+30), axis=-1)
    probs = low(probs)
    mixed = jnp.einsum('hqk,khd->qhd', probs, values.reshape(length, H, -1), precision=MAXIMUM_ACCURACY)
    return low_back(mixed.reshape(length, -1))

def layer(rows, gains, taps, pair_weight, value_gate, out_weight, gate_up, down_weight, taylor):
    length, window_width = rows.shape
    full = low(rms_scale(rows, gains[0]))
    both = jnp.dot(full, value_gate.reshape(window_width, -1), precision=MAXIMUM_ACCURACY).reshape(length, 2, window_width)
    pre_values = low_back(both[:, 0])
    gate_mix = low_back(both[:, 1])
    values = low(causal_conv(pre_values, taps))
    mixed = mixer(full, values, pair_weight, taylor)
    gated = low(mixed * jax.nn.silu(gate_mix))
    hidden = rows + low_back(jnp.dot(gated, out_weight, precision=MAXIMUM_ACCURACY))
    second = low(rms_scale(hidden, gains[1]))
    halves = jnp.dot(second, gate_up.reshape(window_width, -1), precision=MAXIMUM_ACCURACY).reshape(length, 2, -1)
    gate = low_back(halves[:, 0])
    upper = low_back(halves[:, 1])
    inner = low(jax.nn.silu(gate) * upper)
    return hidden + low_back(jnp.dot(inner, down_weight, precision=MAXIMUM_ACCURACY))

def network(first_rows, gains, taps, lin_weight, win_weight, value_gate, out_weight, gate_up, down_weight, mask):
    middle = layer(first_rows, gains[0], taps[0], lin_weight, value_gate[0], out_weight[0], gate_up[0], down_weight[0], True)
    middle = low_back(low(middle))
    final = layer(middle, gains[1], taps[1], win_weight, value_gate[1], out_weight[1], gate_up[1], down_weight[1], False)
    return final * mask

def reference(boundary, lengths, norm_gains, conv_taps, lin_qk, win_qk, value_gate, out_weight, gate_up, down_weight):
    params = tuple((item.astype(jnp.float32) for item in (norm_gains, conv_taps, lin_qk, win_qk, value_gate, out_weight, gate_up, down_weight)))
    place = jnp.arange(LEN).astype(jnp.int32)

    def step(totals, index):
        first_rows = boundary[0, index].astype(jnp.float32)
        cotangent = boundary[1, index].astype(jnp.float32)
        mask = (place < lengths[index]).astype(jnp.float32)[:, None]
        output, pullback = jax.vjp(partial(network, mask=mask), first_rows, *params)
        grads = pullback(cotangent)
        totals = tuple((total + grad for total, grad in zip(totals, grads[1:])))
        return (totals, (grads[0], output))
    zeros = tuple((jnp.zeros(item.shape, jnp.float32) for item in params))
    totals, (first_grads, outputs) = lax.scan(step, zeros, jnp.arange(SEQS).astype(jnp.int32))
    ends = jnp.stack([first_grads, outputs])
    return (ends, totals[0], totals[1], totals[2], totals[3], totals[4], totals[5], totals[6], totals[7])
```

```python
import math

import jax
import jax.numpy as jnp
from jax import lax
from jax.sharding import PartitionSpec as P

WIN = 64
HD = 112
LANES = 128

EPS = 1e-06


def silu_slope(value):
    sigma = jax.nn.sigmoid(value)
    return sigma * (1.0 + value * (1.0 - sigma))


def rms_rows(rows, gain):
    scale = lax.rsqrt(jnp.mean(rows * rows, axis=-1, keepdims=True) + EPS)
    return (scale, rows * scale * gain)


def rms_back(rows, scale, gain, grad):
    normal = rows * scale
    weighted = grad * gain
    inner = jnp.mean(weighted * normal, axis=-1, keepdims=True)
    return (scale * (weighted - normal * inner), jnp.sum(grad * normal, axis=0))


def causal_conv(values, taps):
    total = values * taps[0]
    for offset in range(1, taps.shape[0]):
        moved = jnp.pad(values[:, :-offset], ((0, 0), (offset, 0), (0, 0)))
        total = total + moved * taps[offset]
    return total


def conv_back(grad, values, taps):
    grad_values = grad * taps[0]
    grad_taps = [jnp.sum(grad * values, axis=(0, 1))]
    for offset in range(1, taps.shape[0]):
        moved = jnp.pad(grad[:, offset:], ((0, 0), (0, offset), (0, 0)))
        grad_values = grad_values + moved * taps[offset]
        grad_taps.append(jnp.sum(grad[:, offset:] * values[:, :-offset], axis=(0, 1)))
    return (grad_values, jnp.stack(grad_taps))


def swap(block):
    return lax.ppermute(block, "section", [(0, 1), (1, 0)])


def spread(rows):
    mine = lax.all_gather(rows.astype(jnp.bfloat16), "tensor", axis=0, tiled=True)
    return jnp.concatenate([mine, swap(mine)], axis=0)


def collect(terms):
    length = terms.shape[0] // 2
    size = lax.axis_size("tensor")
    count = length // size
    index = lax.axis_index("tensor")
    arrived = swap(terms[length:].astype(jnp.bfloat16))
    part = terms[:length] + arrived.astype(jnp.float32)
    low = part.astype(jnp.bfloat16)
    total = lax.dynamic_slice_in_dim(part, index * count, count, 0)
    for offset in range(1, size):
        block = lax.dynamic_slice_in_dim(low, (index ^ offset) * count, count, 0)
        pairs = [(i, i ^ offset) for i in range(size)]
        total = total + lax.ppermute(block, "tensor", pairs).astype(jnp.float32)
    return total


def sum_all(block):
    for axis in ("section", "tensor", "dp"):
        size = lax.axis_size(axis)
        step = 1
        while step < size:
            pairs = [(i, i ^ step) for i in range(size)]
            block = block + lax.ppermute(block, axis, pairs)
            step *= 2
    return block


def widen(columns):
    return jnp.pad(columns, ((0, 0), (0, -columns.shape[1] % LANES)))


def dot(one, two):
    return jnp.dot(one, two, preferred_element_type=jnp.float32)


def dot_nt(one, two):
    return lax.dot_general(one, two, (((1,), (1,)), ((), ())), preferred_element_type=jnp.float32)


def dot_tn(one, two):
    return lax.dot_general(one, two, (((0,), (0,)), ((), ())), preferred_element_type=jnp.float32)


def heads_of(block, width):
    return block.reshape(2, block.shape[0] // 2, -1, width)


def score_parts(queries, keys, first):
    length = queries.shape[1]
    width = queries.shape[-1]
    scores = jnp.einsum(
        "sihc,sjhc->shij", queries, keys, preferred_element_type=jnp.float32
    ) / math.sqrt(width)
    place = jnp.arange(length)
    causal = place[None, :] <= place[:, None]
    if first:
        kernel = jnp.where(causal, 1.0 + scores + 0.5 * scores * scores, 0.0)
        total = jnp.sum(kernel, axis=-1, keepdims=True)
        slope = jnp.where(causal, (1.0 + scores) / total, 0.0)
        return (kernel / total, slope)
    allowed = causal & (place[:, None] - place[None, :] < WIN)
    probs = jax.nn.softmax(jnp.where(allowed, scores, -1e30), axis=-1)
    return (probs, probs)


def layer_forward(rows, gains, taps, attn, feed, channels, first):
    width = (attn.shape[1] - (channels + LANES - 1) // LANES * LANES - 2 * channels) // 2
    hidden_units = feed.shape[1] // 3
    scale_one, normed = rms_rows(rows, gains[0])
    full_one = spread(normed)
    both = dot(full_one, attn[:, : 2 * channels + 2 * width])
    length = full_one.shape[0] // 2
    pre_values = both[:, :channels].reshape(2, length, channels)
    gate_mix = both[:, channels : 2 * channels]
    values = causal_conv(pre_values, taps).astype(jnp.bfloat16).reshape(2, length, -1, HD)
    head_width = width // (channels // HD)
    queries = heads_of(both[:, 2 * channels : 2 * channels + width].astype(jnp.bfloat16), head_width)
    keys = heads_of(both[:, 2 * channels + width :].astype(jnp.bfloat16), head_width)
    probs, slope = score_parts(queries, keys, first)
    mixed = jnp.einsum(
        "shij,sjhc->sihc", probs.astype(jnp.bfloat16), values, preferred_element_type=jnp.float32
    ).reshape(2 * length, channels)
    gated = (mixed * jax.nn.silu(gate_mix)).astype(jnp.bfloat16)
    out_t = attn[:, 2 * channels + 2 * width :][:, :channels]
    hidden = rows + collect(dot_nt(gated, out_t))
    scale_two, normed_two = rms_rows(hidden, gains[1])
    full_two = spread(normed_two)
    halves = dot(full_two, feed[:, : 2 * hidden_units])
    gate = halves[:, :hidden_units]
    upper = halves[:, hidden_units:]
    inner = (jax.nn.silu(gate) * upper).astype(jnp.bfloat16)
    output = hidden + collect(dot_nt(inner, feed[:, 2 * hidden_units :]))
    kept = (
        rows, scale_one, full_one, pre_values, gate_mix, values, queries, keys, probs, slope,
        mixed, gated, out_t, hidden, scale_two, full_two, gate, upper, inner,
    )
    return (output, kept)


def layer_backward(kept, grad_out, gains, taps, attn, feed, channels, first):
    (
        rows, scale_one, full_one, pre_values, gate_mix, values, queries, keys, probs, slope,
        mixed, gated, out_t, hidden, scale_two, full_two, gate, upper, inner,
    ) = kept
    hidden_units = feed.shape[1] // 3
    length = full_one.shape[0] // 2
    branch_two = spread(grad_out)
    grad_down = scatter(dot_tn(branch_two, inner))
    grad_inner = dot(branch_two, feed[:, 2 * hidden_units :])
    grad_gate = (grad_inner * upper * silu_slope(gate)).astype(jnp.bfloat16)
    grad_upper = (grad_inner * jax.nn.silu(gate)).astype(jnp.bfloat16)
    grad_halves = jnp.concatenate([grad_gate, grad_upper], axis=1)
    grad_gate_up = scatter(dot_tn(full_two, grad_halves))
    grad_second = collect(dot_nt(grad_halves, feed[:, : 2 * hidden_units]))
    back_two, gain_two = rms_back(hidden, scale_two, gains[1], grad_second)
    grad_hidden = grad_out + back_two
    branch_one = spread(grad_hidden)
    grad_outw = scatter(dot_tn(branch_one, gated))
    grad_gated = dot(branch_one, out_t)
    grad_mixed = (grad_gated * jax.nn.silu(gate_mix)).astype(jnp.bfloat16)
    grad_mix_gate = (grad_gated * mixed * silu_slope(gate_mix)).astype(jnp.bfloat16)
    grad_heads = heads_of(grad_mixed, HD)
    low = probs.astype(jnp.bfloat16)
    grad_values = jnp.einsum("shij,sihc->sjhc", low, grad_heads, preferred_element_type=jnp.float32)
    grad_probs = jnp.einsum("sihc,sjhc->shij", grad_heads, values, preferred_element_type=jnp.float32)
    centred = grad_probs - jnp.sum(probs * grad_probs, axis=-1, keepdims=True)
    score_grad = (centred * slope).astype(jnp.bfloat16)
    root = math.sqrt(queries.shape[-1])
    grad_queries = jnp.einsum("shij,sjhc->sihc", score_grad, keys, preferred_element_type=jnp.float32)
    grad_keys = jnp.einsum("shij,sihc->sjhc", score_grad, queries, preferred_element_type=jnp.float32)
    grad_queries = (grad_queries / root).astype(jnp.bfloat16).reshape(2 * length, -1)
    grad_keys = (grad_keys / root).astype(jnp.bfloat16).reshape(2 * length, -1)
    grad_pre, grad_taps = conv_back(grad_values.reshape(2, length, channels), pre_values, taps)
    grad_pre = grad_pre.astype(jnp.bfloat16).reshape(2 * length, channels)
    grad_both = jnp.concatenate([grad_pre, grad_mix_gate, grad_queries, grad_keys], axis=1)
    grad_attn = scatter(dot_tn(full_one, grad_both))
    grad_first = collect(dot_nt(grad_both, attn[:, : grad_both.shape[1]]))
    back_one, gain_one = rms_back(rows, scale_one, gains[0], grad_first)
    grad_rows = grad_hidden + back_one
    grads = (grad_attn, grad_outw, grad_gate_up, grad_down)
    return (grad_rows, grads, jnp.stack([gain_one, gain_two]), grad_taps)


def scatter(grad):
    return lax.psum_scatter(grad.astype(jnp.bfloat16), "dp", scatter_dimension=0, tiled=True)


def body(
    boundary, lengths, norm_gains, conv_taps, lin_qk, win_qk, value_gate, out_weight, gate_up, down_weight
):
    core = lax.axis_index("section")
    index = lax.axis_index("tensor")
    lower = core == 0
    rows_dev, model = boundary.shape[2:]
    channels = value_gate.shape[-1] // 2
    units = gate_up.shape[-1] // 2

    def half(block, axis, which):
        size = block.shape[axis] // 2
        return lax.dynamic_slice_in_dim(block, which * size, size, axis)

    def both_layers(build):
        mine = build(core)
        other = swap(build(1 - core))
        return (jnp.where(lower, mine, other), jnp.where(lower, other, mine))

    def attn_piece(which):
        values = half(value_gate[0], 2, which)
        return jnp.concatenate(
            [values[:, 0], values[:, 1], widen(half(out_weight[0], 0, which).T)], axis=1
        )

    def feed_piece(which):
        pair = half(gate_up[0], 2, which)
        down = half(down_weight[0], 0, which).T
        return jnp.concatenate([widen(pair[:, 0]), widen(pair[:, 1]), widen(down)], axis=1)

    def with_pair(piece, pair):
        pair = half(pair, 2, core)
        return jnp.concatenate(
            [piece[:, : 2 * channels], pair[:, 0], pair[:, 1], piece[:, 2 * channels :]], axis=1
        )

    def fetch(piece):
        return lax.all_gather(piece, "dp", axis=0, tiled=True)

    attn_parts = both_layers(attn_piece)
    feed_parts = both_layers(feed_piece)
    attn_zero = fetch(with_pair(attn_parts[0], lin_qk))
    feed_zero = fetch(feed_parts[0])
    attn_one = fetch(with_pair(attn_parts[1], win_qk))
    feed_one = fetch(feed_parts[1])

    small = jnp.concatenate([norm_gains[0], conv_taps[0]], axis=0)
    small_other = swap(small)
    small_zero = jnp.where(lower, small, small_other)
    small_one = jnp.where(lower, small_other, small)
    offset = (2 * index + core) * channels

    def own_taps(block):
        return lax.dynamic_slice_in_dim(block[2:], offset, channels, 1)

    held = boundary[0]
    keep = lax.dynamic_index_in_dim(held, core, 0, keepdims=False)
    other = swap(lax.dynamic_index_in_dim(held, 1 - core, 0, keepdims=False))
    entering = jnp.where(lower, keep, other).astype(jnp.float32)
    cotangent = jnp.where(lower, other, keep).astype(jnp.float32)
    length = lax.dynamic_index_in_dim(lengths, core, 0, keepdims=False)
    place = index * rows_dev + jnp.arange(rows_dev)
    mask = (place < length).astype(jnp.float32)[:, None]

    middle, kept_zero = layer_forward(
        entering, small_zero[:2], own_taps(small_zero), attn_zero, feed_zero, channels, True
    )
    middle = middle.astype(jnp.bfloat16).astype(jnp.float32)
    final, kept_one = layer_forward(
        middle, small_one[:2], own_taps(small_one), attn_one, feed_one, channels, False
    )
    grad_middle, grads_one, gains_one, taps_one = layer_backward(
        kept_one, cotangent * mask, small_one[:2], own_taps(small_one), attn_one, feed_one, channels, False
    )
    grad_middle = grad_middle.astype(jnp.bfloat16).astype(jnp.float32)
    grad_start, grads_zero, gains_zero, taps_zero = layer_backward(
        kept_zero, grad_middle, small_zero[:2], own_taps(small_zero), attn_zero, feed_zero, channels, True
    )

    def own_small(gains, taps):
        spot = jnp.zeros((taps.shape[0], model), jnp.float32)
        return jnp.concatenate([gains, lax.dynamic_update_slice_in_dim(spot, taps, offset, 1)], axis=0)

    sums = sum_all(jnp.stack([own_small(gains_zero, taps_zero), own_small(gains_one, taps_one)]))
    sums = lax.dynamic_index_in_dim(sums, core, 0, keepdims=True)

    final = final * mask
    ends_keep = jnp.where(lower, grad_start, final)
    ends_other = swap(jnp.where(lower, final, grad_start))
    ends = jnp.where(lower, jnp.stack([ends_keep, ends_other]), jnp.stack([ends_other, ends_keep]))

    def home(zero, one):
        mine = jnp.where(lower, zero, one)
        other = swap(jnp.where(lower, one, zero))
        return (jnp.where(lower, mine, other), jnp.where(lower, other, mine))

    def halves(low, high, axis):
        return jnp.concatenate([low, high], axis=axis).astype(jnp.float32)

    def pair_home(grads):
        block = grads[:, 2 * channels :]
        size = block.shape[1] // 2
        other = swap(block)
        low = jnp.where(lower, block, other)
        high = jnp.where(lower, other, block)
        return jnp.stack(
            [halves(low[:, :size], high[:, :size], 1), halves(low[:, size:], high[:, size:], 1)], axis=1
        )

    low, high = home(grads_zero[0][:, : 2 * channels], grads_one[0][:, : 2 * channels])
    vgate_grad = jnp.stack(
        [
            halves(low[:, :channels], high[:, :channels], 1),
            halves(low[:, channels:], high[:, channels:], 1),
        ],
        axis=1,
    )
    low, high = home(grads_zero[1], grads_one[1])
    out_grad = halves(low.T, high.T, 0)
    low, high = home(grads_zero[2], grads_one[2])
    wide = low.shape[1] // 2
    gate_up_grad = jnp.stack(
        [
            halves(low[:, :units], high[:, :units], 1),
            halves(low[:, wide : wide + units], high[:, wide : wide + units], 1),
        ],
        axis=1,
    )
    low, high = home(grads_zero[3], grads_one[3])
    down_grad = halves(low[:, :units].T, high[:, :units].T, 0)
    return (
        ends[None],
        sums[:, :2],
        sums[:, 2:],
        pair_home(grads_zero[0]),
        pair_home(grads_one[0]),
        vgate_grad[None],
        out_grad[None],
        gate_up_grad[None],
        down_grad[None],
    )


def solution(mesh):
    in_specs = (
        P("section", "dp", "tensor", None),
        P("dp"),
        P("section", None, None),
        P("section", None, None),
        P("dp", None, "tensor"),
        P("dp", None, "tensor"),
        P("section", "dp", None, "tensor"),
        P("section", "tensor", "dp"),
        P("section", "dp", None, "tensor"),
        P("section", "tensor", "dp"),
    )
    out_specs = (
        P("section", "dp", "tensor", None),
        P("section", None, None),
        P("section", None, None),
        P("dp", None, "tensor"),
        P("dp", None, "tensor"),
        P("section", "dp", None, "tensor"),
        P("section", "tensor", "dp"),
        P("section", "dp", None, "tensor"),
        P("section", "tensor", "dp"),
    )
    return jax.shard_map(body, mesh=mesh, in_specs=in_specs, out_specs=out_specs, check_vma=False)
```

```python
import math

import jax
import jax.numpy as jnp
from jax import lax
from jax.sharding import PartitionSpec as P

WIN = 64
HD = 112
LANES = 128

EPS = 1e-06


def silu_slope(value):
    sigma = jax.nn.sigmoid(value)
    return sigma * (1.0 + value * (1.0 - sigma))


def rms_rows(rows, gain):
    scale = lax.rsqrt(jnp.mean(rows * rows, axis=-1, keepdims=True) + EPS)
    return (scale, rows * scale * gain)


def rms_back(rows, scale, gain, grad):
    normal = rows * scale
    weighted = grad * gain
    inner = jnp.mean(weighted * normal, axis=-1, keepdims=True)
    return (scale * (weighted - normal * inner), jnp.sum(grad * normal, axis=0))


def causal_conv(values, taps):
    total = values * taps[0]
    for offset in range(1, taps.shape[0]):
        moved = jnp.pad(values[:, :-offset], ((0, 0), (offset, 0), (0, 0)))
        total = total + moved * taps[offset]
    return total


def conv_back(grad, values, taps):
    grad_values = grad * taps[0]
    grad_taps = [jnp.sum(grad * values, axis=(0, 1))]
    for offset in range(1, taps.shape[0]):
        moved = jnp.pad(grad[:, offset:], ((0, 0), (0, offset), (0, 0)))
        grad_values = grad_values + moved * taps[offset]
        grad_taps.append(jnp.sum(grad[:, offset:] * values[:, :-offset], axis=(0, 1)))
    return (grad_values, jnp.stack(grad_taps))


def swap(block):
    return lax.ppermute(block, "section", [(0, 1), (1, 0)])


def spread(rows):
    mine = lax.all_gather(rows.astype(jnp.bfloat16), "tensor", axis=0, tiled=True)
    return jnp.concatenate([mine, swap(mine)], axis=0)


def collect(terms):
    length = terms.shape[0] // 2
    size = lax.axis_size("tensor")
    count = length // size
    index = lax.axis_index("tensor")
    arrived = swap(terms[length:].astype(jnp.bfloat16))
    part = terms[:length] + arrived.astype(jnp.float32)
    low = part.astype(jnp.bfloat16)
    total = lax.dynamic_slice_in_dim(part, index * count, count, 0)
    for offset in range(1, size):
        block = lax.dynamic_slice_in_dim(low, (index ^ offset) * count, count, 0)
        pairs = [(i, i ^ offset) for i in range(size)]
        total = total + lax.ppermute(block, "tensor", pairs).astype(jnp.float32)
    return total


def sum_all(block):
    for axis in ("section", "tensor", "dp"):
        size = lax.axis_size(axis)
        step = 1
        while step < size:
            pairs = [(i, i ^ step) for i in range(size)]
            block = block + lax.ppermute(block, axis, pairs)
            step *= 2
    return block


def widen(columns):
    return jnp.pad(columns, ((0, 0), (0, -columns.shape[1] % LANES)))


def dot(one, two):
    return jnp.dot(one, two, preferred_element_type=jnp.float32)


def dot_nt(one, two):
    return lax.dot_general(one, two, (((1,), (1,)), ((), ())), preferred_element_type=jnp.float32)


def dot_tn(one, two):
    return lax.dot_general(one, two, (((0,), (0,)), ((), ())), preferred_element_type=jnp.float32)


def heads_of(block, width):
    return block.reshape(2, block.shape[0] // 2, -1, width)


def score_parts(queries, keys, first):
    length = queries.shape[1]
    width = queries.shape[-1]
    scores = jnp.einsum(
        "sihc,sjhc->shij", queries, keys, preferred_element_type=jnp.float32
    ) / math.sqrt(width)
    place = jnp.arange(length)
    causal = place[None, :] <= place[:, None]
    if first:
        kernel = jnp.where(causal, 1.0 + scores + 0.5 * scores * scores, 0.0)
        total = jnp.sum(kernel, axis=-1, keepdims=True)
        slope = jnp.where(causal, (1.0 + scores) / total, 0.0)
        return (kernel / total, slope)
    allowed = causal & (place[:, None] - place[None, :] < WIN)
    probs = jax.nn.softmax(jnp.where(allowed, scores, -1e30), axis=-1)
    return (probs, probs)


def layer_forward(rows, gains, taps, attn, feed, channels, first):
    width = (attn.shape[1] - (channels + LANES - 1) // LANES * LANES - 2 * channels) // 2
    hidden_units = feed.shape[1] // 3
    scale_one, normed = rms_rows(rows, gains[0])
    full_one = spread(normed)
    both = dot(full_one, attn[:, : 2 * channels + 2 * width])
    length = full_one.shape[0] // 2
    pre_values = both[:, :channels].reshape(2, length, channels)
    gate_mix = both[:, channels : 2 * channels]
    values = causal_conv(pre_values, taps).astype(jnp.bfloat16).reshape(2, length, -1, HD)
    head_width = width // (channels // HD)
    queries = heads_of(both[:, 2 * channels : 2 * channels + width].astype(jnp.bfloat16), head_width)
    keys = heads_of(both[:, 2 * channels + width :].astype(jnp.bfloat16), head_width)
    probs, slope = score_parts(queries, keys, first)
    mixed = jnp.einsum(
        "shij,sjhc->sihc", probs.astype(jnp.bfloat16), values, preferred_element_type=jnp.float32
    ).reshape(2 * length, channels)
    gated = (mixed * jax.nn.silu(gate_mix)).astype(jnp.bfloat16)
    out_t = attn[:, 2 * channels + 2 * width :][:, :channels]
    hidden = rows + collect(dot_nt(gated, out_t))
    scale_two, normed_two = rms_rows(hidden, gains[1])
    full_two = spread(normed_two)
    halves = dot(full_two, feed[:, : 2 * hidden_units])
    gate = halves[:, :hidden_units]
    upper = halves[:, hidden_units:]
    inner = (jax.nn.silu(gate) * upper).astype(jnp.bfloat16)
    output = hidden + collect(dot_nt(inner, feed[:, 2 * hidden_units :]))
    kept = (
        rows, scale_one, full_one, pre_values, gate_mix, values, queries, keys, probs, slope,
        mixed, gated, out_t, hidden, scale_two, full_two, gate, upper, inner,
    )
    return (output, kept)


def layer_backward(kept, grad_out, gains, taps, attn, feed, channels, first, queue):
    (
        rows, scale_one, full_one, pre_values, gate_mix, values, queries, keys, probs, slope,
        mixed, gated, out_t, hidden, scale_two, full_two, gate, upper, inner,
    ) = kept
    hidden_units = feed.shape[1] // 3
    length = full_one.shape[0] // 2
    branch_two = spread(grad_out)
    branch_two, grad_down = product_first(branch_two, inner, branch_two)
    grad_inner = dot(branch_two, feed[:, 2 * hidden_units :])
    grad_gate = (grad_inner * upper * silu_slope(gate)).astype(jnp.bfloat16)
    grad_upper = (grad_inner * jax.nn.silu(gate)).astype(jnp.bfloat16)
    grad_halves = jnp.concatenate([grad_gate, grad_upper], axis=1)
    grad_halves, grad_gate_up = product_first(full_two, grad_halves, grad_halves)
    feed_grads = queue.scatter(grad_gate_up, grad_down)
    grad_second = collect(dot_nt(grad_halves, feed[:, : 2 * hidden_units]))
    back_two, gain_two = rms_back(hidden, scale_two, gains[1], grad_second)
    grad_hidden = grad_out + back_two
    branch_one = spread(grad_hidden)
    branch_one, grad_outw = product_first(branch_one, gated, branch_one)
    grad_gated = dot(branch_one, out_t)
    grad_mixed = (grad_gated * jax.nn.silu(gate_mix)).astype(jnp.bfloat16)
    grad_mix_gate = (grad_gated * mixed * silu_slope(gate_mix)).astype(jnp.bfloat16)
    grad_heads = heads_of(grad_mixed, HD)
    low = probs.astype(jnp.bfloat16)
    grad_values = jnp.einsum("shij,sihc->sjhc", low, grad_heads, preferred_element_type=jnp.float32)
    grad_probs = jnp.einsum("sihc,sjhc->shij", grad_heads, values, preferred_element_type=jnp.float32)
    centred = grad_probs - jnp.sum(probs * grad_probs, axis=-1, keepdims=True)
    score_grad = (centred * slope).astype(jnp.bfloat16)
    root = math.sqrt(queries.shape[-1])
    grad_queries = jnp.einsum("shij,sjhc->sihc", score_grad, keys, preferred_element_type=jnp.float32)
    grad_keys = jnp.einsum("shij,sihc->sjhc", score_grad, queries, preferred_element_type=jnp.float32)
    grad_queries = (grad_queries / root).astype(jnp.bfloat16).reshape(2 * length, -1)
    grad_keys = (grad_keys / root).astype(jnp.bfloat16).reshape(2 * length, -1)
    grad_pre, grad_taps = conv_back(grad_values.reshape(2, length, channels), pre_values, taps)
    grad_pre = grad_pre.astype(jnp.bfloat16).reshape(2 * length, channels)
    grad_both = jnp.concatenate([grad_pre, grad_mix_gate, grad_queries, grad_keys], axis=1)
    grad_both, grad_attn = product_first(full_one, grad_both, grad_both)
    attn_grads = queue.scatter(grad_attn, grad_outw)
    grad_first = collect(dot_nt(grad_both, attn[:, : grad_both.shape[1]]))
    back_one, gain_one = rms_back(rows, scale_one, gains[0], grad_first)
    grad_rows = grad_hidden + back_one
    return (grad_rows, (feed_grads, attn_grads), jnp.stack([gain_one, gain_two]), grad_taps)


class Queue:
    def __init__(self):
        self.last = None

    def scatter(self, *grads):
        block = jnp.concatenate(grads, axis=1) if len(grads) > 1 else grads[0]
        if self.last is not None:
            block, self.last = lax.optimization_barrier((block, self.last))
        self.last = lax.psum_scatter(block, "dp", scatter_dimension=0, tiled=True)
        return self.last


def product_first(one, two, chain):
    grad = widen(dot_tn(one, two).astype(jnp.bfloat16))
    return lax.optimization_barrier((chain, grad))


def body(
    boundary, lengths, norm_gains, conv_taps, lin_qk, win_qk, value_gate, out_weight, gate_up, down_weight
):
    core = lax.axis_index("section")
    index = lax.axis_index("tensor")
    lower = core == 0
    rows_dev, model = boundary.shape[2:]
    channels = value_gate.shape[-1] // 2
    units = gate_up.shape[-1] // 2

    def half(block, axis, which):
        size = block.shape[axis] // 2
        return lax.dynamic_slice_in_dim(block, which * size, size, axis)

    def both_layers(build):
        mine = build(core)
        other = swap(build(1 - core))
        return (jnp.where(lower, mine, other), jnp.where(lower, other, mine))

    def attn_piece(which):
        values = half(value_gate[0], 2, which)
        return jnp.concatenate(
            [values[:, 0], values[:, 1], widen(half(out_weight[0], 0, which).T)], axis=1
        )

    def feed_piece(which):
        pair = half(gate_up[0], 2, which)
        down = half(down_weight[0], 0, which).T
        return jnp.concatenate([widen(pair[:, 0]), widen(pair[:, 1]), widen(down)], axis=1)

    def with_pair(piece, pair):
        pair = half(pair, 2, core)
        return jnp.concatenate(
            [piece[:, : 2 * channels], pair[:, 0], pair[:, 1], piece[:, 2 * channels :]], axis=1
        )

    def fetch(piece):
        return lax.all_gather(piece, "dp", axis=0, tiled=True)

    attn_parts = both_layers(attn_piece)
    feed_parts = both_layers(feed_piece)
    attn_zero = fetch(with_pair(attn_parts[0], lin_qk))
    feed_zero = fetch(feed_parts[0])
    attn_one = fetch(with_pair(attn_parts[1], win_qk))
    feed_one = fetch(feed_parts[1])

    small = jnp.concatenate([norm_gains[0], conv_taps[0]], axis=0)
    small_other = swap(small)
    small_zero = jnp.where(lower, small, small_other)
    small_one = jnp.where(lower, small_other, small)
    offset = (2 * index + core) * channels

    def own_taps(block):
        return lax.dynamic_slice_in_dim(block[2:], offset, channels, 1)

    held = boundary[0]
    keep = lax.dynamic_index_in_dim(held, core, 0, keepdims=False)
    other = swap(lax.dynamic_index_in_dim(held, 1 - core, 0, keepdims=False))
    entering = jnp.where(lower, keep, other).astype(jnp.float32)
    cotangent = jnp.where(lower, other, keep).astype(jnp.float32)
    length = lax.dynamic_index_in_dim(lengths, core, 0, keepdims=False)
    place = index * rows_dev + jnp.arange(rows_dev)
    mask = (place < length).astype(jnp.float32)[:, None]

    middle, kept_zero = layer_forward(
        entering, small_zero[:2], own_taps(small_zero), attn_zero, feed_zero, channels, True
    )
    middle = middle.astype(jnp.bfloat16).astype(jnp.float32)
    final, kept_one = layer_forward(
        middle, small_one[:2], own_taps(small_one), attn_one, feed_one, channels, False
    )
    queue = Queue()
    grad_middle, grads_one, gains_one, taps_one = layer_backward(
        kept_one, cotangent * mask, small_one[:2], own_taps(small_one), attn_one, feed_one, channels, False,
        queue,
    )
    grad_middle = grad_middle.astype(jnp.bfloat16).astype(jnp.float32)
    grad_start, grads_zero, gains_zero, taps_zero = layer_backward(
        kept_zero, grad_middle, small_zero[:2], own_taps(small_zero), attn_zero, feed_zero, channels, True,
        queue,
    )

    def own_small(gains, taps):
        spot = jnp.zeros((taps.shape[0], model), jnp.float32)
        return jnp.concatenate([gains, lax.dynamic_update_slice_in_dim(spot, taps, offset, 1)], axis=0)

    sums = sum_all(jnp.stack([own_small(gains_zero, taps_zero), own_small(gains_one, taps_one)]))
    sums = lax.dynamic_index_in_dim(sums, core, 0, keepdims=True)

    final = final * mask
    ends_keep = jnp.where(lower, grad_start, final)
    ends_other = swap(jnp.where(lower, final, grad_start))
    ends = jnp.where(lower, jnp.stack([ends_keep, ends_other]), jnp.stack([ends_other, ends_keep]))

    def home(zero, one):
        mine = jnp.where(lower, zero, one)
        other = swap(jnp.where(lower, one, zero))
        return (jnp.where(lower, mine, other), jnp.where(lower, other, mine))

    def halves(low, high, axis):
        return jnp.concatenate([low, high], axis=axis).astype(jnp.float32)

    def pair_home(block):
        size = block.shape[1] // 2
        other = swap(block)
        low = jnp.where(lower, block, other)
        high = jnp.where(lower, other, block)
        return jnp.stack(
            [halves(low[:, :size], high[:, :size], 1), halves(low[:, size:], high[:, size:], 1)], axis=1
        )

    def split_pair(grads):
        out = (channels + LANES - 1) // LANES * LANES
        both = 2 * channels
        width = grads.shape[1] - out
        return (jnp.concatenate([grads[:, :both], grads[:, width:]], axis=1), grads[:, both:width])

    attn_zero, pair_zero = split_pair(grads_zero[1])
    attn_one, pair_one = split_pair(grads_one[1])
    low, high = home(attn_zero, attn_one)
    vgate_grad = jnp.stack(
        [
            halves(low[:, :channels], high[:, :channels], 1),
            halves(low[:, channels : 2 * channels], high[:, channels : 2 * channels], 1),
        ],
        axis=1,
    )
    out_grad = halves(low[:, 2 * channels : 3 * channels].T, high[:, 2 * channels : 3 * channels].T, 0)
    low, high = home(grads_zero[0], grads_one[0])
    wide = low.shape[1] // 3
    gate_up_grad = jnp.stack(
        [
            halves(low[:, :units], high[:, :units], 1),
            halves(low[:, wide : wide + units], high[:, wide : wide + units], 1),
        ],
        axis=1,
    )
    down_grad = halves(low[:, 2 * wide : 2 * wide + units].T, high[:, 2 * wide : 2 * wide + units].T, 0)
    return (
        ends[None],
        sums[:, :2],
        sums[:, 2:],
        pair_home(pair_zero),
        pair_home(pair_one),
        vgate_grad[None],
        out_grad[None],
        gate_up_grad[None],
        down_grad[None],
    )


def solution(mesh):
    in_specs = (
        P("section", "dp", "tensor", None),
        P("dp"),
        P("section", None, None),
        P("section", None, None),
        P("dp", None, "tensor"),
        P("dp", None, "tensor"),
        P("section", "dp", None, "tensor"),
        P("section", "tensor", "dp"),
        P("section", "dp", None, "tensor"),
        P("section", "tensor", "dp"),
    )
    out_specs = (
        P("section", "dp", "tensor", None),
        P("section", None, None),
        P("section", None, None),
        P("dp", None, "tensor"),
        P("dp", None, "tensor"),
        P("section", "dp", None, "tensor"),
        P("section", "tensor", "dp"),
        P("section", "dp", None, "tensor"),
        P("section", "tensor", "dp"),
    )
    return jax.shard_map(body, mesh=mesh, in_specs=in_specs, out_specs=out_specs, check_vma=False)
```

```python
import math

import jax
import jax.numpy as jnp
from jax import lax
from jax.experimental.layout import Layout, with_layout_constraint
from jax.sharding import PartitionSpec as P

WIN = 64
HD = 112
LANES = 128

EPS = 1e-06


def silu_slope(value):
    sigma = jax.nn.sigmoid(value)
    return sigma * (1.0 + value * (1.0 - sigma))


def rms_rows(rows, gain):
    scale = lax.rsqrt(jnp.mean(rows * rows, axis=-1, keepdims=True) + EPS)
    return (scale, rows * scale * gain)


def rms_back(rows, scale, gain, grad):
    normal = rows * scale
    weighted = grad * gain
    inner = jnp.mean(weighted * normal, axis=-1, keepdims=True)
    return (scale * (weighted - normal * inner), jnp.sum(grad * normal, axis=0))


def causal_conv(values, taps):
    total = values * taps[0]
    for offset in range(1, taps.shape[0]):
        moved = jnp.pad(values[:, :-offset], ((0, 0), (offset, 0), (0, 0)))
        total = total + moved * taps[offset]
    return total


def conv_back(grad, values, taps):
    grad_values = grad * taps[0]
    grad_taps = [jnp.sum(grad * values, axis=(0, 1))]
    for offset in range(1, taps.shape[0]):
        moved = jnp.pad(grad[:, offset:], ((0, 0), (0, offset), (0, 0)))
        grad_values = grad_values + moved * taps[offset]
        grad_taps.append(jnp.sum(grad[:, offset:] * values[:, :-offset], axis=(0, 1)))
    return (grad_values, jnp.stack(grad_taps))


def swap(block):
    return lax.ppermute(block, "section", [(0, 1), (1, 0)])


def spread(rows):
    mine = lax.all_gather(rows.astype(jnp.bfloat16), "tensor", axis=0, tiled=True)
    return jnp.concatenate([mine, swap(mine)], axis=0)


def collect(terms):
    length = terms.shape[0] // 2
    size = lax.axis_size("tensor")
    count = length // size
    index = lax.axis_index("tensor")
    arrived = swap(terms[length:].astype(jnp.bfloat16))
    part = terms[:length] + arrived.astype(jnp.float32)
    low = part.astype(jnp.bfloat16)
    total = lax.dynamic_slice_in_dim(part, index * count, count, 0)
    for offset in range(1, size):
        block = lax.dynamic_slice_in_dim(low, (index ^ offset) * count, count, 0)
        pairs = [(i, i ^ offset) for i in range(size)]
        total = total + lax.ppermute(block, "tensor", pairs).astype(jnp.float32)
    return total


def sum_all(block):
    for axis in ("section", "tensor", "dp"):
        size = lax.axis_size(axis)
        step = 1
        while step < size:
            pairs = [(i, i ^ step) for i in range(size)]
            block = block + lax.ppermute(block, axis, pairs)
            step *= 2
    return block


def widen(columns):
    return jnp.pad(columns, ((0, 0), (0, -columns.shape[1] % LANES)))


def dot(one, two):
    return jnp.dot(one, two, preferred_element_type=jnp.float32)


def dot_nt(one, two):
    return lax.dot_general(one, two, (((1,), (1,)), ((), ())), preferred_element_type=jnp.float32)


def dot_tn(one, two):
    return lax.dot_general(one, two, (((0,), (0,)), ((), ())), preferred_element_type=jnp.float32)


def heads_of(block, width):
    return block.reshape(2, block.shape[0] // 2, -1, width)


def score_parts(queries, keys, first):
    length = queries.shape[1]
    width = queries.shape[-1]
    scores = jnp.einsum(
        "sihc,sjhc->shij", queries, keys, preferred_element_type=jnp.float32
    ) / math.sqrt(width)
    place = jnp.arange(length)
    causal = place[None, :] <= place[:, None]
    if first:
        kernel = jnp.where(causal, 1.0 + scores + 0.5 * scores * scores, 0.0)
        total = jnp.sum(kernel, axis=-1, keepdims=True)
        slope = jnp.where(causal, (1.0 + scores) / total, 0.0)
        return (kernel / total, slope)
    allowed = causal & (place[:, None] - place[None, :] < WIN)
    probs = jax.nn.softmax(jnp.where(allowed, scores, -1e30), axis=-1)
    return (probs, probs)


def gates(halves, units):
    main = units // LANES * LANES
    stop = main + units
    return (
        (halves[:, :main], halves[:, main : 2 * main]),
        (halves[:, 2 * main : stop], halves[:, stop : 2 * units]),
    )


def layer_forward(rows, gains, taps, weights, first):
    mix, out_t, pair, down = weights
    channels = out_t.shape[1]
    width = mix.shape[1] // 2 - channels
    units = down.shape[1]
    scale_one, normed = rms_rows(rows, gains[0])
    full_one = spread(normed)
    both = dot(full_one, mix)
    length = full_one.shape[0] // 2
    pre_values = both[:, :channels].reshape(2, length, channels)
    gate_mix = both[:, channels : 2 * channels]
    values = causal_conv(pre_values, taps).astype(jnp.bfloat16).reshape(2, length, -1, HD)
    head_width = width // (channels // HD)
    queries = heads_of(both[:, 2 * channels : 2 * channels + width].astype(jnp.bfloat16), head_width)
    keys = heads_of(both[:, 2 * channels + width :].astype(jnp.bfloat16), head_width)
    probs, slope = score_parts(queries, keys, first)
    mixed = jnp.einsum(
        "shij,sjhc->sihc", probs.astype(jnp.bfloat16), values, preferred_element_type=jnp.float32
    ).reshape(2 * length, channels)
    gated = (mixed * jax.nn.silu(gate_mix)).astype(jnp.bfloat16)
    hidden = rows + collect(dot_nt(gated, out_t))
    scale_two, normed_two = rms_rows(hidden, gains[1])
    full_two = spread(normed_two)
    halves = dot(full_two, pair)
    inner = jnp.concatenate(
        [(jax.nn.silu(gate) * upper).astype(jnp.bfloat16) for gate, upper in gates(halves, units)], axis=1
    )
    output = hidden + collect(dot_nt(inner, down))
    kept = (
        rows, scale_one, full_one, pre_values, gate_mix, values, queries, keys, probs, slope,
        mixed, gated, hidden, scale_two, full_two, halves, inner,
    )
    return (output, kept)


def layer_backward(kept, grad_out, gains, taps, weights, first, queue, tail):
    (
        rows, scale_one, full_one, pre_values, gate_mix, values, queries, keys, probs, slope,
        mixed, gated, hidden, scale_two, full_two, halves, inner,
    ) = kept
    mix, out_t, pair, down = weights
    channels = out_t.shape[1]
    units = down.shape[1]
    main = units // LANES * LANES
    length = full_one.shape[0] // 2
    branch_two = spread(grad_out)
    branch_two, grad_down = product_first(branch_two, inner, branch_two)
    grad_inner = dot(branch_two, down)
    parts = []
    for (gate, upper), grad in zip(gates(halves, units), (grad_inner[:, :main], grad_inner[:, main:])):
        parts.append((grad * upper * silu_slope(gate)).astype(jnp.bfloat16))
        parts.append((grad * jax.nn.silu(gate)).astype(jnp.bfloat16))
    filler = jnp.zeros((2 * length, pair.shape[1] - 2 * units), jnp.bfloat16)
    grad_halves = jnp.concatenate([*parts, filler], axis=1)
    grad_halves, grad_gate_up = product_first(full_two, grad_halves, grad_halves)
    rest = jnp.pad(grad_down[:, main : units - tail], ((0, 0), (2 * units, 0)))
    queue.scatter(grad_down[:, :main], grad_gate_up + rest)
    grad_second = collect(dot_nt(grad_halves, pair))
    back_two, gain_two = rms_back(hidden, scale_two, gains[1], grad_second)
    grad_hidden = grad_out + back_two
    branch_one = spread(grad_hidden)
    branch_one, grad_outw = product_first(branch_one, gated, branch_one)
    grad_gated = dot(branch_one, out_t)
    grad_mixed = (grad_gated * jax.nn.silu(gate_mix)).astype(jnp.bfloat16)
    grad_mix_gate = (grad_gated * mixed * silu_slope(gate_mix)).astype(jnp.bfloat16)
    grad_heads = heads_of(grad_mixed, HD)
    low = probs.astype(jnp.bfloat16)
    grad_values = jnp.einsum("shij,sihc->sjhc", low, grad_heads, preferred_element_type=jnp.float32)
    grad_probs = jnp.einsum("sihc,sjhc->shij", grad_heads, values, preferred_element_type=jnp.float32)
    centred = grad_probs - jnp.sum(probs * grad_probs, axis=-1, keepdims=True)
    score_grad = (centred * slope).astype(jnp.bfloat16)
    root = math.sqrt(queries.shape[-1])
    grad_queries = jnp.einsum("shij,sjhc->sihc", score_grad, keys, preferred_element_type=jnp.float32)
    grad_keys = jnp.einsum("shij,sihc->sjhc", score_grad, queries, preferred_element_type=jnp.float32)
    grad_queries = (grad_queries / root).astype(jnp.bfloat16).reshape(2 * length, -1)
    grad_keys = (grad_keys / root).astype(jnp.bfloat16).reshape(2 * length, -1)
    grad_pre, grad_taps = conv_back(grad_values.reshape(2, length, channels), pre_values, taps)
    grad_pre = grad_pre.astype(jnp.bfloat16).reshape(2 * length, channels)
    grad_both = jnp.concatenate([grad_pre, grad_mix_gate, grad_queries, grad_keys], axis=1)
    grad_both, grad_attn = product_first(full_one, grad_both, grad_both)
    queue.scatter(grad_attn, grad_outw, grad_down[:, units - tail :])
    grad_first = collect(dot_nt(grad_both, mix))
    back_one, gain_one = rms_back(rows, scale_one, gains[0], grad_first)
    grad_rows = grad_hidden + back_one
    return (grad_rows, jnp.stack([gain_one, gain_two]), grad_taps)


def by_rows(block):
    return with_layout_constraint(block, Layout(major_to_minor=(0, 1)))


class Queue:
    def __init__(self):
        self.done = []

    def scatter(self, *grads):
        block = by_rows(jnp.concatenate(grads, axis=1))
        if self.done:
            block, self.done[-1] = lax.optimization_barrier((block, self.done[-1]))
        self.done.append(by_rows(lax.psum_scatter(block, "dp", scatter_dimension=0, tiled=True)))


def product_first(one, two, chain):
    grad = dot_tn(one, two).astype(jnp.bfloat16)
    return lax.optimization_barrier((chain, grad))


def body(
    boundary, lengths, norm_gains, conv_taps, lin_qk, win_qk, value_gate, out_weight, gate_up, down_weight
):
    core = lax.axis_index("section")
    index = lax.axis_index("tensor")
    lower = core == 0
    rows_dev, model = boundary.shape[2:]
    channels = value_gate.shape[-1] // 2
    units = gate_up.shape[-1] // 2
    main = units // LANES * LANES
    tail = -(3 * channels + lin_qk.shape[-1]) % LANES

    def half(block, axis, which):
        size = block.shape[axis] // 2
        return lax.dynamic_slice_in_dim(block, which * size, size, axis)

    def both_layers(build):
        mine = build(core)
        other = swap(build(1 - core))
        return (jnp.where(lower, mine, other), jnp.where(lower, other, mine))

    def attn_piece(which):
        values = half(value_gate[0], 2, which)
        last = half(down_weight[0], 0, which)[units - tail :]
        return jnp.concatenate(
            [values[:, 0], values[:, 1], half(out_weight[0], 0, which).T, last.T], axis=1
        )

    def feed_piece(which):
        pair = half(gate_up[0], 2, which)
        down = half(down_weight[0], 0, which).T
        return jnp.concatenate(
            [down[:, :main], pair[:, 0, :main], pair[:, 1, :main], pair[:, 0, main:], pair[:, 1, main:], down[:, main : units - tail]],
            axis=1,
        )

    def fetch(piece):
        return lax.all_gather(piece, "dp", axis=0, tiled=True)

    def with_pair(attn, pair):
        pair = half(pair, 2, core)
        both = 2 * channels
        return jnp.concatenate([attn[:, :both], pair[:, 0], pair[:, 1], attn[:, both:]], axis=1)

    def parts_of(feed, attn):
        stop = attn.shape[1] - tail
        down = jnp.concatenate([feed[:, :main], feed[:, main + 2 * units :], attn[:, stop:]], axis=1)
        return (attn[:, : stop - channels], attn[:, stop - channels : stop], feed[:, main:], down)

    attn_parts = both_layers(attn_piece)
    feed_parts = both_layers(feed_piece)
    attn_zero = fetch(with_pair(attn_parts[0], lin_qk))
    weights_zero = parts_of(fetch(feed_parts[0]), attn_zero)
    attn_one = fetch(with_pair(attn_parts[1], win_qk))
    weights_one = parts_of(fetch(feed_parts[1]), attn_one)

    small = jnp.concatenate([norm_gains[0], conv_taps[0]], axis=0)
    small_other = swap(small)
    small_zero = jnp.where(lower, small, small_other)
    small_one = jnp.where(lower, small_other, small)
    offset = (2 * index + core) * channels

    def own_taps(block):
        return lax.dynamic_slice_in_dim(block[2:], offset, channels, 1)

    held = boundary[0]
    keep = lax.dynamic_index_in_dim(held, core, 0, keepdims=False)
    other = swap(lax.dynamic_index_in_dim(held, 1 - core, 0, keepdims=False))
    entering = jnp.where(lower, keep, other).astype(jnp.float32)
    cotangent = jnp.where(lower, other, keep).astype(jnp.float32)
    length = lax.dynamic_index_in_dim(lengths, core, 0, keepdims=False)
    place = index * rows_dev + jnp.arange(rows_dev)
    mask = (place < length).astype(jnp.float32)[:, None]

    middle, kept_zero = layer_forward(
        entering, small_zero[:2], own_taps(small_zero), weights_zero, True
    )
    middle = middle.astype(jnp.bfloat16).astype(jnp.float32)
    final, kept_one = layer_forward(
        middle, small_one[:2], own_taps(small_one), weights_one, False
    )
    queue = Queue()
    grad_middle, gains_one, taps_one = layer_backward(
        kept_one, cotangent * mask, small_one[:2], own_taps(small_one), weights_one, False, queue, tail
    )
    grad_middle = grad_middle.astype(jnp.bfloat16).astype(jnp.float32)
    grad_start, gains_zero, taps_zero = layer_backward(
        kept_zero, grad_middle, small_zero[:2], own_taps(small_zero), weights_zero, True, queue, tail
    )

    grads_one, grads_zero = queue.done[:2], queue.done[2:]

    def own_small(gains, taps):
        spot = jnp.zeros((taps.shape[0], model), jnp.float32)
        return jnp.concatenate([gains, lax.dynamic_update_slice_in_dim(spot, taps, offset, 1)], axis=0)

    sums = sum_all(jnp.stack([own_small(gains_zero, taps_zero), own_small(gains_one, taps_one)]))
    sums = lax.dynamic_index_in_dim(sums, core, 0, keepdims=True)

    final = final * mask
    ends_keep = jnp.where(lower, grad_start, final)
    ends_other = swap(jnp.where(lower, final, grad_start))
    ends = jnp.where(lower, jnp.stack([ends_keep, ends_other]), jnp.stack([ends_other, ends_keep]))

    def home(zero, one):
        mine = jnp.where(lower, zero, one)
        other = swap(jnp.where(lower, one, zero))
        return (jnp.where(lower, mine, other), jnp.where(lower, other, mine))

    def halves(low, high, axis):
        return jnp.concatenate([low, high], axis=axis).astype(jnp.float32)

    def pair_home(block):
        size = block.shape[1] // 2
        other = swap(block)
        low = jnp.where(lower, block, other)
        high = jnp.where(lower, other, block)
        return jnp.stack(
            [halves(low[:, :size], high[:, :size], 1), halves(low[:, size:], high[:, size:], 1)], axis=1
        )

    def split_pair(grads, tail):
        both = 2 * channels
        stop = grads.shape[1] - tail
        rest = jnp.concatenate([grads[:, :both], grads[:, stop - channels : stop]], axis=1)
        return (rest, grads[:, both : stop - channels], grads[:, stop:])

    attn_zero, pair_zero, down_zero = split_pair(grads_zero[1], tail)
    attn_one, pair_one, down_one = split_pair(grads_one[1], tail)
    low, high = home(attn_zero, attn_one)
    vgate_grad = jnp.stack(
        [
            halves(low[:, :channels], high[:, :channels], 1),
            halves(low[:, channels : 2 * channels], high[:, channels : 2 * channels], 1),
        ],
        axis=1,
    )
    out_grad = halves(low[:, 2 * channels :].T, high[:, 2 * channels :].T, 0)
    low_tail, high_tail = home(down_zero, down_one)

    def unpack(block, last):
        wide = block[:, main:]
        (gate, upper), (gate_rest, upper_rest) = gates(wide, units)
        down = jnp.concatenate([block[:, :main], wide[:, 2 * units :], last], axis=1)
        return (
            jnp.concatenate([gate, gate_rest], axis=1),
            jnp.concatenate([upper, upper_rest], axis=1),
            down.T,
        )

    low, high = home(grads_zero[0], grads_one[0])
    low, high = unpack(low, low_tail), unpack(high, high_tail)
    gate_up_grad = jnp.stack([halves(low[0], high[0], 1), halves(low[1], high[1], 1)], axis=1)
    down_grad = halves(low[2], high[2], 0)
    return (
        ends[None],
        sums[:, :2],
        sums[:, 2:],
        pair_home(pair_zero),
        pair_home(pair_one),
        vgate_grad[None],
        out_grad[None],
        gate_up_grad[None],
        down_grad[None],
    )


def solution(mesh):
    in_specs = (
        P("section", "dp", "tensor", None),
        P("dp"),
        P("section", None, None),
        P("section", None, None),
        P("dp", None, "tensor"),
        P("dp", None, "tensor"),
        P("section", "dp", None, "tensor"),
        P("section", "tensor", "dp"),
        P("section", "dp", None, "tensor"),
        P("section", "tensor", "dp"),
    )
    out_specs = (
        P("section", "dp", "tensor", None),
        P("section", None, None),
        P("section", None, None),
        P("dp", None, "tensor"),
        P("dp", None, "tensor"),
        P("section", "dp", None, "tensor"),
        P("section", "tensor", "dp"),
        P("section", "dp", None, "tensor"),
        P("section", "tensor", "dp"),
    )
    return jax.shard_map(body, mesh=mesh, in_specs=in_specs, out_specs=out_specs, check_vma=False)
```

```python
import functools
import math

import jax
import jax.numpy as jnp
from jax import lax
from jax.experimental import pallas as pl
from jax.experimental.layout import Layout, with_layout_constraint
from jax.experimental.pallas import tpu as pltpu
from jax.sharding import PartitionSpec as P

WIN = 64
HD = 112
LANES = 128
WIDE = 256

EPS = 1e-06


def silu_slope(value):
    sigma = jax.nn.sigmoid(value)
    return sigma * (1.0 + value * (1.0 - sigma))


def rms_rows(rows, gain):
    scale = lax.rsqrt(jnp.mean(rows * rows, axis=-1, keepdims=True) + EPS)
    return (scale, rows * scale * gain)


def rms_back(rows, scale, gain, grad):
    normal = rows * scale
    weighted = grad * gain
    inner = jnp.mean(weighted * normal, axis=-1, keepdims=True)
    return (scale * (weighted - normal * inner), jnp.sum(grad * normal, axis=0))


def causal_conv(values, taps):
    total = values * taps[0]
    for offset in range(1, taps.shape[0]):
        moved = jnp.pad(values[:, :-offset], ((0, 0), (offset, 0), (0, 0)))
        total = total + moved * taps[offset]
    return total


def conv_back(grad, values, taps):
    grad_values = grad * taps[0]
    grad_taps = [jnp.sum(grad * values, axis=(0, 1))]
    for offset in range(1, taps.shape[0]):
        moved = jnp.pad(grad[:, offset:], ((0, 0), (0, offset), (0, 0)))
        grad_values = grad_values + moved * taps[offset]
        grad_taps.append(jnp.sum(grad[:, offset:] * values[:, :-offset], axis=(0, 1)))
    return (grad_values, jnp.stack(grad_taps))


def swap(block):
    return lax.ppermute(block, "section", [(0, 1), (1, 0)])


def spread_pair(rows):
    mine = lax.all_gather(rows.astype(jnp.bfloat16), "tensor", axis=0, tiled=True)
    return (mine, swap(mine))


def spread(rows):
    return jnp.concatenate(spread_pair(rows), axis=0)


def collect(terms):
    length = terms.shape[0] // 2
    size = lax.axis_size("tensor")
    count = length // size
    index = lax.axis_index("tensor")
    arrived = swap(terms[length:].astype(jnp.bfloat16))
    part = terms[:length] + arrived.astype(jnp.float32)
    low = part.astype(jnp.bfloat16)
    total = lax.dynamic_slice_in_dim(part, index * count, count, 0)
    for offset in range(1, size):
        block = lax.dynamic_slice_in_dim(low, (index ^ offset) * count, count, 0)
        pairs = [(i, i ^ offset) for i in range(size)]
        total = total + lax.ppermute(block, "tensor", pairs).astype(jnp.float32)
    return total


def sum_all(block):
    for axis in ("section", "tensor", "dp"):
        size = lax.axis_size(axis)
        step = 1
        while step < size:
            pairs = [(i, i ^ step) for i in range(size)]
            block = block + lax.ppermute(block, axis, pairs)
            step *= 2
    return block


def widen(columns):
    return jnp.pad(columns, ((0, 0), (0, -columns.shape[1] % LANES)))


def dot(one, two):
    return jnp.dot(one, two, preferred_element_type=jnp.float32)


def dot_nt(one, two):
    return lax.dot_general(one, two, (((1,), (1,)), ((), ())), preferred_element_type=jnp.float32)


def dot_tn(one, two):
    return lax.dot_general(one, two, (((0,), (0,)), ((), ())), preferred_element_type=jnp.float32)


def heads_of(block, width):
    return block.reshape(2, block.shape[0] // 2, -1, width)


def score_parts(queries, keys, first):
    length = queries.shape[1]
    width = queries.shape[-1]
    scores = jnp.einsum(
        "sihc,sjhc->shij", queries, keys, preferred_element_type=jnp.float32
    ) / math.sqrt(width)
    place = jnp.arange(length)
    causal = place[None, :] <= place[:, None]
    if first:
        kernel = jnp.where(causal, 1.0 + scores + 0.5 * scores * scores, 0.0)
        total = jnp.sum(kernel, axis=-1, keepdims=True)
        slope = jnp.where(causal, (1.0 + scores) / total, 0.0)
        return (kernel / total, slope)
    allowed = causal & (place[:, None] - place[None, :] < WIN)
    probs = jax.nn.softmax(jnp.where(allowed, scores, -1e30), axis=-1)
    return (probs, probs)


def gates(halves, units):
    main = units // LANES * LANES
    stop = main + units
    return (
        (halves[:, :main], halves[:, main : 2 * main]),
        (halves[:, 2 * main : stop], halves[:, stop : 2 * units]),
    )


def attn_forward(rows, gain, taps, weights, first):
    mix, out_t, pair, down = weights
    channels = out_t.shape[1]
    width = mix.shape[1] // 2 - channels
    scale, normed = rms_rows(rows, gain)
    full = spread(normed)
    both = dot(full, mix)
    length = full.shape[0] // 2
    pre_values = both[:, :channels].reshape(2, length, channels)
    gate_mix = both[:, channels : 2 * channels]
    values = causal_conv(pre_values, taps).astype(jnp.bfloat16).reshape(2, length, -1, HD)
    head_width = width // (channels // HD)
    queries = heads_of(both[:, 2 * channels : 2 * channels + width].astype(jnp.bfloat16), head_width)
    keys = heads_of(both[:, 2 * channels + width :].astype(jnp.bfloat16), head_width)
    probs, slope = score_parts(queries, keys, first)
    mixed = jnp.einsum(
        "shij,sjhc->sihc", probs.astype(jnp.bfloat16), values, preferred_element_type=jnp.float32
    ).reshape(2 * length, channels)
    gated = (mixed * jax.nn.silu(gate_mix)).astype(jnp.bfloat16)
    hidden = rows + collect(dot_nt(gated, out_t))
    kept = (
        rows, scale, full, pre_values, gate_mix, values, queries, keys, probs, slope, mixed, gated,
    )
    return (hidden, kept)


def feed_forward(hidden, gain, weights):
    mix, out_t, pair, down = weights
    scale, normed = rms_rows(hidden, gain)
    full = spread(normed)
    halves = dot(full, pair)
    inner = jnp.concatenate(
        [(jax.nn.silu(gate) * upper).astype(jnp.bfloat16) for gate, upper in gates(halves, down.shape[1])],
        axis=1,
    )
    output = hidden + collect(dot_nt(inner, down))
    return (output, (hidden, scale, full, halves, inner))


def feed_backward(kept, grad_out, gain, weights, queue, tail):
    hidden, scale, full, halves, inner = kept
    mix, out_t, pair, down = weights
    units = down.shape[1]
    main = units // LANES * LANES
    branch = spread(grad_out)
    branch, grad_down = product_first(branch, inner, branch)
    grad_inner = dot(branch, down)
    parts = []
    for (gate, upper), grad in zip(gates(halves, units), (grad_inner[:, :main], grad_inner[:, main:])):
        parts.append((grad * upper * silu_slope(gate)).astype(jnp.bfloat16))
        parts.append((grad * jax.nn.silu(gate)).astype(jnp.bfloat16))
    filler = jnp.zeros((full.shape[0], pair.shape[1] - 2 * units), jnp.bfloat16)
    grad_halves = jnp.concatenate([*parts, filler], axis=1)
    grad_halves, grad_gate_up = product_first(full, grad_halves, grad_halves)
    rest = jnp.pad(grad_down[:, main : units - tail], ((0, 0), (2 * units, 0)))
    queue.scatter(grad_down[:, :main], grad_gate_up + rest)
    grad = collect(dot_nt(grad_halves, pair))
    back, grad_gain = rms_back(hidden, scale, gain, grad)
    return (grad_out + back, grad_gain, grad_down[:, units - tail :])


def feed_kernel(
    units, tail, near_ref, far_ref, near_grad_ref, far_grad_ref, feed_ref, last_ref,
    block_ref, rest_ref, halves_ref, inner_ref, rows_ref, grads_ref,
):
    main = units // LANES * LANES
    over = units - main
    length = near_ref.shape[0]
    rows_ref[:length] = near_ref[...]
    rows_ref[length:] = far_ref[...]
    grads_ref[:length] = near_grad_ref[...]
    grads_ref[length:] = far_grad_ref[...]
    rows = rows_ref[...]
    branch = grads_ref[...]

    def lanes(block):
        return lax.broadcasted_iota(jnp.int32, block.shape, 1)

    def parts(gate, upper, grad):
        sigma = jax.nn.sigmoid(gate)
        act = gate * sigma
        slope = sigma * (1.0 + gate * (1.0 - sigma))
        return (act * upper, grad * upper * slope, grad * act)

    for start in range(0, main, WIDE):
        first, second, third = (pl.ds(start + i * main, WIDE) for i in range(3))
        gate = dot(rows, feed_ref[:, second])
        upper = dot(rows, feed_ref[:, third])
        grad = dot(branch, feed_ref[:, first])
        inner, grad_gate, grad_upper = (part.astype(jnp.bfloat16) for part in parts(gate, upper, grad))
        inner_ref[:, first] = inner
        halves_ref[:, first] = grad_gate
        halves_ref[:, second] = grad_upper
        block_ref[:, first] = dot_tn(branch, inner).astype(jnp.bfloat16)
        block_ref[:, second] = dot_tn(rows, grad_gate).astype(jnp.bfloat16)
        block_ref[:, third] = dot_tn(rows, grad_upper).astype(jnp.bfloat16)

    ends = feed_ref[:, pl.ds(3 * main, WIDE)]
    both = dot(rows, ends)
    upper = pltpu.roll(both, WIDE - over, 1)
    grad = pltpu.roll(dot(branch, ends), WIDE - 2 * over, 1)[:, :LANES]
    more = pltpu.roll(dot(branch, last_ref[...]), over, 1)
    grad = jnp.where(lanes(grad) < over - tail, grad, more)
    inner, grad_gate, grad_upper = (
        jnp.where(lanes(part) < over, part, 0.0)
        for part in parts(both[:, :LANES], upper[:, :LANES], grad)
    )
    inner = inner.astype(jnp.bfloat16)
    inner_ref[:, pl.ds(main, over)] = inner[:, :over]
    empty = jnp.zeros_like(grad_gate)
    wide = jnp.concatenate([grad_gate, empty], axis=1)
    wide = wide + pltpu.roll(jnp.concatenate([grad_upper, empty], axis=1), over, 1)
    wide = wide.astype(jnp.bfloat16)
    halves_ref[:, pl.ds(2 * main, WIDE)] = wide
    down = dot_tn(branch, inner)
    moved = pltpu.roll(jnp.concatenate([down, jnp.zeros_like(down)], axis=1), 2 * over, 1)
    wide = dot_tn(rows, wide)
    block_ref[:, pl.ds(3 * main, WIDE)] = jnp.where(lanes(wide) < 2 * over, wide, moved).astype(jnp.bfloat16)
    rest_ref[...] = pltpu.roll(down, LANES - over + tail, 1)[:, :tail].astype(jnp.bfloat16)


def feed_both(units, tail, near, far, near_grad, far_grad, feed, attn):
    count, model = 2 * near.shape[0], near.shape[1]
    main = units // LANES * LANES
    shapes = (
        (model, feed.shape[1]),
        (model, tail),
        (count, feed.shape[1] - main),
        (count, units),
    )

    def whole(shape):
        return pl.BlockSpec(shape, lambda step: (0, 0))

    end = attn.shape[1] // LANES - 1
    return pl.pallas_call(
        functools.partial(feed_kernel, units, tail),
        grid=(1,),
        out_shape=[jax.ShapeDtypeStruct(shape, jnp.bfloat16) for shape in shapes],
        in_specs=[whole(block.shape) for block in (near, far, near_grad, far_grad, feed)]
        + [pl.BlockSpec((model, LANES), lambda step: (0, end))],
        out_specs=[whole(shape) for shape in shapes],
        scratch_shapes=[pltpu.VMEM((count, model), jnp.bfloat16)] * 2,
        compiler_params=pltpu.CompilerParams(vmem_limit_bytes=56 * 2**20),
        cost_estimate=pl.CostEstimate(
            flops=8 * count * model * feed.shape[1] // 2,
            bytes_accessed=20 * 2**20,
            transcendentals=count * units,
        ),
    )(near, far, near_grad, far_grad, feed, attn)


def attn_backward(kept, grad_hidden, gain, taps, weights, queue, rest):
    (
        rows, scale, full, pre_values, gate_mix, values, queries, keys, probs, slope, mixed, gated,
    ) = kept
    mix, out_t, pair, down = weights
    channels = out_t.shape[1]
    length = full.shape[0] // 2
    branch = spread(grad_hidden)
    branch, grad_outw = product_first(branch, gated, branch)
    grad_gated = dot(branch, out_t)
    grad_mixed = (grad_gated * jax.nn.silu(gate_mix)).astype(jnp.bfloat16)
    grad_mix_gate = (grad_gated * mixed * silu_slope(gate_mix)).astype(jnp.bfloat16)
    grad_heads = heads_of(grad_mixed, HD)
    low = probs.astype(jnp.bfloat16)
    grad_values = jnp.einsum("shij,sihc->sjhc", low, grad_heads, preferred_element_type=jnp.float32)
    grad_probs = jnp.einsum("sihc,sjhc->shij", grad_heads, values, preferred_element_type=jnp.float32)
    centred = grad_probs - jnp.sum(probs * grad_probs, axis=-1, keepdims=True)
    score_grad = (centred * slope).astype(jnp.bfloat16)
    root = math.sqrt(queries.shape[-1])
    grad_queries = jnp.einsum("shij,sjhc->sihc", score_grad, keys, preferred_element_type=jnp.float32)
    grad_keys = jnp.einsum("shij,sihc->sjhc", score_grad, queries, preferred_element_type=jnp.float32)
    grad_queries = (grad_queries / root).astype(jnp.bfloat16).reshape(2 * length, -1)
    grad_keys = (grad_keys / root).astype(jnp.bfloat16).reshape(2 * length, -1)
    grad_pre, grad_taps = conv_back(grad_values.reshape(2, length, channels), pre_values, taps)
    grad_pre = grad_pre.astype(jnp.bfloat16).reshape(2 * length, channels)
    grad_both = jnp.concatenate([grad_pre, grad_mix_gate, grad_queries, grad_keys], axis=1)
    grad_both, grad_attn = product_first(full, grad_both, grad_both)
    queue.scatter(grad_attn, grad_outw, rest)
    grad = collect(dot_nt(grad_both, mix))
    back, grad_gain = rms_back(rows, scale, gain, grad)
    return (grad_hidden + back, grad_gain, grad_taps)


def by_rows(block):
    return with_layout_constraint(block, Layout(major_to_minor=(0, 1)))


class Queue:
    def __init__(self):
        self.done = []

    def scatter(self, *grads):
        block = by_rows(jnp.concatenate(grads, axis=1) if len(grads) > 1 else grads[0])
        if self.done:
            block, self.done[-1] = lax.optimization_barrier((block, self.done[-1]))
        self.done.append(by_rows(lax.psum_scatter(block, "dp", scatter_dimension=0, tiled=True)))


def product_first(one, two, chain):
    grad = dot_tn(one, two).astype(jnp.bfloat16)
    return lax.optimization_barrier((chain, grad))


def body(
    boundary, lengths, norm_gains, conv_taps, lin_qk, win_qk, value_gate, out_weight, gate_up, down_weight
):
    core = lax.axis_index("section")
    index = lax.axis_index("tensor")
    lower = core == 0
    rows_dev, model = boundary.shape[2:]
    channels = value_gate.shape[-1] // 2
    units = gate_up.shape[-1] // 2
    main = units // LANES * LANES
    tail = -(3 * channels + lin_qk.shape[-1]) % LANES

    def half(block, axis, which):
        size = block.shape[axis] // 2
        return lax.dynamic_slice_in_dim(block, which * size, size, axis)

    def both_layers(build):
        mine = build(core)
        other = swap(build(1 - core))
        return (jnp.where(lower, mine, other), jnp.where(lower, other, mine))

    def attn_piece(which):
        values = half(value_gate[0], 2, which)
        last = half(down_weight[0], 0, which)[units - tail :]
        return jnp.concatenate(
            [values[:, 0], values[:, 1], half(out_weight[0], 0, which).T, last.T], axis=1
        )

    def feed_piece(which):
        pair = half(gate_up[0], 2, which)
        down = half(down_weight[0], 0, which).T
        return jnp.concatenate(
            [down[:, :main], pair[:, 0, :main], pair[:, 1, :main], pair[:, 0, main:], pair[:, 1, main:], down[:, main : units - tail]],
            axis=1,
        )

    def fetch(piece):
        return lax.all_gather(piece, "dp", axis=0, tiled=True)

    def with_pair(attn, pair):
        pair = half(pair, 2, core)
        both = 2 * channels
        return jnp.concatenate([attn[:, :both], pair[:, 0], pair[:, 1], attn[:, both:]], axis=1)

    def parts_of(feed, attn):
        stop = attn.shape[1] - tail
        down = jnp.concatenate([feed[:, :main], feed[:, main + 2 * units :], attn[:, stop:]], axis=1)
        return (attn[:, : stop - channels], attn[:, stop - channels : stop], feed[:, main:], down)

    attn_parts = both_layers(attn_piece)
    feed_parts = both_layers(feed_piece)
    attn_zero = fetch(with_pair(attn_parts[0], lin_qk))
    weights_zero = parts_of(fetch(feed_parts[0]), attn_zero)
    attn_one = fetch(with_pair(attn_parts[1], win_qk))
    feed_one = fetch(feed_parts[1])
    weights_one = parts_of(feed_one, attn_one)

    small = jnp.concatenate([norm_gains[0], conv_taps[0]], axis=0)
    small_other = swap(small)
    small_zero = jnp.where(lower, small, small_other)
    small_one = jnp.where(lower, small_other, small)
    offset = (2 * index + core) * channels

    def own_taps(block):
        return lax.dynamic_slice_in_dim(block[2:], offset, channels, 1)

    held = boundary[0]
    keep = lax.dynamic_index_in_dim(held, core, 0, keepdims=False)
    other = swap(lax.dynamic_index_in_dim(held, 1 - core, 0, keepdims=False))
    entering = jnp.where(lower, keep, other).astype(jnp.float32)
    cotangent = jnp.where(lower, other, keep).astype(jnp.float32)
    length = lax.dynamic_index_in_dim(lengths, core, 0, keepdims=False)
    place = index * rows_dev + jnp.arange(rows_dev)
    mask = (place < length).astype(jnp.float32)[:, None]

    queue = Queue()
    gains_zero, gains_one = small_zero[:2], small_one[:2]
    hidden, kept_zero = attn_forward(entering, gains_zero[0], own_taps(small_zero), weights_zero, True)
    middle, kept_feed = feed_forward(hidden, gains_zero[1], weights_zero)
    middle = middle.astype(jnp.bfloat16).astype(jnp.float32)

    hidden, kept_one = attn_forward(middle, gains_one[0], own_taps(small_one), weights_one, False)
    scale, normed = rms_rows(hidden, gains_one[1])
    grad_out = cotangent * mask
    block, rest, grad_halves, inner = feed_both(
        units, tail, *spread_pair(normed), *spread_pair(grad_out), feed_one, attn_one
    )
    queue.scatter(block)
    final = hidden + collect(dot_nt(inner, weights_one[3]))
    back, gain_two = rms_back(hidden, scale, gains_one[1], collect(dot_nt(grad_halves, weights_one[2])))
    grad_middle, gain_one, taps_one = attn_backward(
        kept_one, grad_out + back, gains_one[0], own_taps(small_one), weights_one, queue, rest
    )
    gains_one = jnp.stack([gain_one, gain_two])

    grad_middle = grad_middle.astype(jnp.bfloat16).astype(jnp.float32)
    grad_hidden, gain_two, rest = feed_backward(
        kept_feed, grad_middle, gains_zero[1], weights_zero, queue, tail
    )
    grad_start, gain_one, taps_zero = attn_backward(
        kept_zero, grad_hidden, gains_zero[0], own_taps(small_zero), weights_zero, queue, rest
    )
    gains_zero = jnp.stack([gain_one, gain_two])

    grads_one, grads_zero = queue.done[:2], queue.done[2:]

    def own_small(gains, taps):
        spot = jnp.zeros((taps.shape[0], model), jnp.float32)
        return jnp.concatenate([gains, lax.dynamic_update_slice_in_dim(spot, taps, offset, 1)], axis=0)

    sums = sum_all(jnp.stack([own_small(gains_zero, taps_zero), own_small(gains_one, taps_one)]))
    sums = lax.dynamic_index_in_dim(sums, core, 0, keepdims=True)

    final = final * mask
    ends_keep = jnp.where(lower, grad_start, final)
    ends_other = swap(jnp.where(lower, final, grad_start))
    ends = jnp.where(lower, jnp.stack([ends_keep, ends_other]), jnp.stack([ends_other, ends_keep]))

    def home(zero, one):
        mine = jnp.where(lower, zero, one)
        other = swap(jnp.where(lower, one, zero))
        return (jnp.where(lower, mine, other), jnp.where(lower, other, mine))

    def halves(low, high, axis):
        return jnp.concatenate([low, high], axis=axis).astype(jnp.float32)

    def pair_home(block):
        size = block.shape[1] // 2
        other = swap(block)
        low = jnp.where(lower, block, other)
        high = jnp.where(lower, other, block)
        return jnp.stack(
            [halves(low[:, :size], high[:, :size], 1), halves(low[:, size:], high[:, size:], 1)], axis=1
        )

    def split_pair(grads, tail):
        both = 2 * channels
        stop = grads.shape[1] - tail
        rest = jnp.concatenate([grads[:, :both], grads[:, stop - channels : stop]], axis=1)
        return (rest, grads[:, both : stop - channels], grads[:, stop:])

    attn_zero, pair_zero, down_zero = split_pair(grads_zero[1], tail)
    attn_one, pair_one, down_one = split_pair(grads_one[1], tail)
    low, high = home(attn_zero, attn_one)
    vgate_grad = jnp.stack(
        [
            halves(low[:, :channels], high[:, :channels], 1),
            halves(low[:, channels : 2 * channels], high[:, channels : 2 * channels], 1),
        ],
        axis=1,
    )
    out_grad = halves(low[:, 2 * channels :].T, high[:, 2 * channels :].T, 0)
    low_tail, high_tail = home(down_zero, down_one)

    def unpack(block, last):
        wide = block[:, main:]
        (gate, upper), (gate_rest, upper_rest) = gates(wide, units)
        down = jnp.concatenate([block[:, :main], wide[:, 2 * units :], last], axis=1)
        return (
            jnp.concatenate([gate, gate_rest], axis=1),
            jnp.concatenate([upper, upper_rest], axis=1),
            down.T,
        )

    low, high = home(grads_zero[0], grads_one[0])
    low, high = unpack(low, low_tail), unpack(high, high_tail)
    gate_up_grad = jnp.stack([halves(low[0], high[0], 1), halves(low[1], high[1], 1)], axis=1)
    down_grad = halves(low[2], high[2], 0)
    return (
        ends[None],
        sums[:, :2],
        sums[:, 2:],
        pair_home(pair_zero),
        pair_home(pair_one),
        vgate_grad[None],
        out_grad[None],
        gate_up_grad[None],
        down_grad[None],
    )


def solution(mesh):
    in_specs = (
        P("section", "dp", "tensor", None),
        P("dp"),
        P("section", None, None),
        P("section", None, None),
        P("dp", None, "tensor"),
        P("dp", None, "tensor"),
        P("section", "dp", None, "tensor"),
        P("section", "tensor", "dp"),
        P("section", "dp", None, "tensor"),
        P("section", "tensor", "dp"),
    )
    out_specs = (
        P("section", "dp", "tensor", None),
        P("section", None, None),
        P("section", None, None),
        P("dp", None, "tensor"),
        P("dp", None, "tensor"),
        P("section", "dp", None, "tensor"),
        P("section", "tensor", "dp"),
        P("section", "dp", None, "tensor"),
        P("section", "tensor", "dp"),
    )
    return jax.shard_map(body, mesh=mesh, in_specs=in_specs, out_specs=out_specs, check_vma=False)
```

```python
import functools
import math

import jax
import jax.numpy as jnp
from jax import lax
from jax.experimental import pallas as pl
from jax.experimental.layout import Layout, with_layout_constraint
from jax.experimental.pallas import tpu as pltpu
from jax.sharding import PartitionSpec as P

WIN = 64
HD = 112
LANES = 128
WIDE = 256
SUBLANES = 8

EPS = 1e-06


def silu_slope(value):
    sigma = jax.nn.sigmoid(value)
    return sigma * (1.0 + value * (1.0 - sigma))


def rms_rows(rows, gain):
    scale = lax.rsqrt(jnp.mean(rows * rows, axis=-1, keepdims=True) + EPS)
    return (scale, rows * scale * gain)


def rms_back(rows, scale, gain, grad):
    normal = rows * scale
    weighted = grad * gain
    inner = jnp.mean(weighted * normal, axis=-1, keepdims=True)
    return (scale * (weighted - normal * inner), jnp.sum(grad * normal, axis=0))


def swap(block):
    return lax.ppermute(block, "section", [(0, 1), (1, 0)])


def spread_pair(rows):
    mine = lax.all_gather(rows.astype(jnp.bfloat16), "tensor", axis=0, tiled=True)
    return (mine, swap(mine))


def spread(rows):
    return jnp.concatenate(spread_pair(rows), axis=0)


def collect(terms):
    length = terms.shape[0] // 2
    return collect_pair(terms[:length], terms[length:].astype(jnp.bfloat16))


def collect_pair(mine, other):
    size = lax.axis_size("tensor")
    count = mine.shape[0] // size
    index = lax.axis_index("tensor")
    part = mine + swap(other).astype(jnp.float32)
    low = part.astype(jnp.bfloat16)
    total = lax.dynamic_slice_in_dim(part, index * count, count, 0)
    for offset in range(1, size):
        block = lax.dynamic_slice_in_dim(low, (index ^ offset) * count, count, 0)
        pairs = [(i, i ^ offset) for i in range(size)]
        total = total + lax.ppermute(block, "tensor", pairs).astype(jnp.float32)
    return total


def sum_all(block):
    for axis in ("section", "tensor", "dp"):
        size = lax.axis_size(axis)
        step = 1
        while step < size:
            pairs = [(i, i ^ step) for i in range(size)]
            block = block + lax.ppermute(block, axis, pairs)
            step *= 2
    return block


def dot(one, two):
    return jnp.dot(one, two, preferred_element_type=jnp.float32)


def dot_nt(one, two):
    return lax.dot_general(one, two, (((1,), (1,)), ((), ())), preferred_element_type=jnp.float32)


def dot_tn(one, two):
    return lax.dot_general(one, two, (((0,), (0,)), ((), ())), preferred_element_type=jnp.float32)


def gates(halves, units):
    main = units // LANES * LANES
    stop = main + units
    return (
        (halves[:, :main], halves[:, main : 2 * main]),
        (halves[:, 2 * main : stop], halves[:, stop : 2 * units]),
    )


def lanes(block):
    return lax.broadcasted_iota(jnp.int32, block.shape, 1)


def forward_kernel(units, tail, near_ref, far_ref, feed_ref, last_ref, mine_ref, other_ref, rows_ref, inner_ref):
    main = units // LANES * LANES
    over = units - main
    length = near_ref.shape[0]
    rows_ref[:length] = near_ref[...]
    rows_ref[length:] = far_ref[...]
    rows = rows_ref[...]
    for start in range(0, main, WIDE):
        gate = dot(rows, feed_ref[:, pl.ds(main + start, WIDE)])
        upper = dot(rows, feed_ref[:, pl.ds(2 * main + start, WIDE)])
        inner_ref[:, pl.ds(start, WIDE)] = (jax.nn.silu(gate) * upper).astype(jnp.bfloat16)
    ends = feed_ref[:, pl.ds(3 * main, WIDE)]
    both = dot(rows, ends)
    upper = pltpu.roll(both, WIDE - over, 1)
    inner = jax.nn.silu(both[:, :LANES]) * upper[:, :LANES]
    inner = jnp.where(lanes(inner) < over, inner, 0.0)
    low = pltpu.roll(jnp.concatenate([inner, jnp.zeros_like(inner)], axis=1), 2 * over, 1)
    low = jnp.where(lanes(low) < 2 * over, 0.0, low).astype(jnp.bfloat16)
    high = pltpu.roll(inner, LANES - over, 1)
    high = jnp.where(lanes(high) < LANES - tail, 0.0, high).astype(jnp.bfloat16)
    terms = dot_nt(inner_ref[...], feed_ref[:, pl.ds(0, main)]) + dot_nt(low, ends) + dot_nt(high, last_ref[...])
    mine_ref[...] = terms[:length]
    other_ref[...] = terms[length:].astype(jnp.bfloat16)


def feed_terms(units, tail, near, far, feed, attn):
    length, model = near.shape
    main = units // LANES * LANES
    width = 3 * units - tail
    end = attn.shape[1] // LANES - 1

    def whole(shape):
        return pl.BlockSpec(shape, lambda step: (0, 0), pipeline_mode=pl.Buffered(1))

    return pl.pallas_call(
        functools.partial(forward_kernel, units, tail),
        grid=(1,),
        out_shape=[
            jax.ShapeDtypeStruct((length, model), jnp.float32),
            jax.ShapeDtypeStruct((length, model), jnp.bfloat16),
        ],
        in_specs=[
            whole((length, model)),
            whole((length, model)),
            whole((model, width)),
            pl.BlockSpec((model, LANES), lambda step: (0, end)),
        ],
        out_specs=[whole((length, model))] * 2,
        scratch_shapes=[
            pltpu.VMEM((2 * length, model), jnp.bfloat16),
            pltpu.VMEM((2 * length, main), jnp.bfloat16),
        ],
        compiler_params=pltpu.CompilerParams(vmem_limit_bytes=48 * 2**20),
        cost_estimate=pl.CostEstimate(flops=2**20, bytes_accessed=2**16, transcendentals=0),
    )(near, far, feed, attn)


def feed_kernel(
    units, tail, near_ref, far_ref, near_grad_ref, far_grad_ref, feed_ref, last_ref, *refs
):
    extras, (block_ref, rest_ref, halves_ref, inner_ref, rows_ref, grads_ref) = refs[:-6], refs[-6:]
    main = units // LANES * LANES
    over = units - main
    base = 0
    for extra in extras:
        block_ref[:, pl.ds(base, extra.shape[1])] = extra[...]
        base += extra.shape[1]

    def give(column, value):
        block_ref[:, pl.ds(base + column, WIDE)] = value.astype(jnp.bfloat16)

    length = near_ref.shape[0]
    rows_ref[:length] = near_ref[...]
    rows_ref[length:] = far_ref[...]
    grads_ref[:length] = near_grad_ref[...]
    grads_ref[length:] = far_grad_ref[...]
    rows = rows_ref[...]
    branch = grads_ref[...]

    def parts(gate, upper, grad):
        sigma = jax.nn.sigmoid(gate)
        act = gate * sigma
        slope = sigma * (1.0 + gate * (1.0 - sigma))
        return (act * upper, grad * upper * slope, grad * act)

    for start in range(0, main, WIDE):
        places = tuple(start + i * main for i in range(3))
        first, second, third = (pl.ds(place, WIDE) for place in places)
        gate = dot(rows, feed_ref[:, second])
        upper = dot(rows, feed_ref[:, third])
        grad = dot(branch, feed_ref[:, first])
        inner, grad_gate, grad_upper = (part.astype(jnp.bfloat16) for part in parts(gate, upper, grad))
        inner_ref[:, first] = inner
        halves_ref[:, first] = grad_gate
        halves_ref[:, second] = grad_upper
        give(places[0], dot_tn(branch, inner))
        give(places[1], dot_tn(rows, grad_gate))
        give(places[2], dot_tn(rows, grad_upper))

    ends = feed_ref[:, pl.ds(3 * main, WIDE)]
    both = dot(rows, ends)
    upper = pltpu.roll(both, WIDE - over, 1)
    grad = pltpu.roll(dot(branch, ends), WIDE - 2 * over, 1)[:, :LANES]
    more = pltpu.roll(dot(branch, last_ref[...]), over, 1)
    grad = jnp.where(lanes(grad) < over - tail, grad, more)
    inner, grad_gate, grad_upper = (
        jnp.where(lanes(part) < over, part, 0.0)
        for part in parts(both[:, :LANES], upper[:, :LANES], grad)
    )
    inner = inner.astype(jnp.bfloat16)
    inner_ref[:, pl.ds(main, over)] = inner[:, :over]
    empty = jnp.zeros_like(grad_gate)
    wide = jnp.concatenate([grad_gate, empty], axis=1)
    wide = wide + pltpu.roll(jnp.concatenate([grad_upper, empty], axis=1), over, 1)
    wide = wide.astype(jnp.bfloat16)
    halves_ref[:, pl.ds(2 * main, WIDE)] = wide
    down = dot_tn(branch, inner)
    moved = pltpu.roll(jnp.concatenate([down, jnp.zeros_like(down)], axis=1), 2 * over, 1)
    wide = dot_tn(rows, wide)
    give(3 * main, jnp.where(lanes(wide) < 2 * over, wide, moved))
    moved = pltpu.roll(jnp.concatenate([down, jnp.zeros_like(down)], axis=1), WIDE - over, 1)
    rest_ref[...] = jnp.where(lanes(moved) < WIDE - tail, 0.0, moved).astype(jnp.bfloat16)


def feed_both(units, tail, near, far, near_grad, far_grad, feed, attn, *extras):
    count, model = 2 * near.shape[0], near.shape[1]
    main = units // LANES * LANES
    width = 3 * units - tail
    shapes = (
        (model, width + sum(extra.shape[1] for extra in extras)),
        (model, WIDE),
        (count, width - main),
        (count, units),
    )
    blocks = (near, far, near_grad, far_grad)

    def whole(shape):
        return pl.BlockSpec(shape, lambda step: (0, 0), pipeline_mode=pl.Buffered(1))

    end = attn.shape[1] // LANES - 1
    return pl.pallas_call(
        functools.partial(feed_kernel, units, tail),
        grid=(1,),
        out_shape=[jax.ShapeDtypeStruct(shape, jnp.bfloat16) for shape in shapes],
        in_specs=[whole(block.shape) for block in blocks]
        + [whole((model, width)), pl.BlockSpec((model, LANES), lambda step: (0, end))]
        + [whole(extra.shape) for extra in extras],
        out_specs=[whole(shape) for shape in shapes],
        scratch_shapes=[pltpu.VMEM((count, model), jnp.bfloat16)] * 2,
        compiler_params=pltpu.CompilerParams(vmem_limit_bytes=56 * 2**20),
        cost_estimate=pl.CostEstimate(
            flops=4 * count * model * width,
            bytes_accessed=20 * 2**20,
            transcendentals=count * units,
        ),
    )(*blocks, feed, attn, *extras)


def take(block, column, width):
    base = column // LANES * LANES
    shift = column - base
    stop = base + -(-(shift + width) // LANES) * LANES
    part = block[:, base:stop]
    if shift:
        part = pltpu.roll(part, stop - base - shift, 1)
    part = part[:, : -(-width // LANES) * LANES]
    return jnp.where(lanes(part) < width, part, 0.0)


def put(target, rows, column, width, part):
    base = column // LANES * LANES
    shift = column - base
    size = -(-(shift + width) // LANES) * LANES
    if size > part.shape[1]:
        empty = jnp.zeros((part.shape[0], size - part.shape[1]), part.dtype)
        part = jnp.concatenate([part, empty], axis=1)
    if shift:
        part = pltpu.roll(part, shift, 1)
    target[rows, pl.ds(base, size)] += part


def moved(block, distance):
    count = block.shape[0]
    if distance == 0:
        return block
    row = lax.broadcasted_iota(jnp.int32, block.shape, 0)
    rolled = pltpu.roll(block, distance % count, 0)
    inside = row >= distance if distance > 0 else row < count + distance
    return jnp.where(inside, rolled, 0.0)


def mixer_parts(both, taps, channels, first):
    length = both.shape[0]
    heads = channels // HD
    width = (both.shape[1] - 2 * channels) // (2 * heads)
    pre_values = take(both, 0, channels)
    values = sum(moved(pre_values, tap) * taps[tap : tap + 1] for tap in range(3))
    values = values.astype(jnp.bfloat16).astype(jnp.float32)
    gate = take(both, channels, channels)
    query = lax.broadcasted_iota(jnp.int32, (length, length), 0)
    key = lax.broadcasted_iota(jnp.int32, (length, length), 1)
    allowed = key <= query
    if not first:
        allowed = allowed & (query - key < WIN)
    parts = []
    for head in range(heads):
        queries = take(both, 2 * channels + head * width, width).astype(jnp.bfloat16)
        keys = take(both, 2 * channels + (heads + head) * width, width).astype(jnp.bfloat16)
        scores = dot_nt(queries, keys) / math.sqrt(width)
        if first:
            kernel = jnp.where(allowed, 1.0 + scores + 0.5 * scores * scores, 0.0)
            total = jnp.sum(kernel, axis=-1, keepdims=True)
            probs = kernel / total
            slope = jnp.where(allowed, (1.0 + scores) / total, 0.0)
        else:
            scores = jnp.where(allowed, scores, -1e30)
            kernel = jnp.exp(scores - jnp.max(scores, axis=-1, keepdims=True))
            probs = kernel / jnp.sum(kernel, axis=-1, keepdims=True)
            slope = probs
        own = take(values, head * HD, HD).astype(jnp.bfloat16)
        parts.append((queries, keys, probs, slope, own, dot(probs.astype(jnp.bfloat16), own)))
    return (pre_values, gate, parts)


def join(parts):
    empty = jnp.zeros_like(parts[0])
    total = 0.0
    for head, part in enumerate(parts):
        part = jnp.concatenate([part, empty], axis=1)
        total = total + (pltpu.roll(part, head * HD, 1) if head else part)
    return total


def mixer_kernel(
    channels, first, near_ref, far_ref, attn_ref, taps_ref, mine_ref, other_ref, both_ref, gated_ref
):
    length = near_ref.shape[0]
    stop = both_ref.shape[1]
    for index, rows in enumerate((near_ref, far_ref)):
        both = dot(rows[...], attn_ref[:, pl.ds(0, stop)])
        both_ref[pl.ds(index * length, length), :] = both
        _, gate, parts = mixer_parts(both, taps_ref[...], channels, first)
        gated = (join([part[-1] for part in parts]) * gate * jax.nn.sigmoid(gate)).astype(jnp.bfloat16)
        gated_ref[pl.ds(index * length, length), :] = gated
        terms = dot_nt(gated, attn_ref[:, pl.ds(stop, WIDE)])
        if index == 0:
            mine_ref[...] = terms
        else:
            other_ref[...] = terms.astype(jnp.bfloat16)


def mixer_back_kernel(
    channels, first, near_ref, far_ref, near_grad_ref, far_grad_ref, attn_ref, taps_ref, both_ref,
    gated_ref, rest_ref, block_ref, mine_ref, other_ref, taps_grad_ref, rows_ref, grads_ref, sums_ref, low_ref,
):
    length = near_ref.shape[0]
    stop = both_ref.shape[1]
    heads = channels // HD
    width = (stop - 2 * channels) // (2 * heads)
    taps = taps_ref[...]
    sums_ref[...] = jnp.zeros_like(sums_ref)
    taps_grad = [0.0] * 3
    rows_ref[:length] = near_ref[...]
    rows_ref[length:] = far_ref[...]
    grads_ref[:length] = near_grad_ref[...]
    grads_ref[length:] = far_grad_ref[...]
    for index in range(2):
        rows = pl.ds(index * length, length)
        pre_values, gate, parts = mixer_parts(both_ref[rows, :], taps, channels, first)
        mixed = join([part[-1] for part in parts])
        grad = dot(grads_ref[rows, :], attn_ref[:, pl.ds(stop, WIDE)])
        grad = jnp.where(lanes(grad) < channels, grad, 0.0)
        sigma = jax.nn.sigmoid(gate)
        grad_mixed = (grad * (gate * sigma)).astype(jnp.bfloat16).astype(jnp.float32)
        grad_gate = (grad * mixed * silu_slope(gate)).astype(jnp.bfloat16).astype(jnp.float32)
        put(sums_ref, rows, channels, channels, grad_gate)
        grad_values = []
        for head, (queries, keys, probs, slope, own, _) in enumerate(parts):
            part = take(grad_mixed, head * HD, HD).astype(jnp.bfloat16)
            grad_values.append(dot_tn(probs.astype(jnp.bfloat16), part))
            grad_probs = dot_nt(part, own)
            centred = grad_probs - jnp.sum(probs * grad_probs, axis=-1, keepdims=True)
            score_grad = (centred * slope).astype(jnp.bfloat16)
            for place, value in (
                (head, dot(score_grad, keys)),
                (heads + head, dot_tn(score_grad, queries)),
            ):
                value = (value / math.sqrt(width)).astype(jnp.bfloat16).astype(jnp.float32)
                put(sums_ref, rows, 2 * channels + place * width, width, value)
        grad_values = join(grad_values)
        grad_pre = sum(moved(grad_values, -tap) * taps[tap : tap + 1] for tap in range(3))
        put(sums_ref, rows, 0, channels, grad_pre.astype(jnp.bfloat16).astype(jnp.float32))
        for tap in range(3):
            taps_grad[tap] = taps_grad[tap] + jnp.sum(
                grad_values * moved(pre_values, tap), axis=0, keepdims=True
            )
    for tap in range(3):
        taps_grad_ref[pl.ds(tap, 1), :] = taps_grad[tap]
    low_ref[...] = sums_ref[...].astype(jnp.bfloat16)
    for column in range(0, stop, LANES):
        size = min(WIDE, stop - column)
        if column % WIDE:
            continue
        place = pl.ds(column, size)
        block_ref[:, place] = dot_tn(rows_ref[...], low_ref[:, place]).astype(jnp.bfloat16)
    last = dot_tn(grads_ref[...], gated_ref[...]).astype(jnp.bfloat16)
    block_ref[:, pl.ds(stop, WIDE)] = last + rest_ref[...]
    for index in range(2):
        terms = dot_nt(low_ref[pl.ds(index * length, length), :], attn_ref[:, pl.ds(0, stop)])
        if index == 0:
            mine_ref[...] = terms
        else:
            other_ref[...] = terms.astype(jnp.bfloat16)


def whole_call(kernel, inputs, shapes, scratch, flops):
    def whole(shape):
        return pl.BlockSpec(shape, lambda step: (0,) * len(shape), pipeline_mode=pl.Buffered(1))

    return pl.pallas_call(
        kernel,
        grid=(1,),
        out_shape=[jax.ShapeDtypeStruct(shape, kind) for shape, kind in shapes],
        in_specs=[whole(block.shape) for block in inputs],
        out_specs=[whole(shape) for shape, _ in shapes],
        scratch_shapes=[pltpu.VMEM(shape, kind) for shape, kind in scratch],
        compiler_params=pltpu.CompilerParams(vmem_limit_bytes=56 * 2**20),
        cost_estimate=pl.CostEstimate(flops=flops, bytes_accessed=2**16, transcendentals=0),
    )(*inputs)


def mixer_forward(channels, first, near, far, attn, taps):
    length, model = near.shape
    stop = attn.shape[1] - WIDE
    shapes = (
        ((length, model), jnp.float32),
        ((length, model), jnp.bfloat16),
        ((2 * length, stop), jnp.float32),
        ((2 * length, WIDE), jnp.bfloat16),
    )
    kernel = functools.partial(mixer_kernel, channels, first)
    return whole_call(kernel, (near, far, attn, taps), shapes, (), 2**20)


def mixer_backward(channels, first, near, far, near_grad, far_grad, attn, taps, both, gated, rest):
    length, model = near.shape
    stop = both.shape[1]
    shapes = (
        ((model, stop + WIDE), jnp.bfloat16),
        ((length, model), jnp.float32),
        ((length, model), jnp.bfloat16),
        (taps.shape, jnp.float32),
    )
    scratch = (
        ((2 * length, model), jnp.bfloat16),
        ((2 * length, model), jnp.bfloat16),
        ((2 * length, stop), jnp.float32),
        ((2 * length, stop), jnp.bfloat16),
    )
    inputs = (near, far, near_grad, far_grad, attn, taps, both, gated, rest)
    return whole_call(functools.partial(mixer_back_kernel, channels, first), inputs, shapes, scratch, 2**20)


def by_rows(block):
    return with_layout_constraint(block, Layout(major_to_minor=(0, 1)))


class Queue:
    def __init__(self):
        self.done = []

    def scatter(self, *grads):
        block = by_rows(jnp.concatenate(grads, axis=1) if len(grads) > 1 else grads[0])
        if self.done:
            block, self.done[-1] = lax.optimization_barrier((block, self.done[-1]))
        self.done.append(by_rows(lax.psum_scatter(block, "dp", scatter_dimension=0, tiled=True)))


def body(
    boundary, lengths, norm_gains, conv_taps, lin_qk, win_qk, value_gate, out_weight, gate_up, down_weight
):
    core = lax.axis_index("section")
    index = lax.axis_index("tensor")
    lower = core == 0
    rows_dev, model = boundary.shape[2:]
    channels = value_gate.shape[-1] // 2
    units = gate_up.shape[-1] // 2
    main = units // LANES * LANES
    tail = -(3 * channels + lin_qk.shape[-1]) % LANES

    def half(block, axis, which):
        size = block.shape[axis] // 2
        return lax.dynamic_slice_in_dim(block, which * size, size, axis)

    def both_layers(build):
        mine = build(core)
        other = swap(build(1 - core))
        return (jnp.where(lower, mine, other), jnp.where(lower, other, mine))

    def attn_piece(which):
        values = half(value_gate[0], 2, which)
        last = half(down_weight[0], 0, which)[units - tail :]
        return jnp.concatenate(
            [values[:, 0], values[:, 1], half(out_weight[0], 0, which).T, last.T], axis=1
        )

    def feed_piece(which):
        pair = half(gate_up[0], 2, which)
        down = half(down_weight[0], 0, which).T
        return jnp.concatenate(
            [down[:, :main], pair[:, 0, :main], pair[:, 1, :main], pair[:, 0, main:], pair[:, 1, main:], down[:, main : units - tail]],
            axis=1,
        )

    def fetch(piece):
        return lax.all_gather(piece, "dp", axis=0, tiled=True)

    def with_pair(attn, pair):
        pair = half(pair, 2, core)
        both = 2 * channels
        return jnp.concatenate([attn[:, :both], pair[:, 0], pair[:, 1], attn[:, both:]], axis=1)

    attn_parts = both_layers(attn_piece)
    feed_parts = both_layers(feed_piece)
    attn_zero = fetch(with_pair(attn_parts[0], lin_qk))
    packed = fetch(jnp.concatenate([feed_parts[0], with_pair(attn_parts[1], win_qk)], axis=1))
    split = feed_parts[0].shape[1]
    attn_one = packed[:, split:]
    feed_one = fetch(feed_parts[1])
    down_one = jnp.concatenate(
        [feed_one[:, :main], feed_one[:, main + 2 * units :], attn_one[:, attn_one.shape[1] - tail :]], axis=1
    )

    small = jnp.concatenate([norm_gains[0], conv_taps[0]], axis=0)
    small_other = swap(small)
    small_zero = jnp.where(lower, small, small_other)
    small_one = jnp.where(lower, small_other, small)
    offset = (2 * index + core) * channels

    def own_taps(block):
        own = lax.dynamic_slice_in_dim(block[2:], offset, channels, 1)
        return jnp.pad(own, ((0, -own.shape[0] % SUBLANES), (0, WIDE - channels)))

    held = boundary[0]
    keep = lax.dynamic_index_in_dim(held, core, 0, keepdims=False)
    other = swap(lax.dynamic_index_in_dim(held, 1 - core, 0, keepdims=False))
    entering = jnp.where(lower, keep, other).astype(jnp.float32)
    cotangent = jnp.where(lower, other, keep).astype(jnp.float32)
    length = lax.dynamic_index_in_dim(lengths, core, 0, keepdims=False)
    place = index * rows_dev + jnp.arange(rows_dev)
    mask = (place < length).astype(jnp.float32)[:, None]

    queue = Queue()
    gains_zero, gains_one = small_zero[:2], small_one[:2]
    taps_zero, taps_one = own_taps(small_zero), own_taps(small_one)

    def mix(rows, gain, attn, taps, first):
        scale, normed = rms_rows(rows, gain)
        near, far = spread_pair(normed)
        mine, other, both, gated = mixer_forward(channels, first, near, far, attn, taps)
        return (rows + collect_pair(mine, other), (rows, scale, near, far, both, gated))

    def mix_back(kept, grad_out, gain, attn, taps, rest, first):
        rows, scale, near, far, both, gated = kept
        block, mine, other, grad_taps = mixer_backward(
            channels, first, near, far, *spread_pair(grad_out), attn, taps, both, gated, rest
        )
        back, grad_gain = rms_back(rows, scale, gain, collect_pair(mine, other))
        return (block, grad_out + back, grad_gain, grad_taps[: conv_taps.shape[1], :channels])

    hidden, kept_zero = mix(entering, gains_zero[0], attn_zero, taps_zero, True)
    scale, normed = rms_rows(hidden, gains_zero[1])
    near, far = spread_pair(normed)
    kept_feed = (hidden, scale, near, far)
    middle = hidden + collect_pair(*feed_terms(units, tail, near, far, packed, attn_zero))
    middle = middle.astype(jnp.bfloat16).astype(jnp.float32)

    hidden, kept_one = mix(middle, gains_one[0], attn_one, taps_one, False)
    scale, normed = rms_rows(hidden, gains_one[1])
    grad_out = cotangent * mask
    block, rest, grad_halves, inner = feed_both(
        units, tail, *spread_pair(normed), *spread_pair(grad_out), feed_one, packed
    )
    queue.scatter(block)
    final = hidden + collect(dot_nt(inner, down_one))
    back, gain_two = rms_back(hidden, scale, gains_one[1], collect(dot_nt(grad_halves, feed_one[:, main:])))
    attn_grads, grad_middle, gain_one, taps_one = mix_back(
        kept_one, grad_out + back, gains_one[0], attn_one, taps_one, rest, False
    )
    gains_one = jnp.stack([gain_one, gain_two])

    grad_middle = grad_middle.astype(jnp.bfloat16).astype(jnp.float32)
    hidden, scale, near, far = kept_feed
    block, rest, grad_halves, _ = feed_both(
        units, tail, near, far, *spread_pair(grad_middle), packed, attn_zero, attn_grads
    )
    queue.scatter(block)
    terms = dot_nt(grad_halves, packed[:, main:split])
    back, gain_two = rms_back(hidden, scale, gains_zero[1], collect(terms))
    attn_grads, grad_start, gain_one, taps_zero = mix_back(
        kept_zero, grad_middle + back, gains_zero[0], attn_zero, taps_zero, rest, True
    )
    queue.scatter(attn_grads)
    gains_zero = jnp.stack([gain_one, gain_two])

    edge = attn_one.shape[1]
    grads_one = (queue.done[0], queue.done[1][:, :edge])
    grads_zero = (queue.done[1][:, edge:], queue.done[2])

    def own_small(gains, taps):
        spot = jnp.zeros((taps.shape[0], model), jnp.float32)
        return jnp.concatenate([gains, lax.dynamic_update_slice_in_dim(spot, taps, offset, 1)], axis=0)

    sums = sum_all(jnp.stack([own_small(gains_zero, taps_zero), own_small(gains_one, taps_one)]))
    sums = lax.dynamic_index_in_dim(sums, core, 0, keepdims=True)

    final = final * mask
    ends_keep = jnp.where(lower, grad_start, final)
    ends_other = swap(jnp.where(lower, final, grad_start))
    ends = jnp.where(lower, jnp.stack([ends_keep, ends_other]), jnp.stack([ends_other, ends_keep]))

    def home(zero, one):
        mine = jnp.where(lower, zero, one)
        other = swap(jnp.where(lower, one, zero))
        return (jnp.where(lower, mine, other), jnp.where(lower, other, mine))

    def halves(low, high, axis):
        return jnp.concatenate([low, high], axis=axis).astype(jnp.float32)

    def pair_home(block):
        size = block.shape[1] // 2
        other = swap(block)
        low = jnp.where(lower, block, other)
        high = jnp.where(lower, other, block)
        return jnp.stack(
            [halves(low[:, :size], high[:, :size], 1), halves(low[:, size:], high[:, size:], 1)], axis=1
        )

    def split_pair(grads, tail):
        both = 2 * channels
        stop = grads.shape[1] - tail
        rest = jnp.concatenate([grads[:, :both], grads[:, stop - channels : stop]], axis=1)
        return (rest, grads[:, both : stop - channels], grads[:, stop:])

    attn_zero, pair_zero, down_zero = split_pair(grads_zero[1], tail)
    attn_one, pair_one, down_one = split_pair(grads_one[1], tail)
    low, high = home(attn_zero, attn_one)
    vgate_grad = jnp.stack(
        [
            halves(low[:, :channels], high[:, :channels], 1),
            halves(low[:, channels : 2 * channels], high[:, channels : 2 * channels], 1),
        ],
        axis=1,
    )
    out_grad = halves(low[:, 2 * channels :].T, high[:, 2 * channels :].T, 0)
    low_tail, high_tail = home(down_zero, down_one)

    def unpack(block, last):
        wide = block[:, main:]
        (gate, upper), (gate_rest, upper_rest) = gates(wide, units)
        down = jnp.concatenate([block[:, :main], wide[:, 2 * units :], last], axis=1)
        return (
            jnp.concatenate([gate, gate_rest], axis=1),
            jnp.concatenate([upper, upper_rest], axis=1),
            down.T,
        )

    low, high = home(grads_zero[0], grads_one[0])
    low, high = unpack(low, low_tail), unpack(high, high_tail)
    gate_up_grad = jnp.stack([halves(low[0], high[0], 1), halves(low[1], high[1], 1)], axis=1)
    down_grad = halves(low[2], high[2], 0)
    return (
        ends[None],
        sums[:, :2],
        sums[:, 2:],
        pair_home(pair_zero),
        pair_home(pair_one),
        vgate_grad[None],
        out_grad[None],
        gate_up_grad[None],
        down_grad[None],
    )


def solution(mesh):
    in_specs = (
        P("section", "dp", "tensor", None),
        P("dp"),
        P("section", None, None),
        P("section", None, None),
        P("dp", None, "tensor"),
        P("dp", None, "tensor"),
        P("section", "dp", None, "tensor"),
        P("section", "tensor", "dp"),
        P("section", "dp", None, "tensor"),
        P("section", "tensor", "dp"),
    )
    out_specs = (
        P("section", "dp", "tensor", None),
        P("section", None, None),
        P("section", None, None),
        P("dp", None, "tensor"),
        P("dp", None, "tensor"),
        P("section", "dp", None, "tensor"),
        P("section", "tensor", "dp"),
        P("section", "dp", None, "tensor"),
        P("section", "tensor", "dp"),
    )
    return jax.shard_map(body, mesh=mesh, in_specs=in_specs, out_specs=out_specs, check_vma=False)
```

```python
import functools
import math

import jax
import jax.numpy as jnp
from jax import lax
from jax.experimental import pallas as pl
from jax.experimental.layout import Layout, with_layout_constraint
from jax.experimental.pallas import tpu as pltpu
from jax.sharding import PartitionSpec as P

WIN = 64
HD = 112
LANES = 128
WIDE = 256
SUBLANES = 8

EPS = 1e-06


def silu_slope(value):
    sigma = jax.nn.sigmoid(value)
    return sigma * (1.0 + value * (1.0 - sigma))


def rms_rows(rows, gain):
    scale = lax.rsqrt(jnp.mean(rows * rows, axis=-1, keepdims=True) + EPS)
    return (scale, rows * scale * gain)


def rms_back(rows, scale, gain, grad):
    normal = rows * scale
    weighted = grad * gain
    inner = jnp.mean(weighted * normal, axis=-1, keepdims=True)
    return (scale * (weighted - normal * inner), jnp.sum(grad * normal, axis=0))


def swap(block):
    return lax.ppermute(block, "section", [(0, 1), (1, 0)])


def spread_pair(rows):
    mine = lax.all_gather(rows.astype(jnp.bfloat16), "tensor", axis=0, tiled=True)
    return (mine, swap(mine))


def spread(rows):
    return jnp.concatenate(spread_pair(rows), axis=0)


def collect(terms):
    length = terms.shape[0] // 2
    return collect_pair(terms[:length], terms[length:].astype(jnp.bfloat16))


def collect_pair(mine, other):
    size = lax.axis_size("tensor")
    count = mine.shape[0] // size
    index = lax.axis_index("tensor")
    part = mine + swap(other).astype(jnp.float32)
    low = part.astype(jnp.bfloat16)
    total = lax.dynamic_slice_in_dim(part, index * count, count, 0)
    for offset in range(1, size):
        block = lax.dynamic_slice_in_dim(low, (index ^ offset) * count, count, 0)
        pairs = [(i, i ^ offset) for i in range(size)]
        total = total + lax.ppermute(block, "tensor", pairs).astype(jnp.float32)
    return total


def sum_all(block):
    for axis in ("section", "tensor", "dp"):
        size = lax.axis_size(axis)
        step = 1
        while step < size:
            pairs = [(i, i ^ step) for i in range(size)]
            block = block + lax.ppermute(block, axis, pairs)
            step *= 2
    return block


def dot(one, two):
    return jnp.dot(one, two, preferred_element_type=jnp.float32)


def dot_nt(one, two):
    return lax.dot_general(one, two, (((1,), (1,)), ((), ())), preferred_element_type=jnp.float32)


def dot_tn(one, two):
    return lax.dot_general(one, two, (((0,), (0,)), ((), ())), preferred_element_type=jnp.float32)


def gates(halves, units):
    main = units // LANES * LANES
    stop = main + units
    return (
        (halves[:, :main], halves[:, main : 2 * main]),
        (halves[:, 2 * main : stop], halves[:, stop : 2 * units]),
    )


def lanes(block):
    return lax.broadcasted_iota(jnp.int32, block.shape, 1)


def forward_kernel(units, tail, near_ref, far_ref, feed_ref, last_ref, mine_ref, other_ref, rows_ref, inner_ref):
    main = units // LANES * LANES
    over = units - main
    length = near_ref.shape[0]
    rows_ref[:length] = near_ref[...]
    rows_ref[length:] = far_ref[...]
    rows = rows_ref[...]
    for start in range(0, main, WIDE):
        gate = dot(rows, feed_ref[:, pl.ds(main + start, WIDE)])
        upper = dot(rows, feed_ref[:, pl.ds(2 * main + start, WIDE)])
        inner_ref[:, pl.ds(start, WIDE)] = (jax.nn.silu(gate) * upper).astype(jnp.bfloat16)
    ends = feed_ref[:, pl.ds(3 * main, WIDE)]
    both = dot(rows, ends)
    upper = pltpu.roll(both, WIDE - over, 1)
    inner = jax.nn.silu(both[:, :LANES]) * upper[:, :LANES]
    inner = jnp.where(lanes(inner) < over, inner, 0.0)
    low = pltpu.roll(jnp.concatenate([inner, jnp.zeros_like(inner)], axis=1), 2 * over, 1)
    low = jnp.where(lanes(low) < 2 * over, 0.0, low).astype(jnp.bfloat16)
    high = pltpu.roll(inner, LANES - over, 1)
    high = jnp.where(lanes(high) < LANES - tail, 0.0, high).astype(jnp.bfloat16)
    terms = dot_nt(inner_ref[...], feed_ref[:, pl.ds(0, main)]) + dot_nt(low, ends) + dot_nt(high, last_ref[...])
    mine_ref[...] = terms[:length]
    other_ref[...] = terms[length:].astype(jnp.bfloat16)


def feed_terms(units, tail, near, far, feed, attn):
    length, model = near.shape
    main = units // LANES * LANES
    width = 3 * units - tail
    end = attn.shape[1] // LANES - 1

    def whole(shape):
        return pl.BlockSpec(shape, lambda step: (0, 0), pipeline_mode=pl.Buffered(1))

    return pl.pallas_call(
        functools.partial(forward_kernel, units, tail),
        grid=(1,),
        out_shape=[
            jax.ShapeDtypeStruct((length, model), jnp.float32),
            jax.ShapeDtypeStruct((length, model), jnp.bfloat16),
        ],
        in_specs=[
            whole((length, model)),
            whole((length, model)),
            whole((model, width)),
            pl.BlockSpec((model, LANES), lambda step: (0, end)),
        ],
        out_specs=[whole((length, model))] * 2,
        scratch_shapes=[
            pltpu.VMEM((2 * length, model), jnp.bfloat16),
            pltpu.VMEM((2 * length, main), jnp.bfloat16),
        ],
        compiler_params=pltpu.CompilerParams(vmem_limit_bytes=48 * 2**20),
        cost_estimate=pl.CostEstimate(flops=2**20, bytes_accessed=2**16, transcendentals=0),
    )(near, far, feed, attn)


def feed_kernel(
    units, tail, near_ref, far_ref, near_grad_ref, far_grad_ref, feed_ref, last_ref, *refs
):
    extras, (block_ref, rest_ref, halves_ref, inner_ref, rows_ref, grads_ref) = refs[:-6], refs[-6:]
    main = units // LANES * LANES
    over = units - main
    base = 0
    for extra in extras:
        block_ref[:, pl.ds(base, extra.shape[1])] = extra[...]
        base += extra.shape[1]

    def give(column, value):
        block_ref[:, pl.ds(base + column, WIDE)] = value.astype(jnp.bfloat16)

    length = near_ref.shape[0]
    rows_ref[:length] = near_ref[...]
    rows_ref[length:] = far_ref[...]
    grads_ref[:length] = near_grad_ref[...]
    grads_ref[length:] = far_grad_ref[...]
    rows = rows_ref[...]
    branch = grads_ref[...]

    def parts(gate, upper, grad):
        sigma = jax.nn.sigmoid(gate)
        act = gate * sigma
        slope = sigma * (1.0 + gate * (1.0 - sigma))
        return (act * upper, grad * upper * slope, grad * act)

    for start in range(0, main, WIDE):
        places = tuple(start + i * main for i in range(3))
        first, second, third = (pl.ds(place, WIDE) for place in places)
        gate = dot(rows, feed_ref[:, second])
        upper = dot(rows, feed_ref[:, third])
        grad = dot(branch, feed_ref[:, first])
        inner, grad_gate, grad_upper = (part.astype(jnp.bfloat16) for part in parts(gate, upper, grad))
        inner_ref[:, first] = inner
        halves_ref[:, first] = grad_gate
        halves_ref[:, second] = grad_upper
        give(places[0], dot_tn(branch, inner))
        give(places[1], dot_tn(rows, grad_gate))
        give(places[2], dot_tn(rows, grad_upper))

    ends = feed_ref[:, pl.ds(3 * main, WIDE)]
    both = dot(rows, ends)
    upper = pltpu.roll(both, WIDE - over, 1)
    grad = pltpu.roll(dot(branch, ends), WIDE - 2 * over, 1)[:, :LANES]
    more = pltpu.roll(dot(branch, last_ref[...]), over, 1)
    grad = jnp.where(lanes(grad) < over - tail, grad, more)
    inner, grad_gate, grad_upper = (
        jnp.where(lanes(part) < over, part, 0.0)
        for part in parts(both[:, :LANES], upper[:, :LANES], grad)
    )
    inner = inner.astype(jnp.bfloat16)
    inner_ref[:, pl.ds(main, over)] = inner[:, :over]
    empty = jnp.zeros_like(grad_gate)
    wide = jnp.concatenate([grad_gate, empty], axis=1)
    wide = wide + pltpu.roll(jnp.concatenate([grad_upper, empty], axis=1), over, 1)
    wide = wide.astype(jnp.bfloat16)
    halves_ref[:, pl.ds(2 * main, WIDE)] = wide
    down = dot_tn(branch, inner)
    moved = pltpu.roll(jnp.concatenate([down, jnp.zeros_like(down)], axis=1), 2 * over, 1)
    wide = dot_tn(rows, wide)
    give(3 * main, jnp.where(lanes(wide) < 2 * over, wide, moved))
    moved = pltpu.roll(jnp.concatenate([down, jnp.zeros_like(down)], axis=1), WIDE - over, 1)
    rest_ref[...] = jnp.where(lanes(moved) < WIDE - tail, 0.0, moved).astype(jnp.bfloat16)


def feed_both(units, tail, near, far, near_grad, far_grad, feed, attn, *extras):
    count, model = 2 * near.shape[0], near.shape[1]
    main = units // LANES * LANES
    width = 3 * units - tail
    shapes = (
        (model, width + sum(extra.shape[1] for extra in extras)),
        (model, WIDE),
        (count, width - main),
        (count, units),
    )
    blocks = (near, far, near_grad, far_grad)

    def whole(shape):
        return pl.BlockSpec(shape, lambda step: (0, 0), pipeline_mode=pl.Buffered(1))

    end = attn.shape[1] // LANES - 1
    return pl.pallas_call(
        functools.partial(feed_kernel, units, tail),
        grid=(1,),
        out_shape=[jax.ShapeDtypeStruct(shape, jnp.bfloat16) for shape in shapes],
        in_specs=[whole(block.shape) for block in blocks]
        + [whole((model, width)), pl.BlockSpec((model, LANES), lambda step: (0, end))]
        + [whole(extra.shape) for extra in extras],
        out_specs=[whole(shape) for shape in shapes],
        scratch_shapes=[pltpu.VMEM((count, model), jnp.bfloat16)] * 2,
        compiler_params=pltpu.CompilerParams(vmem_limit_bytes=56 * 2**20),
        cost_estimate=pl.CostEstimate(
            flops=4 * count * model * width,
            bytes_accessed=20 * 2**20,
            transcendentals=count * units,
        ),
    )(*blocks, feed, attn, *extras)


def take(block, column, width):
    base = column // LANES * LANES
    shift = column - base
    stop = base + -(-(shift + width) // LANES) * LANES
    part = block[:, base:stop]
    if shift:
        part = pltpu.roll(part, stop - base - shift, 1)
    part = part[:, : -(-width // LANES) * LANES]
    return jnp.where(lanes(part) < width, part, 0.0)


def put(target, rows, column, width, part):
    base = column // LANES * LANES
    shift = column - base
    size = -(-(shift + width) // LANES) * LANES
    if size > part.shape[1]:
        empty = jnp.zeros((part.shape[0], size - part.shape[1]), part.dtype)
        part = jnp.concatenate([part, empty], axis=1)
    if shift:
        part = pltpu.roll(part, shift, 1)
    target[rows, pl.ds(base, size)] += part


def moved(block, distance):
    count = block.shape[0]
    if distance == 0:
        return block
    row = lax.broadcasted_iota(jnp.int32, block.shape, 0)
    rolled = pltpu.roll(block, distance % count, 0)
    inside = row >= distance if distance > 0 else row < count + distance
    return jnp.where(inside, rolled, 0.0)


def mixer_parts(both, taps, channels, first):
    length = both.shape[0]
    heads = channels // HD
    width = (both.shape[1] - 2 * channels) // (2 * heads)
    pre_values = take(both, 0, channels)
    values = sum(moved(pre_values, tap) * taps[tap : tap + 1] for tap in range(3))
    values = values.astype(jnp.bfloat16).astype(jnp.float32)
    gate = take(both, channels, channels)
    query = lax.broadcasted_iota(jnp.int32, (length, length), 0)
    key = lax.broadcasted_iota(jnp.int32, (length, length), 1)
    allowed = key <= query
    if not first:
        allowed = allowed & (query - key < WIN)
    parts = []
    for head in range(heads):
        queries = take(both, 2 * channels + head * width, width).astype(jnp.bfloat16)
        keys = take(both, 2 * channels + (heads + head) * width, width).astype(jnp.bfloat16)
        scores = dot_nt(queries, keys) / math.sqrt(width)
        if first:
            kernel = jnp.where(allowed, 1.0 + scores + 0.5 * scores * scores, 0.0)
            total = jnp.sum(kernel, axis=-1, keepdims=True)
            probs = kernel / total
            slope = jnp.where(allowed, (1.0 + scores) / total, 0.0)
        else:
            scores = jnp.where(allowed, scores, -1e30)
            kernel = jnp.exp(scores - jnp.max(scores, axis=-1, keepdims=True))
            probs = kernel / jnp.sum(kernel, axis=-1, keepdims=True)
            slope = probs
        own = take(values, head * HD, HD).astype(jnp.bfloat16)
        parts.append((queries, keys, probs, slope, own, dot(probs.astype(jnp.bfloat16), own)))
    return (pre_values, gate, parts)


def join(parts):
    empty = jnp.zeros_like(parts[0])
    total = 0.0
    for head, part in enumerate(parts):
        part = jnp.concatenate([part, empty], axis=1)
        total = total + (pltpu.roll(part, head * HD, 1) if head else part)
    return total


def mixer_kernel(
    channels, first, near_ref, far_ref, attn_ref, taps_ref, mine_ref, other_ref, both_ref, gated_ref
):
    length = near_ref.shape[0]
    stop = both_ref.shape[1]
    for index, rows in enumerate((near_ref, far_ref)):
        both = dot(rows[...], attn_ref[:, pl.ds(0, stop)])
        both_ref[pl.ds(index * length, length), :] = both
        _, gate, parts = mixer_parts(both, taps_ref[...], channels, first)
        gated = (join([part[-1] for part in parts]) * gate * jax.nn.sigmoid(gate)).astype(jnp.bfloat16)
        gated_ref[pl.ds(index * length, length), :] = gated
        terms = dot_nt(gated, attn_ref[:, pl.ds(stop, WIDE)])
        if index == 0:
            mine_ref[...] = terms
        else:
            other_ref[...] = terms.astype(jnp.bfloat16)


def mixer_back_kernel(
    channels, first, near_ref, far_ref, near_grad_ref, far_grad_ref, attn_ref, taps_ref, both_ref,
    gated_ref, rest_ref, block_ref, mine_ref, other_ref, taps_grad_ref, rows_ref, grads_ref, sums_ref, low_ref,
):
    length = near_ref.shape[0]
    stop = both_ref.shape[1]
    heads = channels // HD
    width = (stop - 2 * channels) // (2 * heads)
    taps = taps_ref[...]
    sums_ref[...] = jnp.zeros_like(sums_ref)
    taps_grad = [0.0] * 3
    rows_ref[:length] = near_ref[...]
    rows_ref[length:] = far_ref[...]
    grads_ref[:length] = near_grad_ref[...]
    grads_ref[length:] = far_grad_ref[...]
    for index in range(2):
        rows = pl.ds(index * length, length)
        pre_values, gate, parts = mixer_parts(both_ref[rows, :], taps, channels, first)
        mixed = join([part[-1] for part in parts])
        grad = dot(grads_ref[rows, :], attn_ref[:, pl.ds(stop, WIDE)])
        grad = jnp.where(lanes(grad) < channels, grad, 0.0)
        sigma = jax.nn.sigmoid(gate)
        grad_mixed = (grad * (gate * sigma)).astype(jnp.bfloat16).astype(jnp.float32)
        grad_gate = (grad * mixed * silu_slope(gate)).astype(jnp.bfloat16).astype(jnp.float32)
        put(sums_ref, rows, channels, channels, grad_gate)
        grad_values = []
        for head, (queries, keys, probs, slope, own, _) in enumerate(parts):
            part = take(grad_mixed, head * HD, HD).astype(jnp.bfloat16)
            grad_values.append(dot_tn(probs.astype(jnp.bfloat16), part))
            grad_probs = dot_nt(part, own)
            centred = grad_probs - jnp.sum(probs * grad_probs, axis=-1, keepdims=True)
            score_grad = (centred * slope).astype(jnp.bfloat16)
            for place, value in (
                (head, dot(score_grad, keys)),
                (heads + head, dot_tn(score_grad, queries)),
            ):
                value = (value / math.sqrt(width)).astype(jnp.bfloat16).astype(jnp.float32)
                put(sums_ref, rows, 2 * channels + place * width, width, value)
        grad_values = join(grad_values)
        grad_pre = sum(moved(grad_values, -tap) * taps[tap : tap + 1] for tap in range(3))
        put(sums_ref, rows, 0, channels, grad_pre.astype(jnp.bfloat16).astype(jnp.float32))
        for tap in range(3):
            taps_grad[tap] = taps_grad[tap] + jnp.sum(
                grad_values * moved(pre_values, tap), axis=0, keepdims=True
            )
    for tap in range(3):
        taps_grad_ref[pl.ds(tap, 1), :] = taps_grad[tap]
    low_ref[...] = sums_ref[...].astype(jnp.bfloat16)
    for column in range(0, stop, LANES):
        size = min(WIDE, stop - column)
        if column % WIDE:
            continue
        place = pl.ds(column, size)
        block_ref[:, place] = dot_tn(rows_ref[...], low_ref[:, place]).astype(jnp.bfloat16)
    last = dot_tn(grads_ref[...], gated_ref[...]).astype(jnp.bfloat16)
    block_ref[:, pl.ds(stop, WIDE)] = last + rest_ref[...]
    for index in range(2):
        terms = dot_nt(low_ref[pl.ds(index * length, length), :], attn_ref[:, pl.ds(0, stop)])
        if index == 0:
            mine_ref[...] = terms
        else:
            other_ref[...] = terms.astype(jnp.bfloat16)


def whole_call(kernel, inputs, shapes, scratch, flops):
    def whole(shape):
        return pl.BlockSpec(shape, lambda step: (0,) * len(shape), pipeline_mode=pl.Buffered(1))

    return pl.pallas_call(
        kernel,
        grid=(1,),
        out_shape=[jax.ShapeDtypeStruct(shape, kind) for shape, kind in shapes],
        in_specs=[whole(block.shape) for block in inputs],
        out_specs=[whole(shape) for shape, _ in shapes],
        scratch_shapes=[pltpu.VMEM(shape, kind) for shape, kind in scratch],
        compiler_params=pltpu.CompilerParams(vmem_limit_bytes=56 * 2**20),
        cost_estimate=pl.CostEstimate(flops=flops, bytes_accessed=2**16, transcendentals=0),
    )(*inputs)


def mixer_forward(channels, first, near, far, attn, taps):
    length, model = near.shape
    stop = attn.shape[1] - WIDE
    shapes = (
        ((length, model), jnp.float32),
        ((length, model), jnp.bfloat16),
        ((2 * length, stop), jnp.float32),
        ((2 * length, WIDE), jnp.bfloat16),
    )
    kernel = functools.partial(mixer_kernel, channels, first)
    return whole_call(kernel, (near, far, attn, taps), shapes, (), 2**20)


def mixer_backward(channels, first, near, far, near_grad, far_grad, attn, taps, both, gated, rest):
    length, model = near.shape
    stop = both.shape[1]
    shapes = (
        ((model, stop + WIDE), jnp.bfloat16),
        ((length, model), jnp.float32),
        ((length, model), jnp.bfloat16),
        (taps.shape, jnp.float32),
    )
    scratch = (
        ((2 * length, model), jnp.bfloat16),
        ((2 * length, model), jnp.bfloat16),
        ((2 * length, stop), jnp.float32),
        ((2 * length, stop), jnp.bfloat16),
    )
    inputs = (near, far, near_grad, far_grad, attn, taps, both, gated, rest)
    return whole_call(functools.partial(mixer_back_kernel, channels, first), inputs, shapes, scratch, 2**20)


def end_kernel(
    channels, units, tail, core_ref, mine_ref, other_ref, low_ref, high_ref, kept_ref,
    vgate_ref, out_ref, pair_ref, down_ref,
):
    step = pl.program_id(0)
    lower = core_ref[0] == 0
    mine, other = (ref[...].astype(jnp.float32) for ref in (mine_ref, other_ref))
    low = jnp.where(lower, mine, low_ref[...].astype(jnp.float32))
    high = jnp.where(lower, other, high_ref[...].astype(jnp.float32))
    size = mine.shape[1]
    wide = pair_ref.shape[1] // 2

    @pl.when(step == 0)
    def _():
        for place in range(2):
            parts = [take(block, place * channels, channels) for block in (low, high)]
            empty = jnp.zeros_like(parts[0])
            first = jnp.concatenate([parts[0], empty], axis=1)
            second = pltpu.roll(jnp.concatenate([parts[1], empty], axis=1), channels, 1)
            vgate_ref[:, place, :] = (first + second)[:, : 2 * channels]
        for place, block in enumerate((low, high)):
            turned = jnp.swapaxes(block[:, size - WIDE :], 0, 1)
            out_ref[pl.ds(place * channels, channels), :] = turned[:channels]
        for place, block in enumerate((jnp.where(lower, mine, other), jnp.where(lower, other, mine))):
            turned = jnp.swapaxes(block[:, size - WIDE - LANES : size - WIDE], 0, 1)
            for half in range(2):
                start = LANES - (2 - half) * wide
                pair_ref[half, pl.ds(place * wide, wide), :] = turned[start : start + wide]

    for place, block in enumerate((low, high)):

        @pl.when(step == place)
        def _(place=place, block=block):
            stop = units * (place + 1) % LANES or LANES
            last = block[:, size - LANES :]
            if stop < LANES:
                last = pltpu.roll(last, stop, 1)
            column = lanes(last)
            inside = (column >= stop - tail) & (column < stop)
            down_ref[...] = jnp.where(inside, last, kept_ref[...])


def end_call(channels, tail, width, core, mine, other, low, high, down):
    count, size = mine.shape
    units = down.shape[1] // 2
    first, second = (units - 1) // LANES, (2 * units - 1) // LANES

    def whole(shape):
        return pl.BlockSpec(shape, lambda step: (0,) * len(shape))

    tile = pl.BlockSpec((count, LANES), lambda step: (0, first + step * (second - first)))
    shapes = ((count, 2, 2 * channels), (2 * channels, count), (2, width, count))
    return pl.pallas_call(
        functools.partial(end_kernel, channels, units, tail),
        grid=(2,),
        out_shape=[jax.ShapeDtypeStruct(shape, jnp.float32) for shape in (*shapes, down.shape)],
        in_specs=[pl.BlockSpec(memory_space=pltpu.SMEM)]
        + [whole((count, size))] * 4
        + [tile],
        out_specs=[whole(shape) for shape in shapes] + [tile],
        input_output_aliases={5: 3},
        compiler_params=pltpu.CompilerParams(vmem_limit_bytes=48 * 2**20),
        cost_estimate=pl.CostEstimate(flops=2**20, bytes_accessed=2**27, transcendentals=0),
    )(core.reshape(1), mine, other, low, high, down)


def by_rows(block):
    return with_layout_constraint(block, Layout(major_to_minor=tuple(range(block.ndim))))


class Queue:
    def __init__(self):
        self.done = []

    def scatter(self, *grads):
        block = by_rows(jnp.concatenate(grads, axis=1) if len(grads) > 1 else grads[0])
        if self.done:
            block, self.done[-1] = lax.optimization_barrier((block, self.done[-1]))
        self.done.append(by_rows(lax.psum_scatter(block, "dp", scatter_dimension=0, tiled=True)))


def body(
    boundary, lengths, norm_gains, conv_taps, lin_qk, win_qk, value_gate, out_weight, gate_up, down_weight
):
    core = lax.axis_index("section")
    index = lax.axis_index("tensor")
    lower = core == 0
    rows_dev, model = boundary.shape[2:]
    channels = value_gate.shape[-1] // 2
    units = gate_up.shape[-1] // 2
    main = units // LANES * LANES
    tail = -(3 * channels + lin_qk.shape[-1]) % LANES

    def half(block, axis, which):
        size = block.shape[axis] // 2
        return lax.dynamic_slice_in_dim(block, which * size, size, axis)

    def both_layers(build):
        mine = build(core)
        other = swap(build(1 - core))
        return (jnp.where(lower, mine, other), jnp.where(lower, other, mine))

    def attn_piece(which):
        values = half(value_gate[0], 2, which)
        last = half(down_weight[0], 0, which)[units - tail :]
        return jnp.concatenate(
            [values[:, 0], values[:, 1], half(out_weight[0], 0, which).T, last.T], axis=1
        )

    def feed_piece(which):
        pair = half(gate_up[0], 2, which)
        down = half(down_weight[0], 0, which).T
        return jnp.concatenate(
            [down[:, :main], pair[:, 0, :main], pair[:, 1, :main], pair[:, 0, main:], pair[:, 1, main:], down[:, main : units - tail]],
            axis=1,
        )

    def fetch(piece):
        return lax.all_gather(piece, "dp", axis=0, tiled=True)

    def with_pair(attn, pair):
        pair = half(pair, 2, core)
        both = 2 * channels
        return jnp.concatenate([attn[:, :both], pair[:, 0], pair[:, 1], attn[:, both:]], axis=1)

    attn_parts = both_layers(attn_piece)
    feed_parts = both_layers(feed_piece)
    attn_zero = fetch(with_pair(attn_parts[0], lin_qk))
    packed = fetch(jnp.concatenate([feed_parts[0], with_pair(attn_parts[1], win_qk)], axis=1))
    split = feed_parts[0].shape[1]
    attn_one = packed[:, split:]
    feed_one = fetch(feed_parts[1])
    down_one = jnp.concatenate(
        [feed_one[:, :main], feed_one[:, main + 2 * units :], attn_one[:, attn_one.shape[1] - tail :]], axis=1
    )

    small = jnp.concatenate([norm_gains[0], conv_taps[0]], axis=0)
    small_other = swap(small)
    small_zero = jnp.where(lower, small, small_other)
    small_one = jnp.where(lower, small_other, small)
    offset = (2 * index + core) * channels

    def own_taps(block):
        own = lax.dynamic_slice_in_dim(block[2:], offset, channels, 1)
        return jnp.pad(own, ((0, -own.shape[0] % SUBLANES), (0, WIDE - channels)))

    held = boundary[0]
    keep = lax.dynamic_index_in_dim(held, core, 0, keepdims=False)
    other = swap(lax.dynamic_index_in_dim(held, 1 - core, 0, keepdims=False))
    entering = jnp.where(lower, keep, other).astype(jnp.float32)
    cotangent = jnp.where(lower, other, keep).astype(jnp.float32)
    length = lax.dynamic_index_in_dim(lengths, core, 0, keepdims=False)
    place = index * rows_dev + jnp.arange(rows_dev)
    mask = (place < length).astype(jnp.float32)[:, None]

    queue = Queue()
    gains_zero, gains_one = small_zero[:2], small_one[:2]
    taps_zero, taps_one = own_taps(small_zero), own_taps(small_one)

    def mix(rows, gain, attn, taps, first):
        scale, normed = rms_rows(rows, gain)
        near, far = spread_pair(normed)
        mine, other, both, gated = mixer_forward(channels, first, near, far, attn, taps)
        return (rows + collect_pair(mine, other), (rows, scale, near, far, both, gated))

    def mix_back(kept, grad_out, gain, attn, taps, rest, first):
        rows, scale, near, far, both, gated = kept
        block, mine, other, grad_taps = mixer_backward(
            channels, first, near, far, *spread_pair(grad_out), attn, taps, both, gated, rest
        )
        back, grad_gain = rms_back(rows, scale, gain, collect_pair(mine, other))
        return (block, grad_out + back, grad_gain, grad_taps[: conv_taps.shape[1], :channels])

    hidden, kept_zero = mix(entering, gains_zero[0], attn_zero, taps_zero, True)
    scale, normed = rms_rows(hidden, gains_zero[1])
    near, far = spread_pair(normed)
    kept_feed = (hidden, scale, near, far)
    middle = hidden + collect_pair(*feed_terms(units, tail, near, far, packed, attn_zero))
    middle = middle.astype(jnp.bfloat16).astype(jnp.float32)

    hidden, kept_one = mix(middle, gains_one[0], attn_one, taps_one, False)
    scale, normed = rms_rows(hidden, gains_one[1])
    grad_out = cotangent * mask
    block, rest, grad_halves, inner = feed_both(
        units, tail, *spread_pair(normed), *spread_pair(grad_out), feed_one, packed
    )
    queue.scatter(block)
    final = hidden + collect(dot_nt(inner, down_one))
    back, gain_two = rms_back(hidden, scale, gains_one[1], collect(dot_nt(grad_halves, feed_one[:, main:])))
    attn_grads, grad_middle, gain_one, taps_one = mix_back(
        kept_one, grad_out + back, gains_one[0], attn_one, taps_one, rest, False
    )
    gains_one = jnp.stack([gain_one, gain_two])

    grad_middle = grad_middle.astype(jnp.bfloat16).astype(jnp.float32)
    hidden, scale, near, far = kept_feed
    block, rest, grad_halves, _ = feed_both(
        units, tail, near, far, *spread_pair(grad_middle), packed, attn_zero, attn_grads
    )
    queue.scatter(block)
    terms = dot_nt(grad_halves, packed[:, main:split])
    back, gain_two = rms_back(hidden, scale, gains_zero[1], collect(terms))
    attn_grads, grad_start, gain_one, taps_zero = mix_back(
        kept_zero, grad_middle + back, gains_zero[0], attn_zero, taps_zero, rest, True
    )
    queue.scatter(attn_grads)
    gains_zero = jnp.stack([gain_one, gain_two])

    edge = attn_one.shape[1]
    grads_one = (queue.done[0], queue.done[1][:, :edge])
    grads_zero = (queue.done[1][:, edge:], queue.done[2])

    def own_small(gains, taps):
        spot = jnp.zeros((taps.shape[0], model), jnp.float32)
        return jnp.concatenate([gains, lax.dynamic_update_slice_in_dim(spot, taps, offset, 1)], axis=0)

    sums = sum_all(jnp.stack([own_small(gains_zero, taps_zero), own_small(gains_one, taps_one)]))
    sums = lax.dynamic_index_in_dim(sums, core, 0, keepdims=True)

    final = final * mask
    ends_keep = jnp.where(lower, grad_start, final)
    ends_other = swap(jnp.where(lower, final, grad_start))
    ends = jnp.where(lower, jnp.stack([ends_keep, ends_other]), jnp.stack([ends_other, ends_keep]))

    def home(zero, one):
        mine = jnp.where(lower, zero, one)
        other = swap(jnp.where(lower, one, zero))
        return (jnp.where(lower, mine, other), jnp.where(lower, other, mine))

    def halves(low, high, axis):
        return jnp.concatenate([low, high], axis=axis).astype(jnp.float32)

    def pair_home(block):
        size = block.shape[1] // 2
        other = swap(block)
        low = jnp.where(lower, block, other)
        high = jnp.where(lower, other, block)
        return jnp.stack(
            [halves(low[:, :size], high[:, :size], 1), halves(low[:, size:], high[:, size:], 1)], axis=1
        )

    last = grads_zero[1]
    early = grads_one[1]
    both = 2 * channels
    gap = last.shape[1] - both - WIDE
    own = jnp.concatenate(
        [early[:, :both], jnp.zeros((early.shape[0], gap), early.dtype), early[:, early.shape[1] - WIDE :]],
        axis=1,
    )
    away = swap(own)

    def unpack(block):
        wide = block[:, main:]
        (gate, upper), (gate_rest, upper_rest) = gates(wide, units)
        empty = jnp.zeros((block.shape[0], tail), block.dtype)
        down = jnp.concatenate([block[:, :main], wide[:, 2 * units :], empty], axis=1)
        return (
            jnp.concatenate([gate, gate_rest], axis=1),
            jnp.concatenate([upper, upper_rest], axis=1),
            down,
        )

    low, high = home(grads_zero[0], grads_one[0])
    low, high = unpack(low), unpack(high)
    gate_up_grad = jnp.stack([halves(low[0], high[0], 1), halves(low[1], high[1], 1)], axis=1)
    down_grad = by_rows(halves(low[2], high[2], 1))
    win_grad = by_rows(pair_home(early[:, both : early.shape[1] - WIDE]))
    gate_up_grad = by_rows(gate_up_grad)
    low, high = jnp.where(lower, own, away), jnp.where(lower, away, own)
    last, low, high, gate_up_grad, down_grad, win_grad, ends, sums = lax.optimization_barrier(
        (last, low, high, gate_up_grad, down_grad, win_grad, ends, sums)
    )
    vgate_grad, out_grad, pair_grad, down_grad = end_call(
        channels, tail, gap, core, last, swap(last), low, high, down_grad
    )
    return (
        ends[None],
        sums[:, :2],
        sums[:, 2:],
        jnp.transpose(pair_grad, (2, 0, 1)),
        win_grad,
        vgate_grad[None],
        out_grad[None],
        gate_up_grad[None],
        down_grad.T[None],
    )


def solution(mesh):
    in_specs = (
        P("section", "dp", "tensor", None),
        P("dp"),
        P("section", None, None),
        P("section", None, None),
        P("dp", None, "tensor"),
        P("dp", None, "tensor"),
        P("section", "dp", None, "tensor"),
        P("section", "tensor", "dp"),
        P("section", "dp", None, "tensor"),
        P("section", "tensor", "dp"),
    )
    out_specs = (
        P("section", "dp", "tensor", None),
        P("section", None, None),
        P("section", None, None),
        P("dp", None, "tensor"),
        P("dp", None, "tensor"),
        P("section", "dp", None, "tensor"),
        P("section", "tensor", "dp"),
        P("section", "dp", None, "tensor"),
        P("section", "tensor", "dp"),
    )
    return jax.shard_map(body, mesh=mesh, in_specs=in_specs, out_specs=out_specs, check_vma=False)
```

```python
import functools
import math

import jax
import jax.numpy as jnp
from jax import lax
from jax.experimental import pallas as pl
from jax.experimental.layout import Layout, with_layout_constraint
from jax.experimental.pallas import tpu as pltpu
from jax.sharding import PartitionSpec as P

WIN = 64
HD = 112
LANES = 128
WIDE = 256
SUBLANES = 8

EPS = 1e-06


def silu_slope(value):
    sigma = jax.nn.sigmoid(value)
    return sigma * (1.0 + value * (1.0 - sigma))


def rms_rows(rows, gain):
    scale = lax.rsqrt(jnp.mean(rows * rows, axis=-1, keepdims=True) + EPS)
    return (scale, rows * scale * gain)


def rms_back(rows, scale, gain, grad):
    normal = rows * scale
    weighted = grad * gain
    inner = jnp.mean(weighted * normal, axis=-1, keepdims=True)
    return (scale * (weighted - normal * inner), jnp.sum(grad * normal, axis=0))


def swap(block):
    return lax.ppermute(block, "section", [(0, 1), (1, 0)])


def spread_pair(rows):
    mine = lax.all_gather(rows.astype(jnp.bfloat16), "tensor", axis=0, tiled=True)
    return (mine, swap(mine))


def spread(rows):
    return jnp.concatenate(spread_pair(rows), axis=0)


def collect(terms):
    length = terms.shape[0] // 2
    return collect_pair(terms[:length], terms[length:].astype(jnp.bfloat16))


def collect_pair(mine, other):
    size = lax.axis_size("tensor")
    count = mine.shape[0] // size
    index = lax.axis_index("tensor")
    part = mine + swap(other).astype(jnp.float32)
    low = part.astype(jnp.bfloat16)
    total = lax.dynamic_slice_in_dim(part, index * count, count, 0)
    for offset in range(1, size):
        block = lax.dynamic_slice_in_dim(low, (index ^ offset) * count, count, 0)
        pairs = [(i, i ^ offset) for i in range(size)]
        total = total + lax.ppermute(block, "tensor", pairs).astype(jnp.float32)
    return total


def ring_gather(piece):
    size = lax.axis_size("dp")
    index = lax.axis_index("dp")
    count = piece.shape[0]
    full = jnp.zeros((size * count, piece.shape[1]), piece.dtype)
    for step in range(size):
        if step:
            piece = lax.ppermute(piece, "dp", [(i, (i + 1) % size) for i in range(size)])
        full = lax.dynamic_update_slice_in_dim(full, piece, (index - step) % size * count, 0)
    return full


def sum_all(block):
    for axis in ("section", "tensor", "dp"):
        size = lax.axis_size(axis)
        step = 1
        while step < size:
            pairs = [(i, i ^ step) for i in range(size)]
            block = block + lax.ppermute(block, axis, pairs)
            step *= 2
    return block


def dot(one, two):
    return jnp.dot(one, two, preferred_element_type=jnp.float32)


def dot_nt(one, two):
    return lax.dot_general(one, two, (((1,), (1,)), ((), ())), preferred_element_type=jnp.float32)


def dot_tn(one, two):
    return lax.dot_general(one, two, (((0,), (0,)), ((), ())), preferred_element_type=jnp.float32)


def gates(halves, units):
    main = units // LANES * LANES
    stop = main + units
    return (
        (halves[:, :main], halves[:, main : 2 * main]),
        (halves[:, 2 * main : stop], halves[:, stop : 2 * units]),
    )


def lanes(block):
    return lax.broadcasted_iota(jnp.int32, block.shape, 1)


def forward_kernel(units, tail, near_ref, far_ref, feed_ref, last_ref, mine_ref, other_ref, rows_ref, inner_ref):
    main = units // LANES * LANES
    over = units - main
    length = near_ref.shape[0]
    rows_ref[:length] = near_ref[...]
    rows_ref[length:] = far_ref[...]
    rows = rows_ref[...]
    for start in range(0, main, WIDE):
        gate = dot(rows, feed_ref[:, pl.ds(main + start, WIDE)])
        upper = dot(rows, feed_ref[:, pl.ds(2 * main + start, WIDE)])
        inner_ref[:, pl.ds(start, WIDE)] = (jax.nn.silu(gate) * upper).astype(jnp.bfloat16)
    ends = feed_ref[:, pl.ds(3 * main, WIDE)]
    both = dot(rows, ends)
    upper = pltpu.roll(both, WIDE - over, 1)
    inner = jax.nn.silu(both[:, :LANES]) * upper[:, :LANES]
    inner = jnp.where(lanes(inner) < over, inner, 0.0)
    low = pltpu.roll(jnp.concatenate([inner, jnp.zeros_like(inner)], axis=1), 2 * over, 1)
    low = jnp.where(lanes(low) < 2 * over, 0.0, low).astype(jnp.bfloat16)
    high = pltpu.roll(inner, LANES - over, 1)
    high = jnp.where(lanes(high) < LANES - tail, 0.0, high).astype(jnp.bfloat16)
    terms = dot_nt(inner_ref[...], feed_ref[:, pl.ds(0, main)]) + dot_nt(low, ends) + dot_nt(high, last_ref[...])
    mine_ref[...] = terms[:length]
    other_ref[...] = terms[length:].astype(jnp.bfloat16)


def feed_terms(units, tail, near, far, feed, attn):
    length, model = near.shape
    main = units // LANES * LANES
    width = 3 * units - tail
    end = attn.shape[1] // LANES - 1

    def whole(shape):
        return pl.BlockSpec(shape, lambda step: (0, 0), pipeline_mode=pl.Buffered(1))

    return pl.pallas_call(
        functools.partial(forward_kernel, units, tail),
        grid=(1,),
        out_shape=[
            jax.ShapeDtypeStruct((length, model), jnp.float32),
            jax.ShapeDtypeStruct((length, model), jnp.bfloat16),
        ],
        in_specs=[
            whole((length, model)),
            whole((length, model)),
            whole((model, width)),
            pl.BlockSpec((model, LANES), lambda step: (0, end)),
        ],
        out_specs=[whole((length, model))] * 2,
        scratch_shapes=[
            pltpu.VMEM((2 * length, model), jnp.bfloat16),
            pltpu.VMEM((2 * length, main), jnp.bfloat16),
        ],
        compiler_params=pltpu.CompilerParams(vmem_limit_bytes=48 * 2**20),
        cost_estimate=pl.CostEstimate(flops=2**20, bytes_accessed=2**16, transcendentals=0),
    )(near, far, feed, attn)


def feed_kernel(
    units, tail, near_ref, far_ref, near_grad_ref, far_grad_ref, feed_ref, last_ref, *refs
):
    extras, (block_ref, rest_ref, halves_ref, inner_ref, rows_ref, grads_ref) = refs[:-6], refs[-6:]
    main = units // LANES * LANES
    over = units - main
    base = 0
    for extra in extras:
        block_ref[:, pl.ds(base, extra.shape[1])] = extra[...]
        base += extra.shape[1]

    def give(column, value):
        block_ref[:, pl.ds(base + column, WIDE)] = value.astype(jnp.bfloat16)

    length = near_ref.shape[0]
    rows_ref[:length] = near_ref[...]
    rows_ref[length:] = far_ref[...]
    grads_ref[:length] = near_grad_ref[...]
    grads_ref[length:] = far_grad_ref[...]
    rows = rows_ref[...]
    branch = grads_ref[...]

    def parts(gate, upper, grad):
        sigma = jax.nn.sigmoid(gate)
        act = gate * sigma
        slope = sigma * (1.0 + gate * (1.0 - sigma))
        return (act * upper, grad * upper * slope, grad * act)

    for start in range(0, main, WIDE):
        places = tuple(start + i * main for i in range(3))
        first, second, third = (pl.ds(place, WIDE) for place in places)
        gate = dot(rows, feed_ref[:, second])
        upper = dot(rows, feed_ref[:, third])
        grad = dot(branch, feed_ref[:, first])
        inner, grad_gate, grad_upper = (part.astype(jnp.bfloat16) for part in parts(gate, upper, grad))
        inner_ref[:, first] = inner
        halves_ref[:, first] = grad_gate
        halves_ref[:, second] = grad_upper
        give(places[0], dot_tn(branch, inner))
        give(places[1], dot_tn(rows, grad_gate))
        give(places[2], dot_tn(rows, grad_upper))

    ends = feed_ref[:, pl.ds(3 * main, WIDE)]
    both = dot(rows, ends)
    upper = pltpu.roll(both, WIDE - over, 1)
    grad = pltpu.roll(dot(branch, ends), WIDE - 2 * over, 1)[:, :LANES]
    more = pltpu.roll(dot(branch, last_ref[...]), over, 1)
    grad = jnp.where(lanes(grad) < over - tail, grad, more)
    inner, grad_gate, grad_upper = (
        jnp.where(lanes(part) < over, part, 0.0)
        for part in parts(both[:, :LANES], upper[:, :LANES], grad)
    )
    inner = inner.astype(jnp.bfloat16)
    inner_ref[:, pl.ds(main, over)] = inner[:, :over]
    empty = jnp.zeros_like(grad_gate)
    wide = jnp.concatenate([grad_gate, empty], axis=1)
    wide = wide + pltpu.roll(jnp.concatenate([grad_upper, empty], axis=1), over, 1)
    wide = wide.astype(jnp.bfloat16)
    halves_ref[:, pl.ds(2 * main, WIDE)] = wide
    down = dot_tn(branch, inner)
    moved = pltpu.roll(jnp.concatenate([down, jnp.zeros_like(down)], axis=1), 2 * over, 1)
    wide = dot_tn(rows, wide)
    give(3 * main, jnp.where(lanes(wide) < 2 * over, wide, moved))
    moved = pltpu.roll(jnp.concatenate([down, jnp.zeros_like(down)], axis=1), WIDE - over, 1)
    rest_ref[...] = jnp.where(lanes(moved) < WIDE - tail, 0.0, moved).astype(jnp.bfloat16)


def feed_both(units, tail, near, far, near_grad, far_grad, feed, attn, *extras):
    count, model = 2 * near.shape[0], near.shape[1]
    main = units // LANES * LANES
    width = 3 * units - tail
    shapes = (
        (model, width + sum(extra.shape[1] for extra in extras)),
        (model, WIDE),
        (count, width - main),
        (count, units),
    )
    blocks = (near, far, near_grad, far_grad)

    def whole(shape):
        return pl.BlockSpec(shape, lambda step: (0, 0), pipeline_mode=pl.Buffered(1))

    end = attn.shape[1] // LANES - 1
    return pl.pallas_call(
        functools.partial(feed_kernel, units, tail),
        grid=(1,),
        out_shape=[jax.ShapeDtypeStruct(shape, jnp.bfloat16) for shape in shapes],
        in_specs=[whole(block.shape) for block in blocks]
        + [whole((model, width)), pl.BlockSpec((model, LANES), lambda step: (0, end))]
        + [whole(extra.shape) for extra in extras],
        out_specs=[whole(shape) for shape in shapes],
        scratch_shapes=[pltpu.VMEM((count, model), jnp.bfloat16)] * 2,
        compiler_params=pltpu.CompilerParams(vmem_limit_bytes=56 * 2**20),
        cost_estimate=pl.CostEstimate(
            flops=4 * count * model * width,
            bytes_accessed=20 * 2**20,
            transcendentals=count * units,
        ),
    )(*blocks, feed, attn, *extras)


def take(block, column, width):
    base = column // LANES * LANES
    shift = column - base
    stop = base + -(-(shift + width) // LANES) * LANES
    part = block[:, base:stop]
    if shift:
        part = pltpu.roll(part, stop - base - shift, 1)
    part = part[:, : -(-width // LANES) * LANES]
    return jnp.where(lanes(part) < width, part, 0.0)


def put(target, rows, column, width, part):
    base = column // LANES * LANES
    shift = column - base
    size = -(-(shift + width) // LANES) * LANES
    if size > part.shape[1]:
        empty = jnp.zeros((part.shape[0], size - part.shape[1]), part.dtype)
        part = jnp.concatenate([part, empty], axis=1)
    if shift:
        part = pltpu.roll(part, shift, 1)
    target[rows, pl.ds(base, size)] += part


def moved(block, distance):
    count = block.shape[0]
    if distance == 0:
        return block
    row = lax.broadcasted_iota(jnp.int32, block.shape, 0)
    rolled = pltpu.roll(block, distance % count, 0)
    inside = row >= distance if distance > 0 else row < count + distance
    return jnp.where(inside, rolled, 0.0)


def mixer_parts(both, taps, channels, first):
    length = both.shape[0]
    heads = channels // HD
    width = (both.shape[1] - 2 * channels) // (2 * heads)
    pre_values = take(both, 0, channels)
    values = sum(moved(pre_values, tap) * taps[tap : tap + 1] for tap in range(3))
    values = values.astype(jnp.bfloat16).astype(jnp.float32)
    gate = take(both, channels, channels)
    query = lax.broadcasted_iota(jnp.int32, (length, length), 0)
    key = lax.broadcasted_iota(jnp.int32, (length, length), 1)
    allowed = key <= query
    if not first:
        allowed = allowed & (query - key < WIN)
    parts = []
    for head in range(heads):
        queries = take(both, 2 * channels + head * width, width).astype(jnp.bfloat16)
        keys = take(both, 2 * channels + (heads + head) * width, width).astype(jnp.bfloat16)
        scores = dot_nt(queries, keys) / math.sqrt(width)
        if first:
            kernel = jnp.where(allowed, 1.0 + scores + 0.5 * scores * scores, 0.0)
            total = jnp.sum(kernel, axis=-1, keepdims=True)
            probs = kernel / total
            slope = jnp.where(allowed, (1.0 + scores) / total, 0.0)
        else:
            scores = jnp.where(allowed, scores, -1e30)
            kernel = jnp.exp(scores - jnp.max(scores, axis=-1, keepdims=True))
            probs = kernel / jnp.sum(kernel, axis=-1, keepdims=True)
            slope = probs
        own = take(values, head * HD, HD).astype(jnp.bfloat16)
        parts.append((queries, keys, probs, slope, own, dot(probs.astype(jnp.bfloat16), own)))
    return (pre_values, gate, parts)


def join(parts):
    empty = jnp.zeros_like(parts[0])
    total = 0.0
    for head, part in enumerate(parts):
        part = jnp.concatenate([part, empty], axis=1)
        total = total + (pltpu.roll(part, head * HD, 1) if head else part)
    return total


def mixer_kernel(
    channels, first, near_ref, far_ref, attn_ref, taps_ref, mine_ref, other_ref, both_ref, gated_ref
):
    length = near_ref.shape[0]
    stop = both_ref.shape[1]
    for index, rows in enumerate((near_ref, far_ref)):
        both = dot(rows[...], attn_ref[:, pl.ds(0, stop)])
        both_ref[pl.ds(index * length, length), :] = both
        _, gate, parts = mixer_parts(both, taps_ref[...], channels, first)
        gated = (join([part[-1] for part in parts]) * gate * jax.nn.sigmoid(gate)).astype(jnp.bfloat16)
        gated_ref[pl.ds(index * length, length), :] = gated
        terms = dot_nt(gated, attn_ref[:, pl.ds(stop, WIDE)])
        if index == 0:
            mine_ref[...] = terms
        else:
            other_ref[...] = terms.astype(jnp.bfloat16)


def mixer_back_kernel(
    channels, first, near_ref, far_ref, near_grad_ref, far_grad_ref, attn_ref, taps_ref, both_ref,
    gated_ref, rest_ref, block_ref, mine_ref, other_ref, taps_grad_ref, rows_ref, grads_ref, sums_ref, low_ref,
):
    length = near_ref.shape[0]
    stop = both_ref.shape[1]
    heads = channels // HD
    width = (stop - 2 * channels) // (2 * heads)
    taps = taps_ref[...]
    sums_ref[...] = jnp.zeros_like(sums_ref)
    taps_grad = [0.0] * 3
    rows_ref[:length] = near_ref[...]
    rows_ref[length:] = far_ref[...]
    grads_ref[:length] = near_grad_ref[...]
    grads_ref[length:] = far_grad_ref[...]
    for index in range(2):
        rows = pl.ds(index * length, length)
        pre_values, gate, parts = mixer_parts(both_ref[rows, :], taps, channels, first)
        mixed = join([part[-1] for part in parts])
        grad = dot(grads_ref[rows, :], attn_ref[:, pl.ds(stop, WIDE)])
        grad = jnp.where(lanes(grad) < channels, grad, 0.0)
        sigma = jax.nn.sigmoid(gate)
        grad_mixed = (grad * (gate * sigma)).astype(jnp.bfloat16).astype(jnp.float32)
        grad_gate = (grad * mixed * silu_slope(gate)).astype(jnp.bfloat16).astype(jnp.float32)
        put(sums_ref, rows, channels, channels, grad_gate)
        grad_values = []
        for head, (queries, keys, probs, slope, own, _) in enumerate(parts):
            part = take(grad_mixed, head * HD, HD).astype(jnp.bfloat16)
            grad_values.append(dot_tn(probs.astype(jnp.bfloat16), part))
            grad_probs = dot_nt(part, own)
            centred = grad_probs - jnp.sum(probs * grad_probs, axis=-1, keepdims=True)
            score_grad = (centred * slope).astype(jnp.bfloat16)
            for place, value in (
                (head, dot(score_grad, keys)),
                (heads + head, dot_tn(score_grad, queries)),
            ):
                value = (value / math.sqrt(width)).astype(jnp.bfloat16).astype(jnp.float32)
                put(sums_ref, rows, 2 * channels + place * width, width, value)
        grad_values = join(grad_values)
        grad_pre = sum(moved(grad_values, -tap) * taps[tap : tap + 1] for tap in range(3))
        put(sums_ref, rows, 0, channels, grad_pre.astype(jnp.bfloat16).astype(jnp.float32))
        for tap in range(3):
            taps_grad[tap] = taps_grad[tap] + jnp.sum(
                grad_values * moved(pre_values, tap), axis=0, keepdims=True
            )
    for tap in range(3):
        taps_grad_ref[pl.ds(tap, 1), :] = taps_grad[tap]
    low_ref[...] = sums_ref[...].astype(jnp.bfloat16)
    for column in range(0, stop, LANES):
        size = min(WIDE, stop - column)
        if column % WIDE:
            continue
        place = pl.ds(column, size)
        block_ref[:, place] = dot_tn(rows_ref[...], low_ref[:, place]).astype(jnp.bfloat16)
    last = dot_tn(grads_ref[...], gated_ref[...]).astype(jnp.bfloat16)
    block_ref[:, pl.ds(stop, WIDE)] = last + rest_ref[...]
    for index in range(2):
        terms = dot_nt(low_ref[pl.ds(index * length, length), :], attn_ref[:, pl.ds(0, stop)])
        if index == 0:
            mine_ref[...] = terms
        else:
            other_ref[...] = terms.astype(jnp.bfloat16)


def whole_call(kernel, inputs, shapes, scratch, flops):
    def whole(shape):
        return pl.BlockSpec(shape, lambda step: (0,) * len(shape), pipeline_mode=pl.Buffered(1))

    return pl.pallas_call(
        kernel,
        grid=(1,),
        out_shape=[jax.ShapeDtypeStruct(shape, kind) for shape, kind in shapes],
        in_specs=[whole(block.shape) for block in inputs],
        out_specs=[whole(shape) for shape, _ in shapes],
        scratch_shapes=[pltpu.VMEM(shape, kind) for shape, kind in scratch],
        compiler_params=pltpu.CompilerParams(vmem_limit_bytes=56 * 2**20),
        cost_estimate=pl.CostEstimate(flops=flops, bytes_accessed=2**16, transcendentals=0),
    )(*inputs)


def mixer_forward(channels, first, near, far, attn, taps):
    length, model = near.shape
    stop = attn.shape[1] - WIDE
    shapes = (
        ((length, model), jnp.float32),
        ((length, model), jnp.bfloat16),
        ((2 * length, stop), jnp.float32),
        ((2 * length, WIDE), jnp.bfloat16),
    )
    kernel = functools.partial(mixer_kernel, channels, first)
    return whole_call(kernel, (near, far, attn, taps), shapes, (), 2**20)


def mixer_backward(channels, first, near, far, near_grad, far_grad, attn, taps, both, gated, rest):
    length, model = near.shape
    stop = both.shape[1]
    shapes = (
        ((model, stop + WIDE), jnp.bfloat16),
        ((length, model), jnp.float32),
        ((length, model), jnp.bfloat16),
        (taps.shape, jnp.float32),
    )
    scratch = (
        ((2 * length, model), jnp.bfloat16),
        ((2 * length, model), jnp.bfloat16),
        ((2 * length, stop), jnp.float32),
        ((2 * length, stop), jnp.bfloat16),
    )
    inputs = (near, far, near_grad, far_grad, attn, taps, both, gated, rest)
    return whole_call(functools.partial(mixer_back_kernel, channels, first), inputs, shapes, scratch, 2**20)


def end_kernel(
    channels, units, tail, core_ref, mine_ref, other_ref, low_ref, high_ref, kept_ref,
    vgate_ref, out_ref, pair_ref, down_ref,
):
    step = pl.program_id(0)
    lower = core_ref[0] == 0
    mine, other = (ref[...].astype(jnp.float32) for ref in (mine_ref, other_ref))
    low = jnp.where(lower, mine, low_ref[...].astype(jnp.float32))
    high = jnp.where(lower, other, high_ref[...].astype(jnp.float32))
    size = mine.shape[1]
    wide = pair_ref.shape[1] // 2

    @pl.when(step == 0)
    def _():
        for place in range(2):
            parts = [take(block, place * channels, channels) for block in (low, high)]
            empty = jnp.zeros_like(parts[0])
            first = jnp.concatenate([parts[0], empty], axis=1)
            second = pltpu.roll(jnp.concatenate([parts[1], empty], axis=1), channels, 1)
            vgate_ref[:, place, :] = (first + second)[:, : 2 * channels]
        for place, block in enumerate((low, high)):
            turned = jnp.swapaxes(block[:, size - WIDE :], 0, 1)
            out_ref[pl.ds(place * channels, channels), :] = turned[:channels]
        for place, block in enumerate((jnp.where(lower, mine, other), jnp.where(lower, other, mine))):
            turned = jnp.swapaxes(block[:, size - WIDE - LANES : size - WIDE], 0, 1)
            for half in range(2):
                start = LANES - (2 - half) * wide
                pair_ref[half, pl.ds(place * wide, wide), :] = turned[start : start + wide]

    for place, block in enumerate((low, high)):

        @pl.when(step == place)
        def _(place=place, block=block):
            stop = units * (place + 1) % LANES or LANES
            last = block[:, size - LANES :]
            if stop < LANES:
                last = pltpu.roll(last, stop, 1)
            column = lanes(last)
            inside = (column >= stop - tail) & (column < stop)
            down_ref[...] = jnp.where(inside, last, kept_ref[...])


def end_call(channels, tail, width, core, mine, other, low, high, down):
    count, size = mine.shape
    units = down.shape[1] // 2
    first, second = (units - 1) // LANES, (2 * units - 1) // LANES

    def whole(shape):
        return pl.BlockSpec(shape, lambda step: (0,) * len(shape))

    tile = pl.BlockSpec((count, LANES), lambda step: (0, first + step * (second - first)))
    shapes = ((count, 2, 2 * channels), (2 * channels, count), (2, width, count))
    return pl.pallas_call(
        functools.partial(end_kernel, channels, units, tail),
        grid=(2,),
        out_shape=[jax.ShapeDtypeStruct(shape, jnp.float32) for shape in (*shapes, down.shape)],
        in_specs=[pl.BlockSpec(memory_space=pltpu.SMEM)]
        + [whole((count, size))] * 4
        + [tile],
        out_specs=[whole(shape) for shape in shapes] + [tile],
        input_output_aliases={5: 3},
        compiler_params=pltpu.CompilerParams(vmem_limit_bytes=48 * 2**20),
        cost_estimate=pl.CostEstimate(flops=2**20, bytes_accessed=2**27, transcendentals=0),
    )(core.reshape(1), mine, other, low, high, down)


def by_rows(block):
    return with_layout_constraint(block, Layout(major_to_minor=tuple(range(block.ndim))))


class Queue:
    def __init__(self):
        self.done = []

    def scatter(self, *grads):
        block = by_rows(jnp.concatenate(grads, axis=1) if len(grads) > 1 else grads[0])
        if self.done:
            block, self.done[-1] = lax.optimization_barrier((block, self.done[-1]))
        self.done.append(by_rows(lax.psum_scatter(block, "dp", scatter_dimension=0, tiled=True)))


def body(
    boundary, lengths, norm_gains, conv_taps, lin_qk, win_qk, value_gate, out_weight, gate_up, down_weight
):
    core = lax.axis_index("section")
    index = lax.axis_index("tensor")
    lower = core == 0
    rows_dev, model = boundary.shape[2:]
    channels = value_gate.shape[-1] // 2
    units = gate_up.shape[-1] // 2
    main = units // LANES * LANES
    tail = -(3 * channels + lin_qk.shape[-1]) % LANES

    def half(block, axis, which):
        size = block.shape[axis] // 2
        return lax.dynamic_slice_in_dim(block, which * size, size, axis)

    def both_layers(build):
        mine = build(core)
        other = swap(build(1 - core))
        return (jnp.where(lower, mine, other), jnp.where(lower, other, mine))

    def attn_piece(which):
        values = half(value_gate[0], 2, which)
        last = half(down_weight[0], 0, which)[units - tail :]
        return jnp.concatenate(
            [values[:, 0], values[:, 1], half(out_weight[0], 0, which).T, last.T], axis=1
        )

    def feed_piece(which):
        pair = half(gate_up[0], 2, which)
        down = half(down_weight[0], 0, which).T
        return jnp.concatenate(
            [down[:, :main], pair[:, 0, :main], pair[:, 1, :main], pair[:, 0, main:], pair[:, 1, main:], down[:, main : units - tail]],
            axis=1,
        )

    def fetch(piece):
        return lax.all_gather(piece, "dp", axis=0, tiled=True)

    def with_pair(attn, pair):
        pair = half(pair, 2, core)
        both = 2 * channels
        return jnp.concatenate([attn[:, :both], pair[:, 0], pair[:, 1], attn[:, both:]], axis=1)

    attn_parts = both_layers(attn_piece)
    feed_parts = both_layers(feed_piece)
    attn_zero = fetch(with_pair(attn_parts[0], lin_qk))
    packed = fetch(feed_parts[0])
    split = packed.shape[1]
    attn_zero, attn_one = lax.optimization_barrier((attn_zero, with_pair(attn_parts[1], win_qk)))
    attn_one = ring_gather(attn_one)
    feed_one = fetch(feed_parts[1])
    down_one = jnp.concatenate(
        [feed_one[:, :main], feed_one[:, main + 2 * units :], attn_one[:, attn_one.shape[1] - tail :]], axis=1
    )

    small = jnp.concatenate([norm_gains[0], conv_taps[0]], axis=0)
    small_other = swap(small)
    small_zero = jnp.where(lower, small, small_other)
    small_one = jnp.where(lower, small_other, small)
    offset = (2 * index + core) * channels

    def own_taps(block):
        own = lax.dynamic_slice_in_dim(block[2:], offset, channels, 1)
        return jnp.pad(own, ((0, -own.shape[0] % SUBLANES), (0, WIDE - channels)))

    held = boundary[0]
    keep = lax.dynamic_index_in_dim(held, core, 0, keepdims=False)
    other = swap(lax.dynamic_index_in_dim(held, 1 - core, 0, keepdims=False))
    entering = jnp.where(lower, keep, other).astype(jnp.float32)
    cotangent = jnp.where(lower, other, keep).astype(jnp.float32)
    length = lax.dynamic_index_in_dim(lengths, core, 0, keepdims=False)
    place = index * rows_dev + jnp.arange(rows_dev)
    mask = (place < length).astype(jnp.float32)[:, None]

    queue = Queue()
    gains_zero, gains_one = small_zero[:2], small_one[:2]
    taps_zero, taps_one = own_taps(small_zero), own_taps(small_one)

    def mix(rows, gain, attn, taps, first):
        scale, normed = rms_rows(rows, gain)
        near, far = spread_pair(normed)
        mine, other, both, gated = mixer_forward(channels, first, near, far, attn, taps)
        return (rows + collect_pair(mine, other), (rows, scale, near, far, both, gated))

    def mix_back(kept, grad_out, gain, attn, taps, rest, first):
        rows, scale, near, far, both, gated = kept
        block, mine, other, grad_taps = mixer_backward(
            channels, first, near, far, *spread_pair(grad_out), attn, taps, both, gated, rest
        )
        back, grad_gain = rms_back(rows, scale, gain, collect_pair(mine, other))
        return (block, grad_out + back, grad_gain, grad_taps[: conv_taps.shape[1], :channels])

    hidden, kept_zero = mix(entering, gains_zero[0], attn_zero, taps_zero, True)
    scale, normed = rms_rows(hidden, gains_zero[1])
    near, far = spread_pair(normed)
    near, far, attn_one = lax.optimization_barrier((near, far, attn_one))
    kept_feed = (hidden, scale, near, far)
    middle = hidden + collect_pair(*feed_terms(units, tail, near, far, packed, attn_zero))
    middle = middle.astype(jnp.bfloat16).astype(jnp.float32)

    hidden, kept_one = mix(middle, gains_one[0], attn_one, taps_one, False)
    scale, normed = rms_rows(hidden, gains_one[1])
    grad_out = cotangent * mask
    block, rest, grad_halves, inner = feed_both(
        units, tail, *spread_pair(normed), *spread_pair(grad_out), feed_one, attn_one
    )
    queue.scatter(block)
    final = hidden + collect(dot_nt(inner, down_one))
    back, gain_two = rms_back(hidden, scale, gains_one[1], collect(dot_nt(grad_halves, feed_one[:, main:])))
    attn_grads, grad_middle, gain_one, taps_one = mix_back(
        kept_one, grad_out + back, gains_one[0], attn_one, taps_one, rest, False
    )
    gains_one = jnp.stack([gain_one, gain_two])

    grad_middle = grad_middle.astype(jnp.bfloat16).astype(jnp.float32)
    hidden, scale, near, far = kept_feed
    block, rest, grad_halves, _ = feed_both(
        units, tail, near, far, *spread_pair(grad_middle), packed, attn_zero, attn_grads
    )
    queue.scatter(block)
    terms = dot_nt(grad_halves, packed[:, main:split])
    back, gain_two = rms_back(hidden, scale, gains_zero[1], collect(terms))
    attn_grads, grad_start, gain_one, taps_zero = mix_back(
        kept_zero, grad_middle + back, gains_zero[0], attn_zero, taps_zero, rest, True
    )
    queue.scatter(attn_grads)
    gains_zero = jnp.stack([gain_one, gain_two])

    edge = attn_one.shape[1]
    grads_one = (queue.done[0], queue.done[1][:, :edge])
    grads_zero = (queue.done[1][:, edge:], queue.done[2])

    def own_small(gains, taps):
        spot = jnp.zeros((taps.shape[0], model), jnp.float32)
        return jnp.concatenate([gains, lax.dynamic_update_slice_in_dim(spot, taps, offset, 1)], axis=0)

    sums = sum_all(jnp.stack([own_small(gains_zero, taps_zero), own_small(gains_one, taps_one)]))
    sums = lax.dynamic_index_in_dim(sums, core, 0, keepdims=True)

    final = final * mask
    ends_keep = jnp.where(lower, grad_start, final)
    ends_other = swap(jnp.where(lower, final, grad_start))
    ends = jnp.where(lower, jnp.stack([ends_keep, ends_other]), jnp.stack([ends_other, ends_keep]))

    def home(zero, one):
        mine = jnp.where(lower, zero, one)
        other = swap(jnp.where(lower, one, zero))
        return (jnp.where(lower, mine, other), jnp.where(lower, other, mine))

    def halves(low, high, axis):
        return jnp.concatenate([low, high], axis=axis).astype(jnp.float32)

    def pair_home(block):
        size = block.shape[1] // 2
        other = swap(block)
        low = jnp.where(lower, block, other)
        high = jnp.where(lower, other, block)
        return jnp.stack(
            [halves(low[:, :size], high[:, :size], 1), halves(low[:, size:], high[:, size:], 1)], axis=1
        )

    last = grads_zero[1]
    early = grads_one[1]
    both = 2 * channels
    gap = last.shape[1] - both - WIDE
    own = jnp.concatenate(
        [early[:, :both], jnp.zeros((early.shape[0], gap), early.dtype), early[:, early.shape[1] - WIDE :]],
        axis=1,
    )
    away = swap(own)

    def unpack(block):
        wide = block[:, main:]
        (gate, upper), (gate_rest, upper_rest) = gates(wide, units)
        empty = jnp.zeros((block.shape[0], tail), block.dtype)
        down = jnp.concatenate([block[:, :main], wide[:, 2 * units :], empty], axis=1)
        return (
            jnp.concatenate([gate, gate_rest], axis=1),
            jnp.concatenate([upper, upper_rest], axis=1),
            down,
        )

    low, high = home(grads_zero[0], grads_one[0])
    low, high = unpack(low), unpack(high)
    gate_up_grad = jnp.stack([halves(low[0], high[0], 1), halves(low[1], high[1], 1)], axis=1)
    down_grad = by_rows(halves(low[2], high[2], 1))
    win_grad = by_rows(pair_home(early[:, both : early.shape[1] - WIDE]))
    gate_up_grad = by_rows(gate_up_grad)
    low, high = jnp.where(lower, own, away), jnp.where(lower, away, own)
    last, low, high, gate_up_grad, down_grad, win_grad, ends, sums = lax.optimization_barrier(
        (last, low, high, gate_up_grad, down_grad, win_grad, ends, sums)
    )
    vgate_grad, out_grad, pair_grad, down_grad = end_call(
        channels, tail, gap, core, last, swap(last), low, high, down_grad
    )
    return (
        ends[None],
        sums[:, :2],
        sums[:, 2:],
        jnp.transpose(pair_grad, (2, 0, 1)),
        win_grad,
        vgate_grad[None],
        out_grad[None],
        gate_up_grad[None],
        down_grad.T[None],
    )


def solution(mesh):
    in_specs = (
        P("section", "dp", "tensor", None),
        P("dp"),
        P("section", None, None),
        P("section", None, None),
        P("dp", None, "tensor"),
        P("dp", None, "tensor"),
        P("section", "dp", None, "tensor"),
        P("section", "tensor", "dp"),
        P("section", "dp", None, "tensor"),
        P("section", "tensor", "dp"),
    )
    out_specs = (
        P("section", "dp", "tensor", None),
        P("section", None, None),
        P("section", None, None),
        P("dp", None, "tensor"),
        P("dp", None, "tensor"),
        P("section", "dp", None, "tensor"),
        P("section", "tensor", "dp"),
        P("section", "dp", None, "tensor"),
        P("section", "tensor", "dp"),
    )
    return jax.shard_map(body, mesh=mesh, in_specs=in_specs, out_specs=out_specs, check_vma=False)
```

```python
import functools
import math

import jax
import jax.numpy as jnp
from jax import lax
from jax.experimental import pallas as pl
from jax.experimental.layout import Layout, with_layout_constraint
from jax.experimental.pallas import tpu as pltpu
from jax.sharding import PartitionSpec as P

WIN = 64
HD = 112
LANES = 128
WIDE = 256
SUBLANES = 8
CHUNKS = 2

EPS = 1e-06


def silu_slope(value):
    sigma = jax.nn.sigmoid(value)
    return sigma * (1.0 + value * (1.0 - sigma))


def rms_rows(rows, gain):
    scale = lax.rsqrt(jnp.mean(rows * rows, axis=-1, keepdims=True) + EPS)
    return (scale, rows * scale * gain)


def rms_back(rows, scale, gain, grad):
    normal = rows * scale
    weighted = grad * gain
    inner = jnp.mean(weighted * normal, axis=-1, keepdims=True)
    return (scale * (weighted - normal * inner), jnp.sum(grad * normal, axis=0))


def swap(block):
    return lax.ppermute(block, "section", [(0, 1), (1, 0)])


def spread_pair(rows):
    mine = lax.all_gather(rows.astype(jnp.bfloat16), "tensor", axis=0, tiled=True)
    return (mine, swap(mine))


def spread(rows):
    return jnp.concatenate(spread_pair(rows), axis=0)


def collect(terms):
    length = terms.shape[0] // 2
    return collect_pair(terms[:length], terms[length:].astype(jnp.bfloat16))


def collect_pair(mine, other):
    size = lax.axis_size("tensor")
    count = mine.shape[0] // size
    index = lax.axis_index("tensor")
    part = mine + swap(other).astype(jnp.float32)
    low = part.astype(jnp.bfloat16)
    total = lax.dynamic_slice_in_dim(part, index * count, count, 0)
    for offset in range(1, size):
        block = lax.dynamic_slice_in_dim(low, (index ^ offset) * count, count, 0)
        pairs = [(i, i ^ offset) for i in range(size)]
        total = total + lax.ppermute(block, "tensor", pairs).astype(jnp.float32)
    return total


def ring_step(piece):
    size = lax.axis_size("dp")
    return lax.ppermute(piece, "dp", [(i, (i + 1) % size) for i in range(size)])


def ring_gather(piece, moved=None):
    size = lax.axis_size("dp")
    index = lax.axis_index("dp")
    count = piece.shape[0]
    full = jnp.zeros((size * count, piece.shape[1]), piece.dtype)
    for step in range(size):
        if step == 1 and moved is not None:
            piece = moved
        elif step:
            piece = ring_step(piece)
        full = lax.dynamic_update_slice_in_dim(full, piece, (index - step) % size * count, 0)
    return full


def sum_all(block):
    for axis in ("section", "tensor", "dp"):
        size = lax.axis_size(axis)
        step = 1
        while step < size:
            pairs = [(i, i ^ step) for i in range(size)]
            block = block + lax.ppermute(block, axis, pairs)
            step *= 2
    return block


def dot(one, two):
    return jnp.dot(one, two, preferred_element_type=jnp.float32)


def dot_nt(one, two):
    return lax.dot_general(one, two, (((1,), (1,)), ((), ())), preferred_element_type=jnp.float32)


def dot_tn(one, two):
    return lax.dot_general(one, two, (((0,), (0,)), ((), ())), preferred_element_type=jnp.float32)


def gates(halves, units):
    main = units // LANES * LANES
    stop = main + units
    return (
        (halves[:, :main], halves[:, main : 2 * main]),
        (halves[:, 2 * main : stop], halves[:, stop : 2 * units]),
    )


def lanes(block):
    return lax.broadcasted_iota(jnp.int32, block.shape, 1)


def forward_kernel(units, tail, near_ref, far_ref, feed_ref, last_ref, mine_ref, other_ref, rows_ref, inner_ref):
    main = units // LANES * LANES
    over = units - main
    length = near_ref.shape[0]
    rows_ref[:length] = near_ref[...]
    rows_ref[length:] = far_ref[...]
    rows = rows_ref[...]
    for start in range(0, main, WIDE):
        gate = dot(rows, feed_ref[:, pl.ds(main + start, WIDE)])
        upper = dot(rows, feed_ref[:, pl.ds(2 * main + start, WIDE)])
        inner_ref[:, pl.ds(start, WIDE)] = (jax.nn.silu(gate) * upper).astype(jnp.bfloat16)
    ends = feed_ref[:, pl.ds(3 * main, WIDE)]
    both = dot(rows, ends)
    upper = pltpu.roll(both, WIDE - over, 1)
    inner = jax.nn.silu(both[:, :LANES]) * upper[:, :LANES]
    inner = jnp.where(lanes(inner) < over, inner, 0.0)
    low = pltpu.roll(jnp.concatenate([inner, jnp.zeros_like(inner)], axis=1), 2 * over, 1)
    low = jnp.where(lanes(low) < 2 * over, 0.0, low).astype(jnp.bfloat16)
    high = pltpu.roll(inner, LANES - over, 1)
    high = jnp.where(lanes(high) < LANES - tail, 0.0, high).astype(jnp.bfloat16)
    terms = dot_nt(inner_ref[...], feed_ref[:, pl.ds(0, main)]) + dot_nt(low, ends) + dot_nt(high, last_ref[...])
    mine_ref[...] = terms[:length]
    other_ref[...] = terms[length:].astype(jnp.bfloat16)


def feed_terms(units, tail, near, far, feed, attn):
    length, model = near.shape
    main = units // LANES * LANES
    width = 3 * units - tail
    end = attn.shape[1] // LANES - 1

    def whole(shape):
        return pl.BlockSpec(shape, lambda step: (0, 0), pipeline_mode=pl.Buffered(1))

    return pl.pallas_call(
        functools.partial(forward_kernel, units, tail),
        grid=(1,),
        out_shape=[
            jax.ShapeDtypeStruct((length, model), jnp.float32),
            jax.ShapeDtypeStruct((length, model), jnp.bfloat16),
        ],
        in_specs=[
            whole((length, model)),
            whole((length, model)),
            whole((model, width)),
            pl.BlockSpec((model, LANES), lambda step: (0, end)),
        ],
        out_specs=[whole((length, model))] * 2,
        scratch_shapes=[
            pltpu.VMEM((2 * length, model), jnp.bfloat16),
            pltpu.VMEM((2 * length, main), jnp.bfloat16),
        ],
        compiler_params=pltpu.CompilerParams(vmem_limit_bytes=48 * 2**20),
        cost_estimate=pl.CostEstimate(flops=2**20, bytes_accessed=2**16, transcendentals=0),
    )(near, far, feed, attn)


def feed_kernel(
    units, tail, near_ref, far_ref, near_grad_ref, far_grad_ref, feed_ref, last_ref, *refs
):
    extras, refs = refs[:-8], refs[-8:]
    block_ref, rest_ref, halves_ref, inner_ref, rows_ref, grads_ref, wide_ref, down_ref = refs
    main = units // LANES * LANES
    over = units - main
    step = pl.program_id(0)
    length = near_ref.shape[0]
    size = feed_ref.shape[0]
    chunks = rows_ref.shape[1] // size

    def parts(gate, upper, grad):
        sigma = jax.nn.sigmoid(gate)
        act = gate * sigma
        slope = sigma * (1.0 + gate * (1.0 - sigma))
        return (act * upper, grad * upper * slope, grad * act)

    @pl.when(step == 0)
    def _():
        rows_ref[:length] = near_ref[...]
        rows_ref[length:] = far_ref[...]
        grads_ref[:length] = near_grad_ref[...]
        grads_ref[length:] = far_grad_ref[...]

    for chunk in range(chunks):
        place = pl.ds(chunk * size, size)

        @pl.when(step == chunk)
        def _(chunk=chunk, place=place):
            rows, branch = rows_ref[:, place], grads_ref[:, place]
            wide = dot(rows, feed_ref[:, pl.ds(main, 2 * main + WIDE)])
            down = dot(branch, feed_ref[:, pl.ds(0, main)])
            ends = dot(branch, feed_ref[:, pl.ds(3 * main, WIDE)])
            if chunk:
                wide = wide + wide_ref[...]
                down = down + down_ref[:, pl.ds(0, main)]
                ends = ends + down_ref[:, pl.ds(main, WIDE)]
            if chunk < chunks - 1:
                wide_ref[...] = wide
                down_ref[:, pl.ds(0, main)] = down
                down_ref[:, pl.ds(main, WIDE)] = ends
                return
            inner, grad_gate, grad_upper = (
                part.astype(jnp.bfloat16) for part in parts(wide[:, :main], wide[:, main : 2 * main], down)
            )
            inner_ref[:, pl.ds(0, main)] = inner
            halves_ref[:, pl.ds(0, main)] = grad_gate
            halves_ref[:, pl.ds(main, main)] = grad_upper
            both = wide[:, 2 * main :]
            upper = pltpu.roll(both, WIDE - over, 1)
            grad = pltpu.roll(ends, WIDE - 2 * over, 1)[:, :LANES]
            more = pltpu.roll(dot(grads_ref[...], last_ref[...]), over, 1)
            grad = jnp.where(lanes(grad) < over - tail, grad, more)
            inner, grad_gate, grad_upper = (
                jnp.where(lanes(part) < over, part, 0.0)
                for part in parts(both[:, :LANES], upper[:, :LANES], grad)
            )
            inner_ref[:, pl.ds(main, LANES)] = inner.astype(jnp.bfloat16)
            empty = jnp.zeros_like(grad_gate)
            last = jnp.concatenate([grad_gate, empty], axis=1)
            last = last + pltpu.roll(jnp.concatenate([grad_upper, empty], axis=1), over, 1)
            halves_ref[:, pl.ds(2 * main, WIDE)] = last.astype(jnp.bfloat16)

        @pl.when(step == chunks + chunk)
        def _(place=place):
            base = 0
            for extra in extras:
                block_ref[:, pl.ds(base, extra.shape[1])] = extra[...]
                base += extra.shape[1]
            rows, branch = rows_ref[:, place], grads_ref[:, place]
            down = dot_tn(branch, inner_ref[:, pl.ds(0, main)])
            block_ref[:, pl.ds(base, main)] = down.astype(jnp.bfloat16)
            wide = dot_tn(rows, halves_ref[:, pl.ds(0, 2 * main)])
            block_ref[:, pl.ds(base + main, 2 * main)] = wide.astype(jnp.bfloat16)
            down = dot_tn(branch, inner_ref[:, pl.ds(main, LANES)])
            down = jnp.concatenate([down, jnp.zeros_like(down)], axis=1)
            wide = dot_tn(rows, halves_ref[:, pl.ds(2 * main, WIDE)])
            wide = jnp.where(lanes(wide) < 2 * over, wide, pltpu.roll(down, 2 * over, 1))
            block_ref[:, pl.ds(base + 3 * main, WIDE)] = wide.astype(jnp.bfloat16)
            moved = pltpu.roll(down, WIDE - over, 1)
            rest_ref[...] = jnp.where(lanes(moved) < WIDE - tail, 0.0, moved).astype(jnp.bfloat16)


def feed_both(units, tail, near, far, near_grad, far_grad, feed, attn, *extras):
    count, model = 2 * near.shape[0], near.shape[1]
    main = units // LANES * LANES
    width = 3 * units - tail
    size = model // CHUNKS
    total = width + sum(extra.shape[1] for extra in extras)
    shapes = ((model, total), (model, WIDE), (count, width - main), (count, main + LANES))
    end = attn.shape[1] // LANES - 1

    def later(columns):
        return pl.BlockSpec((size, columns), lambda step: (jnp.maximum(step - CHUNKS, 0), 0))

    def whole(shape):
        return pl.BlockSpec(shape, lambda step: (0, 0), pipeline_mode=pl.Buffered(1))

    return pl.pallas_call(
        functools.partial(feed_kernel, units, tail),
        grid=(2 * CHUNKS,),
        out_shape=[jax.ShapeDtypeStruct(shape, jnp.bfloat16) for shape in shapes],
        in_specs=[whole(near.shape)] * 4
        + [
            pl.BlockSpec((size, width), lambda step: (jnp.minimum(step, CHUNKS - 1), 0)),
            pl.BlockSpec((model, LANES), lambda step: (0, end), pipeline_mode=pl.Buffered(1)),
        ]
        + [later(extra.shape[1]) for extra in extras],
        out_specs=[later(total), later(WIDE), whole(shapes[2]), whole(shapes[3])],
        scratch_shapes=[
            pltpu.VMEM((count, model), jnp.bfloat16),
            pltpu.VMEM((count, model), jnp.bfloat16),
            pltpu.VMEM((count, width - main), jnp.float32),
            pltpu.VMEM((count, main + WIDE), jnp.float32),
        ],
        compiler_params=pltpu.CompilerParams(vmem_limit_bytes=56 * 2**20),
        cost_estimate=pl.CostEstimate(
            flops=4 * count * model * width,
            bytes_accessed=20 * 2**20,
            transcendentals=count * units,
        ),
    )(near, far, near_grad, far_grad, feed, attn, *extras)


def take(block, column, width):
    base = column // LANES * LANES
    shift = column - base
    stop = base + -(-(shift + width) // LANES) * LANES
    part = block[:, base:stop]
    if shift:
        part = pltpu.roll(part, stop - base - shift, 1)
    part = part[:, : -(-width // LANES) * LANES]
    return jnp.where(lanes(part) < width, part, 0.0)


def put(target, rows, column, width, part):
    base = column // LANES * LANES
    shift = column - base
    size = -(-(shift + width) // LANES) * LANES
    if size > part.shape[1]:
        empty = jnp.zeros((part.shape[0], size - part.shape[1]), part.dtype)
        part = jnp.concatenate([part, empty], axis=1)
    if shift:
        part = pltpu.roll(part, shift, 1)
    target[rows, pl.ds(base, size)] += part


def moved(block, distance):
    count = block.shape[0]
    if distance == 0:
        return block
    row = lax.broadcasted_iota(jnp.int32, block.shape, 0)
    rolled = pltpu.roll(block, distance % count, 0)
    inside = row >= distance if distance > 0 else row < count + distance
    return jnp.where(inside, rolled, 0.0)


def mixer_parts(both, taps, channels, first):
    length = both.shape[0]
    heads = channels // HD
    width = (both.shape[1] - 2 * channels) // (2 * heads)
    pre_values = take(both, 0, channels)
    values = sum(moved(pre_values, tap) * taps[tap : tap + 1] for tap in range(3))
    values = values.astype(jnp.bfloat16).astype(jnp.float32)
    gate = take(both, channels, channels)
    query = lax.broadcasted_iota(jnp.int32, (length, length), 0)
    key = lax.broadcasted_iota(jnp.int32, (length, length), 1)
    allowed = key <= query
    if not first:
        allowed = allowed & (query - key < WIN)
    parts = []
    for head in range(heads):
        queries = take(both, 2 * channels + head * width, width).astype(jnp.bfloat16)
        keys = take(both, 2 * channels + (heads + head) * width, width).astype(jnp.bfloat16)
        scores = dot_nt(queries, keys) / math.sqrt(width)
        if first:
            kernel = jnp.where(allowed, 1.0 + scores + 0.5 * scores * scores, 0.0)
            total = jnp.sum(kernel, axis=-1, keepdims=True)
            probs = kernel / total
            slope = jnp.where(allowed, (1.0 + scores) / total, 0.0)
        else:
            scores = jnp.where(allowed, scores, -1e30)
            kernel = jnp.exp(scores - jnp.max(scores, axis=-1, keepdims=True))
            probs = kernel / jnp.sum(kernel, axis=-1, keepdims=True)
            slope = probs
        own = take(values, head * HD, HD).astype(jnp.bfloat16)
        parts.append((queries, keys, probs, slope, own, dot(probs.astype(jnp.bfloat16), own)))
    return (pre_values, gate, parts)


def join(parts):
    empty = jnp.zeros_like(parts[0])
    total = 0.0
    for head, part in enumerate(parts):
        part = jnp.concatenate([part, empty], axis=1)
        total = total + (pltpu.roll(part, head * HD, 1) if head else part)
    return total


def mixer_kernel(
    channels, first, near_ref, far_ref, attn_ref, taps_ref, mine_ref, other_ref, both_ref, gated_ref
):
    length = near_ref.shape[0]
    stop = both_ref.shape[1]
    for index, rows in enumerate((near_ref, far_ref)):
        both = dot(rows[...], attn_ref[:, pl.ds(0, stop)])
        both_ref[pl.ds(index * length, length), :] = both
        _, gate, parts = mixer_parts(both, taps_ref[...], channels, first)
        gated = (join([part[-1] for part in parts]) * gate * jax.nn.sigmoid(gate)).astype(jnp.bfloat16)
        gated_ref[pl.ds(index * length, length), :] = gated
        terms = dot_nt(gated, attn_ref[:, pl.ds(stop, WIDE)])
        if index == 0:
            mine_ref[...] = terms
        else:
            other_ref[...] = terms.astype(jnp.bfloat16)


def mixer_back_kernel(
    channels, first, near_ref, far_ref, near_grad_ref, far_grad_ref, attn_ref, taps_ref, both_ref,
    gated_ref, rest_ref, block_ref, mine_ref, other_ref, taps_grad_ref, rows_ref, grads_ref, sums_ref, low_ref,
):
    length = near_ref.shape[0]
    stop = both_ref.shape[1]
    heads = channels // HD
    width = (stop - 2 * channels) // (2 * heads)
    taps = taps_ref[...]
    sums_ref[...] = jnp.zeros_like(sums_ref)
    taps_grad = [0.0] * 3
    rows_ref[:length] = near_ref[...]
    rows_ref[length:] = far_ref[...]
    grads_ref[:length] = near_grad_ref[...]
    grads_ref[length:] = far_grad_ref[...]
    for index in range(2):
        rows = pl.ds(index * length, length)
        pre_values, gate, parts = mixer_parts(both_ref[rows, :], taps, channels, first)
        mixed = join([part[-1] for part in parts])
        grad = dot(grads_ref[rows, :], attn_ref[:, pl.ds(stop, WIDE)])
        grad = jnp.where(lanes(grad) < channels, grad, 0.0)
        sigma = jax.nn.sigmoid(gate)
        grad_mixed = (grad * (gate * sigma)).astype(jnp.bfloat16).astype(jnp.float32)
        grad_gate = (grad * mixed * silu_slope(gate)).astype(jnp.bfloat16).astype(jnp.float32)
        put(sums_ref, rows, channels, channels, grad_gate)
        grad_values = []
        for head, (queries, keys, probs, slope, own, _) in enumerate(parts):
            part = take(grad_mixed, head * HD, HD).astype(jnp.bfloat16)
            grad_values.append(dot_tn(probs.astype(jnp.bfloat16), part))
            grad_probs = dot_nt(part, own)
            centred = grad_probs - jnp.sum(probs * grad_probs, axis=-1, keepdims=True)
            score_grad = (centred * slope).astype(jnp.bfloat16)
            for place, value in (
                (head, dot(score_grad, keys)),
                (heads + head, dot_tn(score_grad, queries)),
            ):
                value = (value / math.sqrt(width)).astype(jnp.bfloat16).astype(jnp.float32)
                put(sums_ref, rows, 2 * channels + place * width, width, value)
        grad_values = join(grad_values)
        grad_pre = sum(moved(grad_values, -tap) * taps[tap : tap + 1] for tap in range(3))
        put(sums_ref, rows, 0, channels, grad_pre.astype(jnp.bfloat16).astype(jnp.float32))
        for tap in range(3):
            taps_grad[tap] = taps_grad[tap] + jnp.sum(
                grad_values * moved(pre_values, tap), axis=0, keepdims=True
            )
    for tap in range(3):
        taps_grad_ref[pl.ds(tap, 1), :] = taps_grad[tap]
    low_ref[...] = sums_ref[...].astype(jnp.bfloat16)
    for column in range(0, stop, LANES):
        size = min(WIDE, stop - column)
        if column % WIDE:
            continue
        place = pl.ds(column, size)
        block_ref[:, place] = dot_tn(rows_ref[...], low_ref[:, place]).astype(jnp.bfloat16)
    last = dot_tn(grads_ref[...], gated_ref[...]).astype(jnp.bfloat16)
    block_ref[:, pl.ds(stop, WIDE)] = last + rest_ref[...]
    for index in range(2):
        terms = dot_nt(low_ref[pl.ds(index * length, length), :], attn_ref[:, pl.ds(0, stop)])
        if index == 0:
            mine_ref[...] = terms
        else:
            other_ref[...] = terms.astype(jnp.bfloat16)


def whole_call(kernel, inputs, shapes, scratch, flops):
    def whole(shape):
        return pl.BlockSpec(shape, lambda step: (0,) * len(shape), pipeline_mode=pl.Buffered(1))

    return pl.pallas_call(
        kernel,
        grid=(1,),
        out_shape=[jax.ShapeDtypeStruct(shape, kind) for shape, kind in shapes],
        in_specs=[whole(block.shape) for block in inputs],
        out_specs=[whole(shape) for shape, _ in shapes],
        scratch_shapes=[pltpu.VMEM(shape, kind) for shape, kind in scratch],
        compiler_params=pltpu.CompilerParams(vmem_limit_bytes=56 * 2**20),
        cost_estimate=pl.CostEstimate(flops=flops, bytes_accessed=2**16, transcendentals=0),
    )(*inputs)


def mixer_forward(channels, first, near, far, attn, taps):
    length, model = near.shape
    stop = attn.shape[1] - WIDE
    shapes = (
        ((length, model), jnp.float32),
        ((length, model), jnp.bfloat16),
        ((2 * length, stop), jnp.float32),
        ((2 * length, WIDE), jnp.bfloat16),
    )
    kernel = functools.partial(mixer_kernel, channels, first)
    return whole_call(kernel, (near, far, attn, taps), shapes, (), 2**20)


def mixer_backward(channels, first, near, far, near_grad, far_grad, attn, taps, both, gated, rest):
    length, model = near.shape
    stop = both.shape[1]
    shapes = (
        ((model, stop + WIDE), jnp.bfloat16),
        ((length, model), jnp.float32),
        ((length, model), jnp.bfloat16),
        (taps.shape, jnp.float32),
    )
    scratch = (
        ((2 * length, model), jnp.bfloat16),
        ((2 * length, model), jnp.bfloat16),
        ((2 * length, stop), jnp.float32),
        ((2 * length, stop), jnp.bfloat16),
    )
    inputs = (near, far, near_grad, far_grad, attn, taps, both, gated, rest)
    return whole_call(functools.partial(mixer_back_kernel, channels, first), inputs, shapes, scratch, 2**20)


def end_kernel(
    channels, units, tail, core_ref, mine_ref, other_ref, low_ref, high_ref, kept_ref,
    vgate_ref, out_ref, pair_ref, down_ref,
):
    step = pl.program_id(0)
    lower = core_ref[0] == 0
    mine, other = (ref[...].astype(jnp.float32) for ref in (mine_ref, other_ref))
    low = jnp.where(lower, mine, low_ref[...].astype(jnp.float32))
    high = jnp.where(lower, other, high_ref[...].astype(jnp.float32))
    size = mine.shape[1]
    wide = pair_ref.shape[1] // 2

    @pl.when(step == 0)
    def _():
        for place in range(2):
            parts = [take(block, place * channels, channels) for block in (low, high)]
            empty = jnp.zeros_like(parts[0])
            first = jnp.concatenate([parts[0], empty], axis=1)
            second = pltpu.roll(jnp.concatenate([parts[1], empty], axis=1), channels, 1)
            vgate_ref[:, place, :] = (first + second)[:, : 2 * channels]
        for place, block in enumerate((low, high)):
            turned = jnp.swapaxes(block[:, size - WIDE :], 0, 1)
            out_ref[pl.ds(place * channels, channels), :] = turned[:channels]
        for place, block in enumerate((jnp.where(lower, mine, other), jnp.where(lower, other, mine))):
            turned = jnp.swapaxes(block[:, size - WIDE - LANES : size - WIDE], 0, 1)
            for half in range(2):
                start = LANES - (2 - half) * wide
                pair_ref[half, pl.ds(place * wide, wide), :] = turned[start : start + wide]

    for place, block in enumerate((low, high)):

        @pl.when(step == place)
        def _(place=place, block=block):
            stop = units * (place + 1) % LANES or LANES
            last = block[:, size - LANES :]
            if stop < LANES:
                last = pltpu.roll(last, stop, 1)
            column = lanes(last)
            inside = (column >= stop - tail) & (column < stop)
            down_ref[...] = jnp.where(inside, last, kept_ref[...])


def end_call(channels, tail, width, core, mine, other, low, high, down):
    count, size = mine.shape
    units = down.shape[1] // 2
    first, second = (units - 1) // LANES, (2 * units - 1) // LANES

    def whole(shape):
        return pl.BlockSpec(shape, lambda step: (0,) * len(shape))

    tile = pl.BlockSpec((count, LANES), lambda step: (0, first + step * (second - first)))
    shapes = ((count, 2, 2 * channels), (2 * channels, count), (2, width, count))
    return pl.pallas_call(
        functools.partial(end_kernel, channels, units, tail),
        grid=(2,),
        out_shape=[jax.ShapeDtypeStruct(shape, jnp.float32) for shape in (*shapes, down.shape)],
        in_specs=[pl.BlockSpec(memory_space=pltpu.SMEM)]
        + [whole((count, size))] * 4
        + [tile],
        out_specs=[whole(shape) for shape in shapes] + [tile],
        input_output_aliases={5: 3},
        compiler_params=pltpu.CompilerParams(vmem_limit_bytes=48 * 2**20),
        cost_estimate=pl.CostEstimate(flops=2**20, bytes_accessed=2**27, transcendentals=0),
    )(core.reshape(1), mine, other, low, high, down)


def by_rows(block):
    return with_layout_constraint(block, Layout(major_to_minor=tuple(range(block.ndim))))


class Queue:
    def __init__(self):
        self.done = []

    def scatter(self, *grads):
        block = by_rows(jnp.concatenate(grads, axis=1) if len(grads) > 1 else grads[0])
        if self.done:
            block, self.done[-1] = lax.optimization_barrier((block, self.done[-1]))
        self.done.append(by_rows(lax.psum_scatter(block, "dp", scatter_dimension=0, tiled=True)))


def body(
    boundary, lengths, norm_gains, conv_taps, lin_qk, win_qk, value_gate, out_weight, gate_up, down_weight
):
    core = lax.axis_index("section")
    index = lax.axis_index("tensor")
    lower = core == 0
    rows_dev, model = boundary.shape[2:]
    channels = value_gate.shape[-1] // 2
    units = gate_up.shape[-1] // 2
    main = units // LANES * LANES
    tail = -(3 * channels + lin_qk.shape[-1]) % LANES

    def half(block, axis, which):
        size = block.shape[axis] // 2
        return lax.dynamic_slice_in_dim(block, which * size, size, axis)

    def both_layers(build):
        mine = build(core)
        other = swap(build(1 - core))
        return (jnp.where(lower, mine, other), jnp.where(lower, other, mine))

    def attn_piece(pair, which):
        own = slice(which * channels, (which + 1) * channels)
        wide = pair.shape[2] // 2
        pair = pair[:, :, which * wide : (which + 1) * wide]
        last = down_weight[0][(which + 1) * units - tail : (which + 1) * units]
        values = value_gate[0][:, :, own]
        parts = [values[:, 0], values[:, 1], pair[:, 0], pair[:, 1], out_weight[0][own].T, last.T]
        return jnp.concatenate(parts, axis=1)

    def feed_piece(which):
        pair = half(gate_up[0], 2, which)
        down = half(down_weight[0], 0, which).T
        return jnp.concatenate(
            [down[:, :main], pair[:, 0, :main], pair[:, 1, :main], pair[:, 0, main:], pair[:, 1, main:], down[:, main : units - tail]],
            axis=1,
        )

    def fetch(piece):
        return lax.all_gather(piece, "dp", axis=0, tiled=True)

    attn_zero = fetch(jnp.where(lower, attn_piece(lin_qk, 0), swap(attn_piece(lin_qk, 1))))
    feed_parts = both_layers(feed_piece)
    split = feed_parts[0].shape[1]
    edge = split - WIDE
    most = fetch(feed_parts[0][:, :edge])
    attn_one = jnp.where(lower, swap(attn_piece(win_qk, 0)), attn_piece(win_qk, 1))
    piece = jnp.concatenate([attn_one, feed_parts[0][:, edge:]], axis=1)
    attn_zero, moved = lax.optimization_barrier((attn_zero, ring_step(piece)))
    ring = ring_gather(piece, moved)
    attn_one, ends_zero = ring[:, : attn_one.shape[1]], ring[:, attn_one.shape[1] :]
    feed_one = fetch(feed_parts[1])
    down_one = jnp.concatenate(
        [feed_one[:, :main], feed_one[:, main + 2 * units :], attn_one[:, attn_one.shape[1] - tail :]], axis=1
    )

    small = jnp.concatenate([norm_gains[0], conv_taps[0]], axis=0)
    small_other = swap(small)
    small_zero = jnp.where(lower, small, small_other)
    small_one = jnp.where(lower, small_other, small)
    offset = (2 * index + core) * channels

    def own_taps(block):
        own = lax.dynamic_slice_in_dim(block[2:], offset, channels, 1)
        return jnp.pad(own, ((0, -own.shape[0] % SUBLANES), (0, WIDE - channels)))

    held = boundary[0]
    keep = lax.dynamic_index_in_dim(held, core, 0, keepdims=False)
    other = swap(lax.dynamic_index_in_dim(held, 1 - core, 0, keepdims=False))
    entering = jnp.where(lower, keep, other).astype(jnp.float32)
    cotangent = jnp.where(lower, other, keep).astype(jnp.float32)
    length = lax.dynamic_index_in_dim(lengths, core, 0, keepdims=False)
    place = index * rows_dev + jnp.arange(rows_dev)
    mask = (place < length).astype(jnp.float32)[:, None]

    queue = Queue()
    gains_zero, gains_one = small_zero[:2], small_one[:2]
    taps_zero, taps_one = own_taps(small_zero), own_taps(small_one)

    def mix(rows, gain, attn, taps, first):
        scale, normed = rms_rows(rows, gain)
        near, far = spread_pair(normed)
        mine, other, both, gated = mixer_forward(channels, first, near, far, attn, taps)
        return (rows + collect_pair(mine, other), (rows, scale, near, far, both, gated))

    def mix_back(kept, grad_out, gain, attn, taps, rest, first):
        rows, scale, near, far, both, gated = kept
        block, mine, other, grad_taps = mixer_backward(
            channels, first, near, far, *spread_pair(grad_out), attn, taps, both, gated, rest
        )
        back, grad_gain = rms_back(rows, scale, gain, collect_pair(mine, other))
        return (block, grad_out + back, grad_gain, grad_taps[: conv_taps.shape[1], :channels])

    hidden, kept_zero = mix(entering, gains_zero[0], attn_zero, taps_zero, True)
    scale, normed = rms_rows(hidden, gains_zero[1])
    near, far = spread_pair(normed)
    grad_out = cotangent * mask
    near, far, attn_one, ends_zero, *grads_one = lax.optimization_barrier(
        (near, far, attn_one, ends_zero, *spread_pair(grad_out))
    )
    packed = jnp.concatenate([most, ends_zero], axis=1)
    kept_feed = (hidden, scale, near, far)
    middle = hidden + collect_pair(*feed_terms(units, tail, near, far, packed, attn_zero))
    middle = middle.astype(jnp.bfloat16).astype(jnp.float32)

    hidden, kept_one = mix(middle, gains_one[0], attn_one, taps_one, False)
    scale, normed = rms_rows(hidden, gains_one[1])
    block, rest, grad_halves, inner = feed_both(
        units, tail, *spread_pair(normed), *grads_one, feed_one, attn_one
    )
    queue.scatter(block)
    final = hidden + collect(dot_nt(inner[:, :units], down_one))
    back, gain_two = rms_back(hidden, scale, gains_one[1], collect(dot_nt(grad_halves, feed_one[:, main:])))
    attn_grads, grad_middle, gain_one, taps_one = mix_back(
        kept_one, grad_out + back, gains_one[0], attn_one, taps_one, rest, False
    )
    gains_one = jnp.stack([gain_one, gain_two])

    grad_middle = grad_middle.astype(jnp.bfloat16).astype(jnp.float32)
    hidden, scale, near, far = kept_feed
    block, rest, grad_halves, _ = feed_both(
        units, tail, near, far, *spread_pair(grad_middle), packed, attn_zero, attn_grads
    )
    queue.scatter(block)
    terms = dot_nt(grad_halves, packed[:, main:split])
    back, gain_two = rms_back(hidden, scale, gains_zero[1], collect(terms))
    attn_grads, grad_start, gain_one, taps_zero = mix_back(
        kept_zero, grad_middle + back, gains_zero[0], attn_zero, taps_zero, rest, True
    )
    queue.scatter(attn_grads)
    gains_zero = jnp.stack([gain_one, gain_two])

    edge = attn_one.shape[1]
    grads_one = (queue.done[0], queue.done[1][:, :edge])
    grads_zero = (queue.done[1][:, edge:], queue.done[2])

    def own_small(gains, taps):
        spot = jnp.zeros((taps.shape[0], model), jnp.float32)
        return jnp.concatenate([gains, lax.dynamic_update_slice_in_dim(spot, taps, offset, 1)], axis=0)

    sums = sum_all(jnp.stack([own_small(gains_zero, taps_zero), own_small(gains_one, taps_one)]))
    sums = lax.dynamic_index_in_dim(sums, core, 0, keepdims=True)

    final = final * mask
    ends_keep = jnp.where(lower, grad_start, final)
    ends_other = swap(jnp.where(lower, final, grad_start))
    ends = jnp.where(lower, jnp.stack([ends_keep, ends_other]), jnp.stack([ends_other, ends_keep]))

    def home(zero, one):
        mine = jnp.where(lower, zero, one)
        other = swap(jnp.where(lower, one, zero))
        return (jnp.where(lower, mine, other), jnp.where(lower, other, mine))

    def halves(low, high, axis):
        return jnp.concatenate([low, high], axis=axis).astype(jnp.float32)

    def pair_home(block):
        size = block.shape[1] // 2
        other = swap(block)
        low = jnp.where(lower, block, other)
        high = jnp.where(lower, other, block)
        return jnp.stack(
            [halves(low[:, :size], high[:, :size], 1), halves(low[:, size:], high[:, size:], 1)], axis=1
        )

    last = grads_zero[1]
    early = grads_one[1]
    both = 2 * channels
    gap = last.shape[1] - both - WIDE
    own = jnp.concatenate(
        [early[:, :both], jnp.zeros((early.shape[0], gap), early.dtype), early[:, early.shape[1] - WIDE :]],
        axis=1,
    )
    away = swap(own)

    def unpack(block):
        wide = block[:, main:]
        (gate, upper), (gate_rest, upper_rest) = gates(wide, units)
        empty = jnp.zeros((block.shape[0], tail), block.dtype)
        down = jnp.concatenate([block[:, :main], wide[:, 2 * units :], empty], axis=1)
        return (
            jnp.concatenate([gate, gate_rest], axis=1),
            jnp.concatenate([upper, upper_rest], axis=1),
            down,
        )

    low, high = home(grads_zero[0], grads_one[0])
    low, high = unpack(low), unpack(high)
    gate_up_grad = jnp.stack([halves(low[0], high[0], 1), halves(low[1], high[1], 1)], axis=1)
    down_grad = by_rows(halves(low[2], high[2], 1))
    win_grad = by_rows(pair_home(early[:, both : early.shape[1] - WIDE]))
    gate_up_grad = by_rows(gate_up_grad)
    low, high = jnp.where(lower, own, away), jnp.where(lower, away, own)
    gain_sums, taps_sums = by_rows(sums[:, :2]), by_rows(sums[:, 2:])
    last, low, high, gate_up_grad, down_grad, win_grad, ends, gain_sums, taps_sums = lax.optimization_barrier(
        (last, low, high, gate_up_grad, down_grad, win_grad, ends, gain_sums, taps_sums)
    )
    vgate_grad, out_grad, pair_grad, down_grad = end_call(
        channels, tail, gap, core, last, swap(last), low, high, down_grad
    )
    return (
        ends[None],
        gain_sums,
        taps_sums,
        jnp.transpose(pair_grad, (2, 0, 1)),
        win_grad,
        vgate_grad[None],
        out_grad[None],
        gate_up_grad[None],
        down_grad.T[None],
    )


def solution(mesh):
    in_specs = (
        P("section", "dp", "tensor", None),
        P("dp"),
        P("section", None, None),
        P("section", None, None),
        P("dp", None, "tensor"),
        P("dp", None, "tensor"),
        P("section", "dp", None, "tensor"),
        P("section", "tensor", "dp"),
        P("section", "dp", None, "tensor"),
        P("section", "tensor", "dp"),
    )
    out_specs = (
        P("section", "dp", "tensor", None),
        P("section", None, None),
        P("section", None, None),
        P("dp", None, "tensor"),
        P("dp", None, "tensor"),
        P("section", "dp", None, "tensor"),
        P("section", "tensor", "dp"),
        P("section", "dp", None, "tensor"),
        P("section", "tensor", "dp"),
    )
    return jax.shard_map(body, mesh=mesh, in_specs=in_specs, out_specs=out_specs, check_vma=False)
```

```python
import functools
import math

import jax
import jax.numpy as jnp
from jax import lax
from jax.experimental import pallas as pl
from jax.experimental.layout import Layout, with_layout_constraint
from jax.experimental.pallas import tpu as pltpu
from jax.sharding import PartitionSpec as P

WIN = 64
HD = 112
LANES = 128
WIDE = 256
SUBLANES = 8
CHUNKS = 2

EPS = 1e-06


def silu_slope(value):
    sigma = jax.nn.sigmoid(value)
    return sigma * (1.0 + value * (1.0 - sigma))


def rms_rows(rows, gain):
    scale = lax.rsqrt(jnp.mean(rows * rows, axis=-1, keepdims=True) + EPS)
    return (scale, rows * scale * gain)


def rms_back(rows, scale, gain, grad):
    normal = rows * scale
    weighted = grad * gain
    inner = jnp.mean(weighted * normal, axis=-1, keepdims=True)
    return (scale * (weighted - normal * inner), jnp.sum(grad * normal, axis=0))


def swap(block):
    return lax.ppermute(block, "section", [(0, 1), (1, 0)])


def spread_pair(rows):
    mine = lax.all_gather(rows.astype(jnp.bfloat16), "tensor", axis=0, tiled=True)
    return (mine, swap(mine))


def spread(rows):
    return jnp.concatenate(spread_pair(rows), axis=0)


def collect(terms):
    length = terms.shape[0] // 2
    return collect_pair(terms[:length], terms[length:].astype(jnp.bfloat16))


def collect_pair(mine, other):
    size = lax.axis_size("tensor")
    count = mine.shape[0] // size
    index = lax.axis_index("tensor")
    part = mine + swap(other).astype(jnp.float32)
    low = part.astype(jnp.bfloat16)
    total = lax.dynamic_slice_in_dim(part, index * count, count, 0)
    for offset in range(1, size):
        block = lax.dynamic_slice_in_dim(low, (index ^ offset) * count, count, 0)
        pairs = [(i, i ^ offset) for i in range(size)]
        total = total + lax.ppermute(block, "tensor", pairs).astype(jnp.float32)
    return total


def ring_step(piece):
    size = lax.axis_size("dp")
    return lax.ppermute(piece, "dp", [(i, (i + 1) % size) for i in range(size)])


def ring_gather(piece, moved=None):
    size = lax.axis_size("dp")
    index = lax.axis_index("dp")
    count = piece.shape[0]
    full = jnp.zeros((size * count, piece.shape[1]), piece.dtype)
    for step in range(size):
        if step == 1 and moved is not None:
            piece = moved
        elif step:
            piece = ring_step(piece)
        full = lax.dynamic_update_slice_in_dim(full, piece, (index - step) % size * count, 0)
    return full


def sum_all(block):
    for axis in ("section", "tensor", "dp"):
        size = lax.axis_size(axis)
        step = 1
        while step < size:
            pairs = [(i, i ^ step) for i in range(size)]
            block = block + lax.ppermute(block, axis, pairs)
            step *= 2
    return block


def dot(one, two):
    return jnp.dot(one, two, preferred_element_type=jnp.float32)


def dot_nt(one, two):
    return lax.dot_general(one, two, (((1,), (1,)), ((), ())), preferred_element_type=jnp.float32)


def dot_tn(one, two):
    return lax.dot_general(one, two, (((0,), (0,)), ((), ())), preferred_element_type=jnp.float32)


def gates(halves, units):
    main = units // LANES * LANES
    stop = main + units
    return (
        (halves[:, :main], halves[:, main : 2 * main]),
        (halves[:, 2 * main : stop], halves[:, stop : 2 * units]),
    )


def lanes(block):
    return lax.broadcasted_iota(jnp.int32, block.shape, 1)


def forward_kernel(units, tail, near_ref, far_ref, feed_ref, last_ref, mine_ref, other_ref, rows_ref, inner_ref):
    main = units // LANES * LANES
    over = units - main
    length = near_ref.shape[0]
    rows_ref[:length] = near_ref[...]
    rows_ref[length:] = far_ref[...]
    rows = rows_ref[...]
    for start in range(0, main, WIDE):
        gate = dot(rows, feed_ref[:, pl.ds(main + start, WIDE)])
        upper = dot(rows, feed_ref[:, pl.ds(2 * main + start, WIDE)])
        inner_ref[:, pl.ds(start, WIDE)] = (jax.nn.silu(gate) * upper).astype(jnp.bfloat16)
    ends = feed_ref[:, pl.ds(3 * main, WIDE)]
    both = dot(rows, ends)
    upper = pltpu.roll(both, WIDE - over, 1)
    inner = jax.nn.silu(both[:, :LANES]) * upper[:, :LANES]
    inner = jnp.where(lanes(inner) < over, inner, 0.0)
    low = pltpu.roll(jnp.concatenate([inner, jnp.zeros_like(inner)], axis=1), 2 * over, 1)
    low = jnp.where(lanes(low) < 2 * over, 0.0, low).astype(jnp.bfloat16)
    high = pltpu.roll(inner, LANES - over, 1)
    high = jnp.where(lanes(high) < LANES - tail, 0.0, high).astype(jnp.bfloat16)
    terms = dot_nt(inner_ref[...], feed_ref[:, pl.ds(0, main)]) + dot_nt(low, ends) + dot_nt(high, last_ref[...])
    mine_ref[...] = terms[:length]
    other_ref[...] = terms[length:].astype(jnp.bfloat16)


def feed_terms(units, tail, near, far, feed, attn):
    length, model = near.shape
    main = units // LANES * LANES
    width = 3 * units - tail
    end = attn.shape[1] // LANES - 1

    def whole(shape):
        return pl.BlockSpec(shape, lambda step: (0, 0), pipeline_mode=pl.Buffered(1))

    return pl.pallas_call(
        functools.partial(forward_kernel, units, tail),
        grid=(1,),
        out_shape=[
            jax.ShapeDtypeStruct((length, model), jnp.float32),
            jax.ShapeDtypeStruct((length, model), jnp.bfloat16),
        ],
        in_specs=[
            whole((length, model)),
            whole((length, model)),
            whole((model, width)),
            pl.BlockSpec((model, LANES), lambda step: (0, end)),
        ],
        out_specs=[whole((length, model))] * 2,
        scratch_shapes=[
            pltpu.VMEM((2 * length, model), jnp.bfloat16),
            pltpu.VMEM((2 * length, main), jnp.bfloat16),
        ],
        compiler_params=pltpu.CompilerParams(vmem_limit_bytes=48 * 2**20),
        cost_estimate=pl.CostEstimate(flops=2**20, bytes_accessed=2**16, transcendentals=0),
    )(near, far, feed, attn)


def feed_kernel(
    units, tail, near_ref, far_ref, near_grad_ref, far_grad_ref, feed_ref, last_ref, *refs
):
    extras, refs = refs[:-8], refs[-8:]
    block_ref, rest_ref, halves_ref, inner_ref, rows_ref, grads_ref, wide_ref, down_ref = refs
    main = units // LANES * LANES
    over = units - main
    step = pl.program_id(0)
    length = near_ref.shape[0]
    size = feed_ref.shape[0]
    chunks = rows_ref.shape[1] // size

    def parts(gate, upper, grad):
        sigma = jax.nn.sigmoid(gate)
        act = gate * sigma
        slope = sigma * (1.0 + gate * (1.0 - sigma))
        return (act * upper, grad * upper * slope, grad * act)

    @pl.when(step == 0)
    def _():
        rows_ref[:length] = near_ref[...]
        rows_ref[length:] = far_ref[...]
        grads_ref[:length] = near_grad_ref[...]
        grads_ref[length:] = far_grad_ref[...]

    for chunk in range(chunks):
        place = pl.ds(chunk * size, size)

        @pl.when(step == chunk)
        def _(chunk=chunk, place=place):
            rows, branch = rows_ref[:, place], grads_ref[:, place]
            wide = dot(rows, feed_ref[:, pl.ds(main, 2 * main + WIDE)])
            down = dot(branch, feed_ref[:, pl.ds(0, main)])
            ends = dot(branch, feed_ref[:, pl.ds(3 * main, WIDE)])
            if chunk:
                wide = wide + wide_ref[...]
                down = down + down_ref[:, pl.ds(0, main)]
                ends = ends + down_ref[:, pl.ds(main, WIDE)]
            if chunk < chunks - 1:
                wide_ref[...] = wide
                down_ref[:, pl.ds(0, main)] = down
                down_ref[:, pl.ds(main, WIDE)] = ends
                return
            inner, grad_gate, grad_upper = (
                part.astype(jnp.bfloat16) for part in parts(wide[:, :main], wide[:, main : 2 * main], down)
            )
            inner_ref[:, pl.ds(0, main)] = inner
            halves_ref[:, pl.ds(0, main)] = grad_gate
            halves_ref[:, pl.ds(main, main)] = grad_upper
            both = wide[:, 2 * main :]
            upper = pltpu.roll(both, WIDE - over, 1)
            grad = pltpu.roll(ends, WIDE - 2 * over, 1)[:, :LANES]
            more = pltpu.roll(dot(grads_ref[...], last_ref[...]), over, 1)
            grad = jnp.where(lanes(grad) < over - tail, grad, more)
            inner, grad_gate, grad_upper = (
                jnp.where(lanes(part) < over, part, 0.0)
                for part in parts(both[:, :LANES], upper[:, :LANES], grad)
            )
            inner_ref[:, pl.ds(main, LANES)] = inner.astype(jnp.bfloat16)
            empty = jnp.zeros_like(grad_gate)
            last = jnp.concatenate([grad_gate, empty], axis=1)
            last = last + pltpu.roll(jnp.concatenate([grad_upper, empty], axis=1), over, 1)
            halves_ref[:, pl.ds(2 * main, WIDE)] = last.astype(jnp.bfloat16)

        @pl.when(step == chunks + chunk)
        def _(place=place):
            base = 0
            for extra in extras:
                block_ref[:, pl.ds(base, extra.shape[1])] = extra[...]
                base += extra.shape[1]
            rows, branch = rows_ref[:, place], grads_ref[:, place]
            down = dot_tn(branch, inner_ref[:, pl.ds(0, main)])
            block_ref[:, pl.ds(base, main)] = down.astype(jnp.bfloat16)
            wide = dot_tn(rows, halves_ref[:, pl.ds(0, 2 * main)])
            block_ref[:, pl.ds(base + main, 2 * main)] = wide.astype(jnp.bfloat16)
            down = dot_tn(branch, inner_ref[:, pl.ds(main, LANES)])
            down = jnp.concatenate([down, jnp.zeros_like(down)], axis=1)
            wide = dot_tn(rows, halves_ref[:, pl.ds(2 * main, WIDE)])
            wide = jnp.where(lanes(wide) < 2 * over, wide, pltpu.roll(down, 2 * over, 1))
            block_ref[:, pl.ds(base + 3 * main, WIDE)] = wide.astype(jnp.bfloat16)
            moved = pltpu.roll(down, WIDE - over, 1)
            rest_ref[...] = jnp.where(lanes(moved) < WIDE - tail, 0.0, moved).astype(jnp.bfloat16)


def feed_both(units, tail, near, far, near_grad, far_grad, feed, attn, *extras):
    count, model = 2 * near.shape[0], near.shape[1]
    main = units // LANES * LANES
    width = 3 * units - tail
    size = model // CHUNKS
    total = width + sum(extra.shape[1] for extra in extras)
    shapes = ((model, total), (model, WIDE), (count, width - main), (count, main + LANES))
    end = attn.shape[1] // LANES - 1

    def later(columns):
        return pl.BlockSpec((size, columns), lambda step: (jnp.maximum(step - CHUNKS, 0), 0))

    def whole(shape):
        return pl.BlockSpec(shape, lambda step: (0, 0), pipeline_mode=pl.Buffered(1))

    return pl.pallas_call(
        functools.partial(feed_kernel, units, tail),
        grid=(2 * CHUNKS,),
        out_shape=[jax.ShapeDtypeStruct(shape, jnp.bfloat16) for shape in shapes],
        in_specs=[whole(near.shape)] * 4
        + [
            pl.BlockSpec((size, width), lambda step: (jnp.minimum(step, CHUNKS - 1), 0)),
            pl.BlockSpec((model, LANES), lambda step: (0, end), pipeline_mode=pl.Buffered(1)),
        ]
        + [later(extra.shape[1]) for extra in extras],
        out_specs=[later(total), later(WIDE), whole(shapes[2]), whole(shapes[3])],
        scratch_shapes=[
            pltpu.VMEM((count, model), jnp.bfloat16),
            pltpu.VMEM((count, model), jnp.bfloat16),
            pltpu.VMEM((count, width - main), jnp.float32),
            pltpu.VMEM((count, main + WIDE), jnp.float32),
        ],
        compiler_params=pltpu.CompilerParams(vmem_limit_bytes=56 * 2**20),
        cost_estimate=pl.CostEstimate(
            flops=4 * count * model * width,
            bytes_accessed=20 * 2**20,
            transcendentals=count * units,
        ),
    )(near, far, near_grad, far_grad, feed, attn, *extras)


def take(block, column, width):
    base = column // LANES * LANES
    shift = column - base
    stop = base + -(-(shift + width) // LANES) * LANES
    part = block[:, base:stop]
    if shift:
        part = pltpu.roll(part, stop - base - shift, 1)
    part = part[:, : -(-width // LANES) * LANES]
    return jnp.where(lanes(part) < width, part, 0.0)


def put(target, rows, column, width, part):
    base = column // LANES * LANES
    shift = column - base
    size = -(-(shift + width) // LANES) * LANES
    if size > part.shape[1]:
        empty = jnp.zeros((part.shape[0], size - part.shape[1]), part.dtype)
        part = jnp.concatenate([part, empty], axis=1)
    if shift:
        part = pltpu.roll(part, shift, 1)
    target[rows, pl.ds(base, size)] += part


def moved(block, distance):
    count = block.shape[0]
    if distance == 0:
        return block
    row = lax.broadcasted_iota(jnp.int32, block.shape, 0)
    rolled = pltpu.roll(block, distance % count, 0)
    inside = row >= distance if distance > 0 else row < count + distance
    return jnp.where(inside, rolled, 0.0)


def mixer_parts(both, taps, channels, first):
    length = both.shape[0]
    heads = channels // HD
    width = (both.shape[1] - 2 * channels) // (2 * heads)
    pre_values = take(both, 0, channels)
    values = sum(moved(pre_values, tap) * taps[tap : tap + 1] for tap in range(3))
    values = values.astype(jnp.bfloat16).astype(jnp.float32)
    gate = take(both, channels, channels)
    query = lax.broadcasted_iota(jnp.int32, (length, length), 0)
    key = lax.broadcasted_iota(jnp.int32, (length, length), 1)
    allowed = key <= query
    if not first:
        allowed = allowed & (query - key < WIN)
    parts = []
    for head in range(heads):
        queries = take(both, 2 * channels + head * width, width).astype(jnp.bfloat16)
        keys = take(both, 2 * channels + (heads + head) * width, width).astype(jnp.bfloat16)
        scores = dot_nt(queries, keys) / math.sqrt(width)
        if first:
            kernel = jnp.where(allowed, 1.0 + scores + 0.5 * scores * scores, 0.0)
            total = jnp.sum(kernel, axis=-1, keepdims=True)
            probs = kernel / total
            slope = jnp.where(allowed, (1.0 + scores) / total, 0.0)
        else:
            scores = jnp.where(allowed, scores, -1e30)
            kernel = jnp.exp(scores - jnp.max(scores, axis=-1, keepdims=True))
            probs = kernel / jnp.sum(kernel, axis=-1, keepdims=True)
            slope = probs
        own = take(values, head * HD, HD).astype(jnp.bfloat16)
        parts.append((queries, keys, probs, slope, own, dot(probs.astype(jnp.bfloat16), own)))
    return (pre_values, gate, parts)


def join(parts):
    empty = jnp.zeros_like(parts[0])
    total = 0.0
    for head, part in enumerate(parts):
        part = jnp.concatenate([part, empty], axis=1)
        total = total + (pltpu.roll(part, head * HD, 1) if head else part)
    return total


def mixer_kernel(
    channels, first, near_ref, far_ref, attn_ref, taps_ref, mine_ref, other_ref, both_ref, gated_ref
):
    length = near_ref.shape[0]
    stop = both_ref.shape[1]
    for index, rows in enumerate((near_ref, far_ref)):
        both = dot(rows[...], attn_ref[:, pl.ds(0, stop)])
        both_ref[pl.ds(index * length, length), :] = both
        _, gate, parts = mixer_parts(both, taps_ref[...], channels, first)
        gated = (join([part[-1] for part in parts]) * gate * jax.nn.sigmoid(gate)).astype(jnp.bfloat16)
        gated_ref[pl.ds(index * length, length), :] = gated
        terms = dot_nt(gated, attn_ref[:, pl.ds(stop, WIDE)])
        if index == 0:
            mine_ref[...] = terms
        else:
            other_ref[...] = terms.astype(jnp.bfloat16)


def mixer_back_kernel(
    channels, first, near_ref, far_ref, near_grad_ref, far_grad_ref, attn_ref, taps_ref, both_ref,
    gated_ref, rest_ref, block_ref, mine_ref, other_ref, taps_grad_ref, rows_ref, grads_ref, sums_ref, low_ref,
):
    length = near_ref.shape[0]
    stop = both_ref.shape[1]
    heads = channels // HD
    width = (stop - 2 * channels) // (2 * heads)
    taps = taps_ref[...]
    sums_ref[...] = jnp.zeros_like(sums_ref)
    taps_grad = [0.0] * 3
    rows_ref[:length] = near_ref[...]
    rows_ref[length:] = far_ref[...]
    grads_ref[:length] = near_grad_ref[...]
    grads_ref[length:] = far_grad_ref[...]
    for index in range(2):
        rows = pl.ds(index * length, length)
        pre_values, gate, parts = mixer_parts(both_ref[rows, :], taps, channels, first)
        mixed = join([part[-1] for part in parts])
        grad = dot(grads_ref[rows, :], attn_ref[:, pl.ds(stop, WIDE)])
        grad = jnp.where(lanes(grad) < channels, grad, 0.0)
        sigma = jax.nn.sigmoid(gate)
        grad_mixed = (grad * (gate * sigma)).astype(jnp.bfloat16).astype(jnp.float32)
        grad_gate = (grad * mixed * silu_slope(gate)).astype(jnp.bfloat16).astype(jnp.float32)
        put(sums_ref, rows, channels, channels, grad_gate)
        grad_values = []
        for head, (queries, keys, probs, slope, own, _) in enumerate(parts):
            part = take(grad_mixed, head * HD, HD).astype(jnp.bfloat16)
            grad_values.append(dot_tn(probs.astype(jnp.bfloat16), part))
            grad_probs = dot_nt(part, own)
            centred = grad_probs - jnp.sum(probs * grad_probs, axis=-1, keepdims=True)
            score_grad = (centred * slope).astype(jnp.bfloat16)
            for place, value in (
                (head, dot(score_grad, keys)),
                (heads + head, dot_tn(score_grad, queries)),
            ):
                value = (value / math.sqrt(width)).astype(jnp.bfloat16).astype(jnp.float32)
                put(sums_ref, rows, 2 * channels + place * width, width, value)
        grad_values = join(grad_values)
        grad_pre = sum(moved(grad_values, -tap) * taps[tap : tap + 1] for tap in range(3))
        put(sums_ref, rows, 0, channels, grad_pre.astype(jnp.bfloat16).astype(jnp.float32))
        for tap in range(3):
            taps_grad[tap] = taps_grad[tap] + jnp.sum(
                grad_values * moved(pre_values, tap), axis=0, keepdims=True
            )
    for tap in range(3):
        taps_grad_ref[pl.ds(tap, 1), :] = taps_grad[tap]
    low_ref[...] = sums_ref[...].astype(jnp.bfloat16)
    for column in range(0, stop, LANES):
        size = min(WIDE, stop - column)
        if column % WIDE:
            continue
        place = pl.ds(column, size)
        block_ref[:, place] = dot_tn(rows_ref[...], low_ref[:, place]).astype(jnp.bfloat16)
    last = dot_tn(grads_ref[...], gated_ref[...]).astype(jnp.bfloat16)
    block_ref[:, pl.ds(stop, WIDE)] = last + rest_ref[...]
    for index in range(2):
        terms = dot_nt(low_ref[pl.ds(index * length, length), :], attn_ref[:, pl.ds(0, stop)])
        if index == 0:
            mine_ref[...] = terms
        else:
            other_ref[...] = terms.astype(jnp.bfloat16)


def whole_call(kernel, inputs, shapes, scratch, flops):
    def whole(shape):
        return pl.BlockSpec(shape, lambda step: (0,) * len(shape), pipeline_mode=pl.Buffered(1))

    return pl.pallas_call(
        kernel,
        grid=(1,),
        out_shape=[jax.ShapeDtypeStruct(shape, kind) for shape, kind in shapes],
        in_specs=[whole(block.shape) for block in inputs],
        out_specs=[whole(shape) for shape, _ in shapes],
        scratch_shapes=[pltpu.VMEM(shape, kind) for shape, kind in scratch],
        compiler_params=pltpu.CompilerParams(vmem_limit_bytes=56 * 2**20),
        cost_estimate=pl.CostEstimate(flops=flops, bytes_accessed=2**16, transcendentals=0),
    )(*inputs)


def mixer_forward(channels, first, near, far, attn, taps):
    length, model = near.shape
    stop = attn.shape[1] - WIDE
    shapes = (
        ((length, model), jnp.float32),
        ((length, model), jnp.bfloat16),
        ((2 * length, stop), jnp.float32),
        ((2 * length, WIDE), jnp.bfloat16),
    )
    kernel = functools.partial(mixer_kernel, channels, first)
    return whole_call(kernel, (near, far, attn, taps), shapes, (), 2**20)


def mixer_backward(channels, first, near, far, near_grad, far_grad, attn, taps, both, gated, rest):
    length, model = near.shape
    stop = both.shape[1]
    shapes = (
        ((model, stop + WIDE), jnp.bfloat16),
        ((length, model), jnp.float32),
        ((length, model), jnp.bfloat16),
        (taps.shape, jnp.float32),
    )
    scratch = (
        ((2 * length, model), jnp.bfloat16),
        ((2 * length, model), jnp.bfloat16),
        ((2 * length, stop), jnp.float32),
        ((2 * length, stop), jnp.bfloat16),
    )
    inputs = (near, far, near_grad, far_grad, attn, taps, both, gated, rest)
    return whole_call(functools.partial(mixer_back_kernel, channels, first), inputs, shapes, scratch, 2**20)


def end_kernel(
    channels, units, tail, core_ref, mine_ref, other_ref, low_ref, high_ref, kept_ref,
    vgate_ref, out_ref, pair_ref, down_ref,
):
    step = pl.program_id(0)
    lower = core_ref[0] == 0
    mine, other = (ref[...].astype(jnp.float32) for ref in (mine_ref, other_ref))
    low = jnp.where(lower, mine, low_ref[...].astype(jnp.float32))
    high = jnp.where(lower, other, high_ref[...].astype(jnp.float32))
    size = mine.shape[1]
    wide = pair_ref.shape[1] // 2

    @pl.when(step == 0)
    def _():
        for place in range(2):
            parts = [take(block, place * channels, channels) for block in (low, high)]
            empty = jnp.zeros_like(parts[0])
            first = jnp.concatenate([parts[0], empty], axis=1)
            second = pltpu.roll(jnp.concatenate([parts[1], empty], axis=1), channels, 1)
            vgate_ref[:, place, :] = (first + second)[:, : 2 * channels]
        for place, block in enumerate((low, high)):
            turned = jnp.swapaxes(block[:, size - WIDE :], 0, 1)
            out_ref[pl.ds(place * channels, channels), :] = turned[:channels]
        for place, block in enumerate((jnp.where(lower, mine, other), jnp.where(lower, other, mine))):
            turned = jnp.swapaxes(block[:, size - WIDE - LANES : size - WIDE], 0, 1)
            for half in range(2):
                start = LANES - (2 - half) * wide
                pair_ref[half, pl.ds(place * wide, wide), :] = turned[start : start + wide]

    for place, block in enumerate((low, high)):

        @pl.when(step == place)
        def _(place=place, block=block):
            stop = units * (place + 1) % LANES or LANES
            last = block[:, size - LANES :]
            if stop < LANES:
                last = pltpu.roll(last, stop, 1)
            column = lanes(last)
            inside = (column >= stop - tail) & (column < stop)
            down_ref[...] = jnp.where(inside, last, kept_ref[...])


def end_call(channels, tail, width, core, mine, other, low, high, down):
    count, size = mine.shape
    units = down.shape[1] // 2
    first, second = (units - 1) // LANES, (2 * units - 1) // LANES

    def whole(shape):
        return pl.BlockSpec(shape, lambda step: (0,) * len(shape))

    tile = pl.BlockSpec((count, LANES), lambda step: (0, first + step * (second - first)))
    shapes = ((count, 2, 2 * channels), (2 * channels, count), (2, width, count))
    return pl.pallas_call(
        functools.partial(end_kernel, channels, units, tail),
        grid=(2,),
        out_shape=[jax.ShapeDtypeStruct(shape, jnp.float32) for shape in (*shapes, down.shape)],
        in_specs=[pl.BlockSpec(memory_space=pltpu.SMEM)]
        + [whole((count, size))] * 4
        + [tile],
        out_specs=[whole(shape) for shape in shapes] + [tile],
        input_output_aliases={5: 3},
        compiler_params=pltpu.CompilerParams(vmem_limit_bytes=48 * 2**20),
        cost_estimate=pl.CostEstimate(flops=2**20, bytes_accessed=2**27, transcendentals=0),
    )(core.reshape(1), mine, other, low, high, down)


def by_rows(block):
    return with_layout_constraint(block, Layout(major_to_minor=tuple(range(block.ndim))))


class Queue:
    def __init__(self):
        self.done = []

    def scatter(self, *grads):
        block = by_rows(jnp.concatenate(grads, axis=1) if len(grads) > 1 else grads[0])
        if self.done:
            block, self.done[-1] = lax.optimization_barrier((block, self.done[-1]))
        self.done.append(by_rows(lax.psum_scatter(block, "dp", scatter_dimension=0, tiled=True)))


def body(
    boundary, lengths, norm_gains, conv_taps, lin_qk, win_qk, value_gate, out_weight, gate_up, down_weight
):
    core = lax.axis_index("section")
    index = lax.axis_index("tensor")
    lower = core == 0
    rows_dev, model = boundary.shape[2:]
    channels = value_gate.shape[-1] // 2
    units = gate_up.shape[-1] // 2
    main = units // LANES * LANES
    tail = -(3 * channels + lin_qk.shape[-1]) % LANES

    def half(block, axis, which):
        size = block.shape[axis] // 2
        return lax.dynamic_slice_in_dim(block, which * size, size, axis)

    def both_layers(build):
        mine = build(core)
        other = swap(build(1 - core))
        return (jnp.where(lower, mine, other), jnp.where(lower, other, mine))

    def attn_piece(pair, which):
        own = slice(which * channels, (which + 1) * channels)
        wide = pair.shape[2] // 2
        pair = pair[:, :, which * wide : (which + 1) * wide]
        last = down_weight[0][(which + 1) * units - tail : (which + 1) * units]
        values = value_gate[0][:, :, own]
        parts = [values[:, 0], values[:, 1], pair[:, 0], pair[:, 1], out_weight[0][own].T, last.T]
        return jnp.concatenate(parts, axis=1)

    def feed_piece(which):
        pair = half(gate_up[0], 2, which)
        down = half(down_weight[0], 0, which).T
        return jnp.concatenate(
            [down[:, :main], pair[:, 0, :main], pair[:, 1, :main], pair[:, 0, main:], pair[:, 1, main:], down[:, main : units - tail]],
            axis=1,
        )

    def fetch(piece):
        return lax.all_gather(piece, "dp", axis=0, tiled=True)

    attn_zero = fetch(jnp.where(lower, attn_piece(lin_qk, 0), swap(attn_piece(lin_qk, 1))))
    feed_parts = both_layers(feed_piece)
    split = feed_parts[0].shape[1]
    edge = split - WIDE
    most = fetch(feed_parts[0][:, :edge])
    attn_one = jnp.where(lower, swap(attn_piece(win_qk, 0)), attn_piece(win_qk, 1))
    piece = jnp.concatenate([attn_one, feed_parts[0][:, edge:]], axis=1)
    attn_zero, moved = lax.optimization_barrier((attn_zero, ring_step(piece)))
    ring = ring_gather(piece, moved)
    wide = attn_one.shape[1]
    feed_one = fetch(feed_parts[1])

    small = jnp.concatenate([norm_gains[0], conv_taps[0]], axis=0)
    small_other = swap(small)
    small_zero = jnp.where(lower, small, small_other)
    small_one = jnp.where(lower, small_other, small)
    offset = (2 * index + core) * channels

    def own_taps(block):
        own = lax.dynamic_slice_in_dim(block[2:], offset, channels, 1)
        return jnp.pad(own, ((0, -own.shape[0] % SUBLANES), (0, WIDE - channels)))

    held = boundary[0]
    keep = lax.dynamic_index_in_dim(held, core, 0, keepdims=False)
    other = swap(lax.dynamic_index_in_dim(held, 1 - core, 0, keepdims=False))
    entering = jnp.where(lower, keep, other).astype(jnp.float32)
    cotangent = jnp.where(lower, other, keep).astype(jnp.float32)
    length = lax.dynamic_index_in_dim(lengths, core, 0, keepdims=False)
    place = index * rows_dev + jnp.arange(rows_dev)
    mask = (place < length).astype(jnp.float32)[:, None]

    queue = Queue()
    gains_zero, gains_one = small_zero[:2], small_one[:2]
    taps_zero, taps_one = own_taps(small_zero), own_taps(small_one)

    def mix(rows, gain, attn, taps, first):
        scale, normed = rms_rows(rows, gain)
        near, far = spread_pair(normed)
        mine, other, both, gated = mixer_forward(channels, first, near, far, attn, taps)
        return (rows + collect_pair(mine, other), (rows, scale, near, far, both, gated))

    def mix_back(kept, grad_out, gain, attn, taps, rest, first):
        rows, scale, near, far, both, gated = kept
        block, mine, other, grad_taps = mixer_backward(
            channels, first, near, far, *spread_pair(grad_out), attn, taps, both, gated, rest
        )
        back, grad_gain = rms_back(rows, scale, gain, collect_pair(mine, other))
        return (block, grad_out + back, grad_gain, grad_taps[: conv_taps.shape[1], :channels])

    hidden, kept_zero = mix(entering, gains_zero[0], attn_zero, taps_zero, True)
    scale, normed = rms_rows(hidden, gains_zero[1])
    near, far = spread_pair(normed)
    grad_out = cotangent * mask
    near, far, ring, *grads_one = lax.optimization_barrier((near, far, ring, *spread_pair(grad_out)))
    packed = jnp.concatenate([most, ring[:, wide:]], axis=1)
    kept_feed = (hidden, scale, near, far)
    mine, other = feed_terms(units, tail, near, far, packed, attn_zero)
    other, ring = lax.optimization_barrier((other, ring))
    attn_one = ring[:, :wide]
    down_one = jnp.concatenate(
        [feed_one[:, :main], feed_one[:, main + 2 * units :], attn_one[:, attn_one.shape[1] - tail :]], axis=1
    )
    middle = hidden + collect_pair(mine, other)
    middle = middle.astype(jnp.bfloat16).astype(jnp.float32)

    hidden, kept_one = mix(middle, gains_one[0], attn_one, taps_one, False)
    scale, normed = rms_rows(hidden, gains_one[1])
    block, rest, grad_halves, inner = feed_both(
        units, tail, *spread_pair(normed), *grads_one, feed_one, attn_one
    )
    queue.scatter(block)
    final = hidden + collect(dot_nt(inner[:, :units], down_one))
    back, gain_two = rms_back(hidden, scale, gains_one[1], collect(dot_nt(grad_halves, feed_one[:, main:])))
    attn_grads, grad_middle, gain_one, taps_one = mix_back(
        kept_one, grad_out + back, gains_one[0], attn_one, taps_one, rest, False
    )
    gains_one = jnp.stack([gain_one, gain_two])

    grad_middle = grad_middle.astype(jnp.bfloat16).astype(jnp.float32)
    hidden, scale, near, far = kept_feed
    block, rest, grad_halves, _ = feed_both(
        units, tail, near, far, *spread_pair(grad_middle), packed, attn_zero, attn_grads
    )
    queue.scatter(block)
    terms = dot_nt(grad_halves, packed[:, main:split])
    back, gain_two = rms_back(hidden, scale, gains_zero[1], collect(terms))
    attn_grads, grad_start, gain_one, taps_zero = mix_back(
        kept_zero, grad_middle + back, gains_zero[0], attn_zero, taps_zero, rest, True
    )
    queue.scatter(attn_grads)
    gains_zero = jnp.stack([gain_one, gain_two])

    edge = attn_one.shape[1]
    grads_one = (queue.done[0], queue.done[1][:, :edge])
    grads_zero = (queue.done[1][:, edge:], queue.done[2])

    def own_small(gains, taps):
        spot = jnp.zeros((taps.shape[0], model), jnp.float32)
        return jnp.concatenate([gains, lax.dynamic_update_slice_in_dim(spot, taps, offset, 1)], axis=0)

    sums = sum_all(jnp.stack([own_small(gains_zero, taps_zero), own_small(gains_one, taps_one)]))
    sums = lax.dynamic_index_in_dim(sums, core, 0, keepdims=True)

    final = final * mask
    ends_keep = jnp.where(lower, grad_start, final)
    ends_other = swap(jnp.where(lower, final, grad_start))
    ends = jnp.where(lower, jnp.stack([ends_keep, ends_other]), jnp.stack([ends_other, ends_keep]))

    def home(zero, one):
        mine = jnp.where(lower, zero, one)
        other = swap(jnp.where(lower, one, zero))
        return (jnp.where(lower, mine, other), jnp.where(lower, other, mine))

    def halves(low, high, axis):
        return jnp.concatenate([low, high], axis=axis).astype(jnp.float32)

    def pair_home(block):
        size = block.shape[1] // 2
        other = swap(block)
        low = jnp.where(lower, block, other)
        high = jnp.where(lower, other, block)
        return jnp.stack(
            [halves(low[:, :size], high[:, :size], 1), halves(low[:, size:], high[:, size:], 1)], axis=1
        )

    last = grads_zero[1]
    early = grads_one[1]
    both = 2 * channels
    gap = last.shape[1] - both - WIDE
    own = jnp.concatenate(
        [early[:, :both], jnp.zeros((early.shape[0], gap), early.dtype), early[:, early.shape[1] - WIDE :]],
        axis=1,
    )
    away = swap(own)

    def unpack(block):
        wide = block[:, main:]
        (gate, upper), (gate_rest, upper_rest) = gates(wide, units)
        empty = jnp.zeros((block.shape[0], tail), block.dtype)
        down = jnp.concatenate([block[:, :main], wide[:, 2 * units :], empty], axis=1)
        return (
            jnp.concatenate([gate, gate_rest], axis=1),
            jnp.concatenate([upper, upper_rest], axis=1),
            down,
        )

    low, high = home(grads_zero[0], grads_one[0])
    low, high = unpack(low), unpack(high)
    gate_up_grad = jnp.stack([halves(low[0], high[0], 1), halves(low[1], high[1], 1)], axis=1)
    down_grad = by_rows(halves(low[2], high[2], 1))
    win_grad = by_rows(pair_home(early[:, both : early.shape[1] - WIDE]))
    gate_up_grad = by_rows(gate_up_grad)
    low, high = jnp.where(lower, own, away), jnp.where(lower, away, own)
    gain_sums, taps_sums = by_rows(sums[:, :2]), by_rows(sums[:, 2:])
    last, low, high, gate_up_grad, down_grad, win_grad, ends, gain_sums, taps_sums = lax.optimization_barrier(
        (last, low, high, gate_up_grad, down_grad, win_grad, ends, gain_sums, taps_sums)
    )
    vgate_grad, out_grad, pair_grad, down_grad = end_call(
        channels, tail, gap, core, last, swap(last), low, high, down_grad
    )
    return (
        ends[None],
        gain_sums,
        taps_sums,
        jnp.transpose(pair_grad, (2, 0, 1)),
        win_grad,
        vgate_grad[None],
        out_grad[None],
        gate_up_grad[None],
        down_grad.T[None],
    )


def solution(mesh):
    in_specs = (
        P("section", "dp", "tensor", None),
        P("dp"),
        P("section", None, None),
        P("section", None, None),
        P("dp", None, "tensor"),
        P("dp", None, "tensor"),
        P("section", "dp", None, "tensor"),
        P("section", "tensor", "dp"),
        P("section", "dp", None, "tensor"),
        P("section", "tensor", "dp"),
    )
    out_specs = (
        P("section", "dp", "tensor", None),
        P("section", None, None),
        P("section", None, None),
        P("dp", None, "tensor"),
        P("dp", None, "tensor"),
        P("section", "dp", None, "tensor"),
        P("section", "tensor", "dp"),
        P("section", "dp", None, "tensor"),
        P("section", "tensor", "dp"),
    )
    return jax.shard_map(body, mesh=mesh, in_specs=in_specs, out_specs=out_specs, check_vma=False)
```

```python
import functools
import math

import jax
import jax.numpy as jnp
from jax import lax
from jax.experimental import pallas as pl
from jax.experimental.layout import Layout, with_layout_constraint
from jax.experimental.pallas import tpu as pltpu
from jax.sharding import PartitionSpec as P

WIN = 64
HD = 112
LANES = 128
WIDE = 256
SUBLANES = 8
CHUNKS = 2

EPS = 1e-06


def silu_slope(value):
    sigma = jax.nn.sigmoid(value)
    return sigma * (1.0 + value * (1.0 - sigma))


def rms_rows(rows, gain):
    scale = lax.rsqrt(jnp.mean(rows * rows, axis=-1, keepdims=True) + EPS)
    return (scale, rows * scale * gain)


def rms_back(rows, scale, gain, grad):
    normal = rows * scale
    weighted = grad * gain
    inner = jnp.mean(weighted * normal, axis=-1, keepdims=True)
    return (scale * (weighted - normal * inner), jnp.sum(grad * normal, axis=0))


def swap(block):
    return lax.ppermute(block, "section", [(0, 1), (1, 0)])


def spread_pair(rows):
    mine = lax.all_gather(rows.astype(jnp.bfloat16), "tensor", axis=0, tiled=True)
    return (mine, swap(mine))


def spread(rows):
    return jnp.concatenate(spread_pair(rows), axis=0)


def collect(terms):
    length = terms.shape[0] // 2
    return collect_pair(terms[:length], terms[length:].astype(jnp.bfloat16))


def collect_pair(mine, other):
    size = lax.axis_size("tensor")
    count = mine.shape[0] // size
    index = lax.axis_index("tensor")
    part = mine + swap(other).astype(jnp.float32)
    low = part.astype(jnp.bfloat16)
    total = lax.dynamic_slice_in_dim(part, index * count, count, 0)
    for offset in range(1, size):
        block = lax.dynamic_slice_in_dim(low, (index ^ offset) * count, count, 0)
        pairs = [(i, i ^ offset) for i in range(size)]
        total = total + lax.ppermute(block, "tensor", pairs).astype(jnp.float32)
    return total


def ring_step(piece):
    size = lax.axis_size("dp")
    return lax.ppermute(piece, "dp", [(i, (i + 1) % size) for i in range(size)])


def ring_gather(piece, moved=None):
    size = lax.axis_size("dp")
    index = lax.axis_index("dp")
    count = piece.shape[0]
    full = jnp.zeros((size * count, piece.shape[1]), piece.dtype)
    for step in range(size):
        if step == 1 and moved is not None:
            piece = moved
        elif step:
            piece = ring_step(piece)
        full = lax.dynamic_update_slice_in_dim(full, piece, (index - step) % size * count, 0)
    return full


def sum_all(block):
    for axis in ("section", "tensor", "dp"):
        size = lax.axis_size(axis)
        step = 1
        while step < size:
            pairs = [(i, i ^ step) for i in range(size)]
            block = block + lax.ppermute(block, axis, pairs)
            step *= 2
    return block


def dot(one, two):
    return jnp.dot(one, two, preferred_element_type=jnp.float32)


def dot_nt(one, two):
    return lax.dot_general(one, two, (((1,), (1,)), ((), ())), preferred_element_type=jnp.float32)


def dot_tn(one, two):
    return lax.dot_general(one, two, (((0,), (0,)), ((), ())), preferred_element_type=jnp.float32)


def gates(halves, units):
    main = units // LANES * LANES
    stop = main + units
    return (
        (halves[:, :main], halves[:, main : 2 * main]),
        (halves[:, 2 * main : stop], halves[:, stop : 2 * units]),
    )


def lanes(block):
    return lax.broadcasted_iota(jnp.int32, block.shape, 1)


def forward_kernel(units, tail, near_ref, far_ref, feed_ref, last_ref, mine_ref, other_ref, rows_ref, inner_ref):
    main = units // LANES * LANES
    over = units - main
    length = near_ref.shape[0]
    rows_ref[:length] = near_ref[...]
    rows_ref[length:] = far_ref[...]
    rows = rows_ref[...]
    for start in range(0, main, WIDE):
        gate = dot(rows, feed_ref[:, pl.ds(main + start, WIDE)])
        upper = dot(rows, feed_ref[:, pl.ds(2 * main + start, WIDE)])
        inner_ref[:, pl.ds(start, WIDE)] = (jax.nn.silu(gate) * upper).astype(jnp.bfloat16)
    ends = feed_ref[:, pl.ds(3 * main, WIDE)]
    both = dot(rows, ends)
    upper = pltpu.roll(both, WIDE - over, 1)
    inner = jax.nn.silu(both[:, :LANES]) * upper[:, :LANES]
    inner = jnp.where(lanes(inner) < over, inner, 0.0)
    low = pltpu.roll(jnp.concatenate([inner, jnp.zeros_like(inner)], axis=1), 2 * over, 1)
    low = jnp.where(lanes(low) < 2 * over, 0.0, low).astype(jnp.bfloat16)
    high = pltpu.roll(inner, LANES - over, 1)
    high = jnp.where(lanes(high) < LANES - tail, 0.0, high).astype(jnp.bfloat16)
    terms = dot_nt(inner_ref[...], feed_ref[:, pl.ds(0, main)]) + dot_nt(low, ends) + dot_nt(high, last_ref[...])
    mine_ref[...] = terms[:length]
    other_ref[...] = terms[length:].astype(jnp.bfloat16)


def feed_terms(units, tail, near, far, feed, attn):
    length, model = near.shape
    main = units // LANES * LANES
    width = 3 * units - tail
    end = attn.shape[1] // LANES - 1

    def whole(shape):
        return pl.BlockSpec(shape, lambda step: (0, 0), pipeline_mode=pl.Buffered(1))

    return pl.pallas_call(
        functools.partial(forward_kernel, units, tail),
        grid=(1,),
        out_shape=[
            jax.ShapeDtypeStruct((length, model), jnp.float32),
            jax.ShapeDtypeStruct((length, model), jnp.bfloat16),
        ],
        in_specs=[
            whole((length, model)),
            whole((length, model)),
            whole((model, width)),
            pl.BlockSpec((model, LANES), lambda step: (0, end)),
        ],
        out_specs=[whole((length, model))] * 2,
        scratch_shapes=[
            pltpu.VMEM((2 * length, model), jnp.bfloat16),
            pltpu.VMEM((2 * length, main), jnp.bfloat16),
        ],
        compiler_params=pltpu.CompilerParams(vmem_limit_bytes=48 * 2**20),
        cost_estimate=pl.CostEstimate(flops=2**20, bytes_accessed=2**16, transcendentals=0),
    )(near, far, feed, attn)


def feed_kernel(
    units, tail, near_ref, far_ref, near_grad_ref, far_grad_ref, feed_ref, last_ref, *refs
):
    extras, refs = refs[:-8], refs[-8:]
    block_ref, rest_ref, halves_ref, inner_ref, rows_ref, grads_ref, wide_ref, down_ref = refs
    main = units // LANES * LANES
    over = units - main
    step = pl.program_id(0)
    length = near_ref.shape[0]
    size = feed_ref.shape[0]
    chunks = rows_ref.shape[1] // size

    def parts(gate, upper, grad):
        sigma = jax.nn.sigmoid(gate)
        act = gate * sigma
        slope = sigma * (1.0 + gate * (1.0 - sigma))
        return (act * upper, grad * upper * slope, grad * act)

    @pl.when(step == 0)
    def _():
        rows_ref[:length] = near_ref[...]
        rows_ref[length:] = far_ref[...]
        grads_ref[:length] = near_grad_ref[...]
        grads_ref[length:] = far_grad_ref[...]

    for chunk in range(chunks):
        place = pl.ds(chunk * size, size)

        @pl.when(step == chunk)
        def _(chunk=chunk, place=place):
            rows, branch = rows_ref[:, place], grads_ref[:, place]
            wide = dot(rows, feed_ref[:, pl.ds(main, 2 * main + WIDE)])
            down = dot(branch, feed_ref[:, pl.ds(0, main)])
            ends = dot(branch, feed_ref[:, pl.ds(3 * main, WIDE)])
            if chunk:
                wide = wide + wide_ref[...]
                down = down + down_ref[:, pl.ds(0, main)]
                ends = ends + down_ref[:, pl.ds(main, WIDE)]
            if chunk < chunks - 1:
                wide_ref[...] = wide
                down_ref[:, pl.ds(0, main)] = down
                down_ref[:, pl.ds(main, WIDE)] = ends
                return
            inner, grad_gate, grad_upper = (
                part.astype(jnp.bfloat16) for part in parts(wide[:, :main], wide[:, main : 2 * main], down)
            )
            inner_ref[:, pl.ds(0, main)] = inner
            halves_ref[:, pl.ds(0, main)] = grad_gate
            halves_ref[:, pl.ds(main, main)] = grad_upper
            both = wide[:, 2 * main :]
            upper = pltpu.roll(both, WIDE - over, 1)
            grad = pltpu.roll(ends, WIDE - 2 * over, 1)[:, :LANES]
            more = pltpu.roll(dot(grads_ref[...], last_ref[...]), over, 1)
            grad = jnp.where(lanes(grad) < over - tail, grad, more)
            inner, grad_gate, grad_upper = (
                jnp.where(lanes(part) < over, part, 0.0)
                for part in parts(both[:, :LANES], upper[:, :LANES], grad)
            )
            inner_ref[:, pl.ds(main, LANES)] = inner.astype(jnp.bfloat16)
            empty = jnp.zeros_like(grad_gate)
            last = jnp.concatenate([grad_gate, empty], axis=1)
            last = last + pltpu.roll(jnp.concatenate([grad_upper, empty], axis=1), over, 1)
            halves_ref[:, pl.ds(2 * main, WIDE)] = last.astype(jnp.bfloat16)

        @pl.when(step == chunks + chunk)
        def _(place=place):
            base = 0
            for extra in extras:
                block_ref[:, pl.ds(base, extra.shape[1])] = extra[...]
                base += extra.shape[1]
            rows, branch = rows_ref[:, place], grads_ref[:, place]
            down = dot_tn(branch, inner_ref[:, pl.ds(0, main)])
            block_ref[:, pl.ds(base, main)] = down.astype(jnp.bfloat16)
            wide = dot_tn(rows, halves_ref[:, pl.ds(0, 2 * main)])
            block_ref[:, pl.ds(base + main, 2 * main)] = wide.astype(jnp.bfloat16)
            down = dot_tn(branch, inner_ref[:, pl.ds(main, LANES)])
            down = jnp.concatenate([down, jnp.zeros_like(down)], axis=1)
            wide = dot_tn(rows, halves_ref[:, pl.ds(2 * main, WIDE)])
            wide = jnp.where(lanes(wide) < 2 * over, wide, pltpu.roll(down, 2 * over, 1))
            block_ref[:, pl.ds(base + 3 * main, WIDE)] = wide.astype(jnp.bfloat16)
            moved = pltpu.roll(down, WIDE - over, 1)
            rest_ref[...] = jnp.where(lanes(moved) < WIDE - tail, 0.0, moved).astype(jnp.bfloat16)


def feed_both(units, tail, near, far, near_grad, far_grad, feed, attn, stop, *extras):
    count, model = 2 * near.shape[0], near.shape[1]
    main = units // LANES * LANES
    width = 3 * units - tail
    size = model // CHUNKS
    total = width + sum(extra.shape[1] for extra in extras)
    shapes = ((model, total), (model, WIDE), (count, width - main), (count, main + LANES))
    end = stop // LANES - 1

    def later(columns):
        return pl.BlockSpec((size, columns), lambda step: (jnp.maximum(step - CHUNKS, 0), 0))

    def whole(shape):
        return pl.BlockSpec(shape, lambda step: (0, 0), pipeline_mode=pl.Buffered(1))

    return pl.pallas_call(
        functools.partial(feed_kernel, units, tail),
        grid=(2 * CHUNKS,),
        out_shape=[jax.ShapeDtypeStruct(shape, jnp.bfloat16) for shape in shapes],
        in_specs=[whole(near.shape)] * 4
        + [
            pl.BlockSpec((size, width), lambda step: (jnp.minimum(step, CHUNKS - 1), 0)),
            pl.BlockSpec((model, LANES), lambda step: (0, end), pipeline_mode=pl.Buffered(1)),
        ]
        + [later(extra.shape[1]) for extra in extras],
        out_specs=[later(total), later(WIDE), whole(shapes[2]), whole(shapes[3])],
        scratch_shapes=[
            pltpu.VMEM((count, model), jnp.bfloat16),
            pltpu.VMEM((count, model), jnp.bfloat16),
            pltpu.VMEM((count, width - main), jnp.float32),
            pltpu.VMEM((count, main + WIDE), jnp.float32),
        ],
        compiler_params=pltpu.CompilerParams(vmem_limit_bytes=56 * 2**20),
        cost_estimate=pl.CostEstimate(
            flops=4 * count * model * width,
            bytes_accessed=20 * 2**20,
            transcendentals=count * units,
        ),
    )(near, far, near_grad, far_grad, feed, attn, *extras)


def take(block, column, width):
    base = column // LANES * LANES
    shift = column - base
    stop = base + -(-(shift + width) // LANES) * LANES
    part = block[:, base:stop]
    if shift:
        part = pltpu.roll(part, stop - base - shift, 1)
    part = part[:, : -(-width // LANES) * LANES]
    return jnp.where(lanes(part) < width, part, 0.0)


def put(target, rows, column, width, part):
    base = column // LANES * LANES
    shift = column - base
    size = -(-(shift + width) // LANES) * LANES
    if size > part.shape[1]:
        empty = jnp.zeros((part.shape[0], size - part.shape[1]), part.dtype)
        part = jnp.concatenate([part, empty], axis=1)
    if shift:
        part = pltpu.roll(part, shift, 1)
    target[rows, pl.ds(base, size)] += part


def moved(block, distance):
    count = block.shape[0]
    if distance == 0:
        return block
    row = lax.broadcasted_iota(jnp.int32, block.shape, 0)
    rolled = pltpu.roll(block, distance % count, 0)
    inside = row >= distance if distance > 0 else row < count + distance
    return jnp.where(inside, rolled, 0.0)


def mixer_parts(both, taps, channels, first):
    length = both.shape[0]
    heads = channels // HD
    width = (both.shape[1] - 2 * channels) // (2 * heads)
    pre_values = take(both, 0, channels)
    values = sum(moved(pre_values, tap) * taps[tap : tap + 1] for tap in range(3))
    values = values.astype(jnp.bfloat16).astype(jnp.float32)
    gate = take(both, channels, channels)
    query = lax.broadcasted_iota(jnp.int32, (length, length), 0)
    key = lax.broadcasted_iota(jnp.int32, (length, length), 1)
    allowed = key <= query
    if not first:
        allowed = allowed & (query - key < WIN)
    parts = []
    for head in range(heads):
        queries = take(both, 2 * channels + head * width, width).astype(jnp.bfloat16)
        keys = take(both, 2 * channels + (heads + head) * width, width).astype(jnp.bfloat16)
        scores = dot_nt(queries, keys) / math.sqrt(width)
        if first:
            kernel = jnp.where(allowed, 1.0 + scores + 0.5 * scores * scores, 0.0)
            total = jnp.sum(kernel, axis=-1, keepdims=True)
            probs = kernel / total
            slope = jnp.where(allowed, (1.0 + scores) / total, 0.0)
        else:
            scores = jnp.where(allowed, scores, -1e30)
            kernel = jnp.exp(scores - jnp.max(scores, axis=-1, keepdims=True))
            probs = kernel / jnp.sum(kernel, axis=-1, keepdims=True)
            slope = probs
        own = take(values, head * HD, HD).astype(jnp.bfloat16)
        parts.append((queries, keys, probs, slope, own, dot(probs.astype(jnp.bfloat16), own)))
    return (pre_values, gate, parts)


def join(parts):
    empty = jnp.zeros_like(parts[0])
    total = 0.0
    for head, part in enumerate(parts):
        part = jnp.concatenate([part, empty], axis=1)
        total = total + (pltpu.roll(part, head * HD, 1) if head else part)
    return total


def mixer_kernel(
    channels, first, near_ref, far_ref, attn_ref, taps_ref, mine_ref, other_ref, both_ref, gated_ref
):
    length = near_ref.shape[0]
    stop = both_ref.shape[1]
    for index, rows in enumerate((near_ref, far_ref)):
        both = dot(rows[...], attn_ref[:, pl.ds(0, stop)])
        both_ref[pl.ds(index * length, length), :] = both
        _, gate, parts = mixer_parts(both, taps_ref[...], channels, first)
        gated = (join([part[-1] for part in parts]) * gate * jax.nn.sigmoid(gate)).astype(jnp.bfloat16)
        gated_ref[pl.ds(index * length, length), :] = gated
        terms = dot_nt(gated, attn_ref[:, pl.ds(stop, WIDE)])
        if index == 0:
            mine_ref[...] = terms
        else:
            other_ref[...] = terms.astype(jnp.bfloat16)


def mixer_back_kernel(
    channels, first, near_ref, far_ref, near_grad_ref, far_grad_ref, attn_ref, taps_ref, both_ref,
    gated_ref, rest_ref, block_ref, mine_ref, other_ref, taps_grad_ref, rows_ref, grads_ref, sums_ref, low_ref,
):
    length = near_ref.shape[0]
    stop = both_ref.shape[1]
    heads = channels // HD
    width = (stop - 2 * channels) // (2 * heads)
    taps = taps_ref[...]
    sums_ref[...] = jnp.zeros_like(sums_ref)
    taps_grad = [0.0] * 3
    rows_ref[:length] = near_ref[...]
    rows_ref[length:] = far_ref[...]
    grads_ref[:length] = near_grad_ref[...]
    grads_ref[length:] = far_grad_ref[...]
    for index in range(2):
        rows = pl.ds(index * length, length)
        pre_values, gate, parts = mixer_parts(both_ref[rows, :], taps, channels, first)
        mixed = join([part[-1] for part in parts])
        grad = dot(grads_ref[rows, :], attn_ref[:, pl.ds(stop, WIDE)])
        grad = jnp.where(lanes(grad) < channels, grad, 0.0)
        sigma = jax.nn.sigmoid(gate)
        grad_mixed = (grad * (gate * sigma)).astype(jnp.bfloat16).astype(jnp.float32)
        grad_gate = (grad * mixed * silu_slope(gate)).astype(jnp.bfloat16).astype(jnp.float32)
        put(sums_ref, rows, channels, channels, grad_gate)
        grad_values = []
        for head, (queries, keys, probs, slope, own, _) in enumerate(parts):
            part = take(grad_mixed, head * HD, HD).astype(jnp.bfloat16)
            grad_values.append(dot_tn(probs.astype(jnp.bfloat16), part))
            grad_probs = dot_nt(part, own)
            centred = grad_probs - jnp.sum(probs * grad_probs, axis=-1, keepdims=True)
            score_grad = (centred * slope).astype(jnp.bfloat16)
            for place, value in (
                (head, dot(score_grad, keys)),
                (heads + head, dot_tn(score_grad, queries)),
            ):
                value = (value / math.sqrt(width)).astype(jnp.bfloat16).astype(jnp.float32)
                put(sums_ref, rows, 2 * channels + place * width, width, value)
        grad_values = join(grad_values)
        grad_pre = sum(moved(grad_values, -tap) * taps[tap : tap + 1] for tap in range(3))
        put(sums_ref, rows, 0, channels, grad_pre.astype(jnp.bfloat16).astype(jnp.float32))
        for tap in range(3):
            taps_grad[tap] = taps_grad[tap] + jnp.sum(
                grad_values * moved(pre_values, tap), axis=0, keepdims=True
            )
    for tap in range(3):
        taps_grad_ref[pl.ds(tap, 1), :] = taps_grad[tap]
    low_ref[...] = sums_ref[...].astype(jnp.bfloat16)
    for column in range(0, stop, LANES):
        size = min(WIDE, stop - column)
        if column % WIDE:
            continue
        place = pl.ds(column, size)
        block_ref[:, place] = dot_tn(rows_ref[...], low_ref[:, place]).astype(jnp.bfloat16)
    last = dot_tn(grads_ref[...], gated_ref[...]).astype(jnp.bfloat16)
    block_ref[:, pl.ds(stop, WIDE)] = last + rest_ref[...]
    for index in range(2):
        terms = dot_nt(low_ref[pl.ds(index * length, length), :], attn_ref[:, pl.ds(0, stop)])
        if index == 0:
            mine_ref[...] = terms
        else:
            other_ref[...] = terms.astype(jnp.bfloat16)


def whole_call(kernel, inputs, shapes, scratch, flops, columns=()):
    columns = dict(columns)

    def whole(shape):
        return pl.BlockSpec(shape, lambda step: (0,) * len(shape), pipeline_mode=pl.Buffered(1))

    return pl.pallas_call(
        kernel,
        grid=(1,),
        out_shape=[jax.ShapeDtypeStruct(shape, kind) for shape, kind in shapes],
        in_specs=[
            whole((*block.shape[:-1], columns.get(place, block.shape[-1]))) for place, block in enumerate(inputs)
        ],
        out_specs=[whole(shape) for shape, _ in shapes],
        scratch_shapes=[pltpu.VMEM(shape, kind) for shape, kind in scratch],
        compiler_params=pltpu.CompilerParams(vmem_limit_bytes=56 * 2**20),
        cost_estimate=pl.CostEstimate(flops=flops, bytes_accessed=2**16, transcendentals=0),
    )(*inputs)


def mixer_forward(channels, first, near, far, attn, width, taps):
    length, model = near.shape
    stop = width - WIDE
    shapes = (
        ((length, model), jnp.float32),
        ((length, model), jnp.bfloat16),
        ((2 * length, stop), jnp.float32),
        ((2 * length, WIDE), jnp.bfloat16),
    )
    kernel = functools.partial(mixer_kernel, channels, first)
    return whole_call(kernel, (near, far, attn, taps), shapes, (), 2**20, ((2, width),))


def mixer_backward(channels, first, near, far, near_grad, far_grad, attn, taps, both, gated, rest):
    length, model = near.shape
    stop = both.shape[1]
    shapes = (
        ((model, stop + WIDE), jnp.bfloat16),
        ((length, model), jnp.float32),
        ((length, model), jnp.bfloat16),
        (taps.shape, jnp.float32),
    )
    scratch = (
        ((2 * length, model), jnp.bfloat16),
        ((2 * length, model), jnp.bfloat16),
        ((2 * length, stop), jnp.float32),
        ((2 * length, stop), jnp.bfloat16),
    )
    inputs = (near, far, near_grad, far_grad, attn, taps, both, gated, rest)
    kernel = functools.partial(mixer_back_kernel, channels, first)
    return whole_call(kernel, inputs, shapes, scratch, 2**20, ((4, stop + WIDE),))


def end_kernel(
    channels, units, tail, core_ref, mine_ref, other_ref, low_ref, high_ref, kept_ref,
    vgate_ref, out_ref, pair_ref, down_ref,
):
    step = pl.program_id(0)
    lower = core_ref[0] == 0
    mine, other = (ref[...].astype(jnp.float32) for ref in (mine_ref, other_ref))
    low = jnp.where(lower, mine, low_ref[...].astype(jnp.float32))
    high = jnp.where(lower, other, high_ref[...].astype(jnp.float32))
    size = mine.shape[1]
    wide = pair_ref.shape[1] // 2

    @pl.when(step == 0)
    def _():
        for place in range(2):
            parts = [take(block, place * channels, channels) for block in (low, high)]
            empty = jnp.zeros_like(parts[0])
            first = jnp.concatenate([parts[0], empty], axis=1)
            second = pltpu.roll(jnp.concatenate([parts[1], empty], axis=1), channels, 1)
            vgate_ref[:, place, :] = (first + second)[:, : 2 * channels]
        for place, block in enumerate((low, high)):
            turned = jnp.swapaxes(block[:, size - WIDE :], 0, 1)
            out_ref[pl.ds(place * channels, channels), :] = turned[:channels]
        for place, block in enumerate((jnp.where(lower, mine, other), jnp.where(lower, other, mine))):
            turned = jnp.swapaxes(block[:, size - WIDE - LANES : size - WIDE], 0, 1)
            for half in range(2):
                start = LANES - (2 - half) * wide
                pair_ref[half, pl.ds(place * wide, wide), :] = turned[start : start + wide]

    for place, block in enumerate((low, high)):

        @pl.when(step == place)
        def _(place=place, block=block):
            stop = units * (place + 1) % LANES or LANES
            last = block[:, size - LANES :]
            if stop < LANES:
                last = pltpu.roll(last, stop, 1)
            column = lanes(last)
            inside = (column >= stop - tail) & (column < stop)
            down_ref[...] = jnp.where(inside, last, kept_ref[...])


def end_call(channels, tail, width, core, mine, other, low, high, down):
    count, size = mine.shape
    units = down.shape[1] // 2
    first, second = (units - 1) // LANES, (2 * units - 1) // LANES

    def whole(shape):
        return pl.BlockSpec(shape, lambda step: (0,) * len(shape))

    tile = pl.BlockSpec((count, LANES), lambda step: (0, first + step * (second - first)))
    shapes = ((count, 2, 2 * channels), (2 * channels, count), (2, width, count))
    return pl.pallas_call(
        functools.partial(end_kernel, channels, units, tail),
        grid=(2,),
        out_shape=[jax.ShapeDtypeStruct(shape, jnp.float32) for shape in (*shapes, down.shape)],
        in_specs=[pl.BlockSpec(memory_space=pltpu.SMEM)]
        + [whole((count, size))] * 4
        + [tile],
        out_specs=[whole(shape) for shape in shapes] + [tile],
        input_output_aliases={5: 3},
        compiler_params=pltpu.CompilerParams(vmem_limit_bytes=48 * 2**20),
        cost_estimate=pl.CostEstimate(flops=2**20, bytes_accessed=2**27, transcendentals=0),
    )(core.reshape(1), mine, other, low, high, down)


def by_rows(block):
    return with_layout_constraint(block, Layout(major_to_minor=tuple(range(block.ndim))))


class Queue:
    def __init__(self):
        self.done = []

    def scatter(self, *grads):
        block = by_rows(jnp.concatenate(grads, axis=1) if len(grads) > 1 else grads[0])
        if self.done:
            block, self.done[-1] = lax.optimization_barrier((block, self.done[-1]))
        self.done.append(by_rows(lax.psum_scatter(block, "dp", scatter_dimension=0, tiled=True)))


def body(
    boundary, lengths, norm_gains, conv_taps, lin_qk, win_qk, value_gate, out_weight, gate_up, down_weight
):
    core = lax.axis_index("section")
    index = lax.axis_index("tensor")
    lower = core == 0
    rows_dev, model = boundary.shape[2:]
    channels = value_gate.shape[-1] // 2
    units = gate_up.shape[-1] // 2
    main = units // LANES * LANES
    tail = -(3 * channels + lin_qk.shape[-1]) % LANES

    def half(block, axis, which):
        size = block.shape[axis] // 2
        return lax.dynamic_slice_in_dim(block, which * size, size, axis)

    def both_layers(build):
        mine = build(core)
        other = swap(build(1 - core))
        return (jnp.where(lower, mine, other), jnp.where(lower, other, mine))

    def attn_piece(pair, which):
        own = slice(which * channels, (which + 1) * channels)
        wide = pair.shape[2] // 2
        pair = pair[:, :, which * wide : (which + 1) * wide]
        last = down_weight[0][(which + 1) * units - tail : (which + 1) * units]
        values = value_gate[0][:, :, own]
        parts = [values[:, 0], values[:, 1], pair[:, 0], pair[:, 1], out_weight[0][own].T, last.T]
        return jnp.concatenate(parts, axis=1)

    def feed_piece(which):
        pair = half(gate_up[0], 2, which)
        down = half(down_weight[0], 0, which).T
        return jnp.concatenate(
            [down[:, :main], pair[:, 0, :main], pair[:, 1, :main], pair[:, 0, main:], pair[:, 1, main:], down[:, main : units - tail]],
            axis=1,
        )

    def fetch(piece):
        return lax.all_gather(piece, "dp", axis=0, tiled=True)

    attn_zero = fetch(jnp.where(lower, attn_piece(lin_qk, 0), swap(attn_piece(lin_qk, 1))))
    feed_parts = both_layers(feed_piece)
    split = feed_parts[0].shape[1]
    edge = split - WIDE
    most = fetch(feed_parts[0][:, :edge])
    attn_one = jnp.where(lower, swap(attn_piece(win_qk, 0)), attn_piece(win_qk, 1))
    piece = jnp.concatenate([attn_one, feed_parts[0][:, edge:]], axis=1)
    attn_zero, moved = lax.optimization_barrier((attn_zero, ring_step(piece)))
    ring = ring_gather(piece, moved)
    wide = attn_one.shape[1]
    feed_one = fetch(feed_parts[1])

    small = jnp.concatenate([norm_gains[0], conv_taps[0]], axis=0)
    small_other = swap(small)
    small_zero = jnp.where(lower, small, small_other)
    small_one = jnp.where(lower, small_other, small)
    offset = (2 * index + core) * channels

    def own_taps(block):
        own = lax.dynamic_slice_in_dim(block[2:], offset, channels, 1)
        return jnp.pad(own, ((0, -own.shape[0] % SUBLANES), (0, WIDE - channels)))

    held = boundary[0]
    keep = lax.dynamic_index_in_dim(held, core, 0, keepdims=False)
    other = swap(lax.dynamic_index_in_dim(held, 1 - core, 0, keepdims=False))
    entering = jnp.where(lower, keep, other).astype(jnp.float32)
    cotangent = jnp.where(lower, other, keep).astype(jnp.float32)
    length = lax.dynamic_index_in_dim(lengths, core, 0, keepdims=False)
    place = index * rows_dev + jnp.arange(rows_dev)
    mask = (place < length).astype(jnp.float32)[:, None]

    queue = Queue()
    gains_zero, gains_one = small_zero[:2], small_one[:2]
    taps_zero, taps_one = own_taps(small_zero), own_taps(small_one)

    def mix(rows, gain, attn, size, taps, first):
        scale, normed = rms_rows(rows, gain)
        near, far = spread_pair(normed)
        mine, other, both, gated = mixer_forward(channels, first, near, far, attn, size, taps)
        return (rows + collect_pair(mine, other), (rows, scale, near, far, both, gated))

    def mix_back(kept, grad_out, gain, attn, taps, rest, first):
        rows, scale, near, far, both, gated = kept
        block, mine, other, grad_taps = mixer_backward(
            channels, first, near, far, *spread_pair(grad_out), attn, taps, both, gated, rest
        )
        back, grad_gain = rms_back(rows, scale, gain, collect_pair(mine, other))
        return (block, grad_out + back, grad_gain, grad_taps[: conv_taps.shape[1], :channels])

    hidden, kept_zero = mix(entering, gains_zero[0], attn_zero, attn_zero.shape[1], taps_zero, True)
    scale, normed = rms_rows(hidden, gains_zero[1])
    near, far = spread_pair(normed)
    grad_out = cotangent * mask
    near, far, ring, *grads_one = lax.optimization_barrier((near, far, ring, *spread_pair(grad_out)))
    packed = jnp.concatenate([most, ring[:, wide:]], axis=1)
    kept_feed = (hidden, scale, near, far)
    mine, other = feed_terms(units, tail, near, far, packed, attn_zero)
    other, ring = lax.optimization_barrier((other, ring))
    down_one = jnp.concatenate(
        [feed_one[:, :main], feed_one[:, main + 2 * units :], ring[:, wide - tail : wide]], axis=1
    )
    middle = hidden + collect_pair(mine, other)
    middle = middle.astype(jnp.bfloat16).astype(jnp.float32)

    hidden, kept_one = mix(middle, gains_one[0], ring, wide, taps_one, False)
    scale, normed = rms_rows(hidden, gains_one[1])
    block, rest, grad_halves, inner = feed_both(
        units, tail, *spread_pair(normed), *grads_one, feed_one, ring, wide
    )
    queue.scatter(block)
    final = hidden + collect(dot_nt(inner[:, :units], down_one))
    back, gain_two = rms_back(hidden, scale, gains_one[1], collect(dot_nt(grad_halves, feed_one[:, main:])))
    attn_grads, grad_middle, gain_one, taps_one = mix_back(
        kept_one, grad_out + back, gains_one[0], ring, taps_one, rest, False
    )
    gains_one = jnp.stack([gain_one, gain_two])

    grad_middle = grad_middle.astype(jnp.bfloat16).astype(jnp.float32)
    hidden, scale, near, far = kept_feed
    block, rest, grad_halves, _ = feed_both(
        units, tail, near, far, *spread_pair(grad_middle), packed, attn_zero, attn_zero.shape[1], attn_grads
    )
    queue.scatter(block)
    terms = dot_nt(grad_halves, packed[:, main:split])
    back, gain_two = rms_back(hidden, scale, gains_zero[1], collect(terms))
    attn_grads, grad_start, gain_one, taps_zero = mix_back(
        kept_zero, grad_middle + back, gains_zero[0], attn_zero, taps_zero, rest, True
    )
    queue.scatter(attn_grads)
    gains_zero = jnp.stack([gain_one, gain_two])

    edge = wide
    grads_one = (queue.done[0], queue.done[1][:, :edge])
    grads_zero = (queue.done[1][:, edge:], queue.done[2])

    def own_small(gains, taps):
        spot = jnp.zeros((taps.shape[0], model), jnp.float32)
        return jnp.concatenate([gains, lax.dynamic_update_slice_in_dim(spot, taps, offset, 1)], axis=0)

    sums = sum_all(jnp.stack([own_small(gains_zero, taps_zero), own_small(gains_one, taps_one)]))
    sums = lax.dynamic_index_in_dim(sums, core, 0, keepdims=True)

    final = final * mask
    ends_keep = jnp.where(lower, grad_start, final)
    ends_other = swap(jnp.where(lower, final, grad_start))
    ends = jnp.where(lower, jnp.stack([ends_keep, ends_other]), jnp.stack([ends_other, ends_keep]))

    def home(zero, one):
        mine = jnp.where(lower, zero, one)
        other = swap(jnp.where(lower, one, zero))
        return (jnp.where(lower, mine, other), jnp.where(lower, other, mine))

    def halves(low, high, axis):
        return jnp.concatenate([low, high], axis=axis).astype(jnp.float32)

    def pair_home(block):
        size = block.shape[1] // 2
        other = swap(block)
        low = jnp.where(lower, block, other)
        high = jnp.where(lower, other, block)
        return jnp.stack(
            [halves(low[:, :size], high[:, :size], 1), halves(low[:, size:], high[:, size:], 1)], axis=1
        )

    last = grads_zero[1]
    early = grads_one[1]
    both = 2 * channels
    gap = last.shape[1] - both - WIDE
    own = jnp.concatenate(
        [early[:, :both], jnp.zeros((early.shape[0], gap), early.dtype), early[:, early.shape[1] - WIDE :]],
        axis=1,
    )
    away = swap(own)

    def unpack(block):
        wide = block[:, main:]
        (gate, upper), (gate_rest, upper_rest) = gates(wide, units)
        empty = jnp.zeros((block.shape[0], tail), block.dtype)
        down = jnp.concatenate([block[:, :main], wide[:, 2 * units :], empty], axis=1)
        return (
            jnp.concatenate([gate, gate_rest], axis=1),
            jnp.concatenate([upper, upper_rest], axis=1),
            down,
        )

    low, high = home(grads_zero[0], grads_one[0])
    low, high = unpack(low), unpack(high)
    gate_up_grad = jnp.stack([halves(low[0], high[0], 1), halves(low[1], high[1], 1)], axis=1)
    down_grad = by_rows(halves(low[2], high[2], 1))
    win_grad = by_rows(pair_home(early[:, both : early.shape[1] - WIDE]))
    gate_up_grad = by_rows(gate_up_grad)
    low, high = jnp.where(lower, own, away), jnp.where(lower, away, own)
    gain_sums, taps_sums = by_rows(sums[:, :2]), by_rows(sums[:, 2:])
    last, low, high, gate_up_grad, down_grad, win_grad, ends, gain_sums, taps_sums = lax.optimization_barrier(
        (last, low, high, gate_up_grad, down_grad, win_grad, ends, gain_sums, taps_sums)
    )
    vgate_grad, out_grad, pair_grad, down_grad = end_call(
        channels, tail, gap, core, last, swap(last), low, high, down_grad
    )
    return (
        ends[None],
        gain_sums,
        taps_sums,
        jnp.transpose(pair_grad, (2, 0, 1)),
        win_grad,
        vgate_grad[None],
        out_grad[None],
        gate_up_grad[None],
        down_grad.T[None],
    )


def solution(mesh):
    in_specs = (
        P("section", "dp", "tensor", None),
        P("dp"),
        P("section", None, None),
        P("section", None, None),
        P("dp", None, "tensor"),
        P("dp", None, "tensor"),
        P("section", "dp", None, "tensor"),
        P("section", "tensor", "dp"),
        P("section", "dp", None, "tensor"),
        P("section", "tensor", "dp"),
    )
    out_specs = (
        P("section", "dp", "tensor", None),
        P("section", None, None),
        P("section", None, None),
        P("dp", None, "tensor"),
        P("dp", None, "tensor"),
        P("section", "dp", None, "tensor"),
        P("section", "tensor", "dp"),
        P("section", "dp", None, "tensor"),
        P("section", "tensor", "dp"),
    )
    return jax.shard_map(body, mesh=mesh, in_specs=in_specs, out_specs=out_specs, check_vma=False)
```
